512 devices in a mesh: dp: 16 (over z, y_hi), tensor: 32 (over y_lo, x, core).
Axes of the slice: x: 4, y: 8 (y_hi: 2, y_lo: 4; y = y_hi * 4 + y_lo), z: 8, core: 2. Of those that a mesh axis runs over, the one named last changes fastest.
Arguments:
- activations: bfloat16 [65536, 8192], P(('dp', 'tensor')), may hold values from -6 to 6
- key_cotangent: bfloat16 [65536, 768], P(('dp', 'tensor')), may hold values from -16 to 16
- doc_lengths: int32 [16, 8], P('dp'), may hold values from 1 to 2048, 4096 in all within a row
- weight_codes: int32 [8192, 768], P('tensor'), may hold values from 0 to 3
- zero_points: int32 [128, 768], P('tensor'), may hold values from 0 to 3
- step_sizes: float32 [128, 768], P('tensor'), may hold values from 0.004 to 0.016
Outputs:
- input_grad: bfloat16 [65536, 8192], P(('dp', 'tensor'))
- step_grad: float32 [128, 768], P('tensor')
The draws below stay inside these ranges and needn't reach their ends.
Inputs may be any that keep to these rules, and one draw needn't show every extreme that they name: `doc_lengths`: each row sums to 4096; its longest document has exactly 2048 tokens.
All inputs are finite; a program needn't handle non-finite values.
Results may differ from the reference program's by a relative error of at most 0.0057.
Values may be sent and summed in bfloat16 or wider, within the bound.
No kernel may reach another device: no remote copies, remote signals or barrier semaphores. Data moves between devices by JAX's collectives and lax.ppermute only.
A program may use at most 64 MiB of HBM per device.

```python
import math
import jax
import jax.numpy as jnp
import numpy as np
from jax import lax

D = 8192
HEAD = 128
GROUP = 64
DOCS = 8
KC = 768
GROUPS = 128
TOKENS = 4096
ALL_TOK = 65536
N_DP = 16


def place_ends(values, own_key, least, high):
    shape = values.shape
    index_at = [jax.random.randint(jax.random.fold_in(own_key, axis), (), 0, shape[axis]) for axis in range(len(shape))]
    values = values.at[tuple(index_at)].set(least)
    longest = shape.index(max(shape))
    index_at[longest] = (index_at[longest] + 1) % shape[longest]
    return values.at[tuple(index_at)].set(high)


def steps_of(stream_key, dims, shards, low, top_value):
    factor_of, own = 1.0, jax.random.fold_in(stream_key, 6)
    for dim, blocks in shards:
        draws = jnp.exp(jax.random.uniform(jax.random.fold_in(own, dim), (blocks,), jnp.float32, low / len(shards), top_value / len(shards)))
        factor_of = factor_of * jnp.repeat(draws, dims[dim] // blocks).reshape([-1 if axis == dim else 1 for axis in range(len(dims))])
    return factor_of


def length_profile(number_of, total, bound, lean):
    weights = [(1 << 20) // math.isqrt(standing ** lean) + 1 for standing in range(2, number_of + 1)]
    rest, counts = total - bound - (number_of - 1), [1] * (number_of - 1)
    while rest > 0:
        candidates = [i for i in range(number_of - 1) if counts[i] < bound]
        mass, remaining = sum([weights[i] for i in candidates]), rest
        for i in candidates:
            extra = min(bound - counts[i], max(1, remaining * weights[i] // mass), rest)
            counts[i] = counts[i] + extra
            rest = rest - extra
    return np.array([bound] + counts)


def uneven(own_key, amount, total, limit, skew):
    if amount == 2:
        one = jax.random.randint(own_key, (), max(1, total - limit), min(limit, total - 1) + 1)
        return jnp.stack([one, total - one])
    lengths = jnp.asarray(length_profile(amount, total, limit, skew), jnp.int32)
    pairs = (amount - 1) // 2
    source_of, sink = lengths[1:1 + 2 * pairs:2], lengths[2:2 + 2 * pairs:2]
    slack = jnp.minimum(source_of - 1, limit - sink)
    passed = jax.random.randint(jax.random.fold_in(own_key, 1), (pairs,), 0, 1 << 20) % (slack + 1)
    lengths = lengths.at[1:1 + 2 * pairs:2].set(source_of - passed).at[2:2 + 2 * pairs:2].set(sink + passed)
    return lengths[jax.random.permutation(jax.random.fold_in(own_key, 2), amount)]


def noise(stream_key, shape, spread, bound, cuts=(), kind=jnp.bfloat16):
    entries = spread * jax.random.normal(stream_key, shape, jnp.float32)
    if cuts:
        entries = entries * steps_of(stream_key, shape, cuts, -0.22, 0.18)
    return jnp.clip(entries, -bound, bound).astype(kind)


def setup_inputs(seed: int = 0) -> dict:
    seeds = jax.random.split(jax.random.key(seed), 7)
    activations = noise(seeds[0], (ALL_TOK, D), 1.0, 6.0, ((0, 512),))
    key_cotangent = noise(seeds[1], (ALL_TOK, KC), 3.0, 16.0, ((0, 512),))
    doc_lengths = jax.vmap(lambda own: uneven(own, DOCS, TOKENS, TOKENS // 2, 2))(jax.random.split(seeds[2], N_DP)).reshape((N_DP, DOCS)).astype(jnp.int32)
    weight_codes = place_ends(jax.random.randint(seeds[3], (D, KC), 0, 4), jax.random.fold_in(seeds[3], 1), 0, 3).astype(jnp.int32)
    zero_points = place_ends(jax.random.randint(seeds[4], (GROUPS, KC), 0, 4), jax.random.fold_in(seeds[4], 1), 0, 3).astype(jnp.int32)
    step_sizes = jnp.clip(jnp.exp(math.log(0.016) - 1.3862944 * jax.random.uniform(seeds[5], (GROUPS, KC), jnp.float32) ** steps_of(seeds[5], (GROUPS, KC), ((0, 32),), -0.2, 0.2)), 0.004, 0.016)
    return {"activations": activations, "key_cotangent": key_cotangent, "doc_lengths": doc_lengths, "weight_codes": weight_codes, "zero_points": zero_points, "step_sizes": step_sizes}


def token_positions(ends, indices):
    starts = jnp.where(ends[None, :] <= indices[:, None], ends[None, :], 0)
    return (indices - jnp.max(starts, axis=1)).astype(jnp.int32)


def rope_back(cotangent, positions):
    count = cotangent.shape[0]
    split = cotangent.astype(jnp.float32).reshape(count, -1, HEAD)
    middle = HEAD // 2
    freqs = jnp.exp(jnp.arange(middle, dtype=jnp.float32) * (-2.0 * math.log(10000.0) / HEAD))
    angles = positions.astype(jnp.float32)[:, None] * freqs[None, :]
    cosine = jnp.cos(angles)[:, None, :]
    sine = jnp.sin(angles)[:, None, :]
    first = split[..., :middle]
    second = split[..., middle:]
    lower = first * cosine + second * sine
    upper = second * cosine - first * sine
    return jnp.concatenate([lower, upper], axis=-1).reshape(count, -1).astype(jnp.bfloat16)


def reference(activations, key_cotangent, doc_lengths, weight_codes, zero_points, step_sizes):
    levels = (weight_codes - jnp.repeat(zero_points, GROUP, axis=0)).astype(jnp.float32)
    weight = (jnp.repeat(step_sizes, GROUP, axis=0) * levels).astype(jnp.bfloat16)
    inputs = activations.reshape(N_DP, TOKENS, D)
    cotangents = key_cotangent.reshape(N_DP, TOKENS, KC)
    indices = jnp.arange(TOKENS, dtype=jnp.int32)

    def one_sequence(operands):
        inputs_one, cot_one, lengths_one = operands
        ends = jnp.cumsum(lengths_one, dtype=jnp.int32)
        rotated = rope_back(cot_one, token_positions(ends, indices))
        grad_in = jnp.dot(rotated, weight.T, preferred_element_type=jnp.float32).astype(jnp.bfloat16)
        weight_grad = jnp.dot(inputs_one.T, rotated, preferred_element_type=jnp.float32)
        partial_grad = (weight_grad * levels).reshape(GROUPS, GROUP, KC).sum(axis=1) / TOKENS
        return grad_in, partial_grad

    grads_in, partials = lax.map(one_sequence, (inputs, cotangents, doc_lengths))
    return grads_in.reshape(ALL_TOK, D), jnp.sum(partials, axis=0)
```

```python
import functools
import math

import jax
import jax.numpy as jnp
from jax import lax
from jax.experimental import pallas as pl
from jax.experimental.pallas import tpu as pltpu
from jax.sharding import PartitionSpec as P

HEAD = 128
GROUP = 64
AXES = ("dp", "tensor")
NX, NY, NYL, NZ = 4, 8, 4, 8
VMEM = 48 * 1024 * 1024


def device_at(x, y, z, core):
    x, y, z = x % NX, y % NY, z % NZ
    dp = z * (NY // NYL) + y // NYL
    return dp * (NX * NYL * 2) + ((y % NYL) * NX + x) * 2 + core


def permutation(target):
    return [
        (device_at(x, y, z, core), device_at(*target(x, y, z, core)))
        for x in range(NX)
        for y in range(NY)
        for z in range(NZ)
        for core in range(2)
    ]


def send(value, dx, dy, cross=False):
    def target(x, y, z, core):
        sign = 1 if (core == 0) != cross else -1
        return x + sign * dx, y + sign * dy, z, core ^ int(cross)

    return lax.ppermute(value, AXES, permutation(target))


def swap(value):
    return lax.ppermute(value, AXES, permutation(lambda x, y, z, core: (x, y, z, core ^ 1)))


def token_positions(lengths, indices):
    count = lengths.shape[0]
    order = jnp.arange(count, dtype=jnp.int32)
    ends = jnp.sum(jnp.where(order[:, None] <= order[None, :], lengths[:, None], 0), axis=0)
    starts = jnp.where(ends[None, :] <= indices[:, None], ends[None, :], 0)
    return indices - jnp.max(starts, axis=1)


def rope_back(cotangent, positions):
    count = cotangent.shape[0]
    split = cotangent.astype(jnp.float32).reshape(count, -1, HEAD)
    middle = HEAD // 2
    freqs = jnp.exp(jnp.arange(middle, dtype=jnp.float32) * (-2.0 * math.log(10000.0) / HEAD))
    angles = positions.astype(jnp.float32)[:, None] * freqs[None, :]
    cosine = jnp.cos(angles)[:, None, :]
    sine = jnp.sin(angles)[:, None, :]
    first = split[..., :middle]
    second = split[..., middle:]
    lower = first * cosine + second * sine
    upper = second * cosine - first * sine
    return jnp.concatenate([lower, upper], axis=-1).reshape(count, -1).astype(jnp.bfloat16)


def dequant_kernel(codes_ref, zeros_ref, steps_ref, weight_ref):
    for group in range(zeros_ref.shape[0]):
        rows = pl.ds(group * GROUP, GROUP)
        levels = (codes_ref[rows, :] - zeros_ref[group : group + 1, :]).astype(jnp.float32)
        weight_ref[rows, :] = (steps_ref[group : group + 1, :] * levels).astype(jnp.bfloat16)


def dequant(codes, zeros, steps):
    return pl.pallas_call(
        dequant_kernel,
        out_shape=jax.ShapeDtypeStruct(codes.shape, jnp.bfloat16),
        compiler_params=pltpu.CompilerParams(vmem_limit_bytes=VMEM),
        name="dequant",
    )(codes, zeros, steps)


def shards_kernel(counts, aliased, table, mine_ref, other_ref, rot_ref, *refs):
    weights = refs[: len(counts)]
    grad_ref, sent_ref, sums_ref = refs[len(counts) + int(aliased) :]
    at = pl.program_id(0)
    half = mine_ref.shape[0]

    def unit(weight_ref):
        weight = weight_ref[...]
        rot = rot_ref[...]
        grad = lax.dot_general(
            rot, weight, (((1,), (1,)), ((), ())), preferred_element_type=jnp.float32
        ).astype(jnp.bfloat16)
        grad_ref[...] = grad[:half]
        sent_ref[...] = grad[half:]
        feats = jnp.concatenate([mine_ref[...], other_ref[...]], axis=0)
        weight_grad = lax.dot_general(
            feats, rot, (((0,), (0,)), ((), ())), preferred_element_type=jnp.float32
        )
        product = weight_grad * weight.astype(jnp.float32)
        groups = product.shape[0] // GROUP
        sums_ref[0] = product.reshape(groups, GROUP, product.shape[1]).sum(axis=1)

    first = 0
    for count, weight_ref in zip(counts, weights):
        if len(counts) == 1:
            unit(weight_ref)
        else:
            inside = jnp.logical_and(at >= first, at < first + count)
            pl.when(inside)(functools.partial(unit, weight_ref))
        first += count


def shards(table, mine, other, rot, weights, rows, grad=None):
    tokens, width = mine.shape
    cols = rot.shape[1]
    counts = tuple(weight.shape[0] // rows for weight in weights)
    total = sum(counts)

    def weight_spec(first, count):
        return pl.BlockSpec((rows, cols), lambda i, t: (jnp.clip(i - first, 0, count - 1), 0))

    firsts = [sum(counts[:k]) for k in range(len(counts))]
    in_specs = [
        pl.BlockSpec((tokens, rows), lambda i, t: (0, t[i])),
        pl.BlockSpec((tokens, rows), lambda i, t: (0, t[i])),
        pl.BlockSpec(rot.shape, lambda i, t: (0, 0)),
    ] + [weight_spec(first, count) for first, count in zip(firsts, counts)]
    operands = [mine, other, rot, *weights]
    aliases = {}
    if grad is not None:
        aliases = {1 + len(operands): 0}
        in_specs.append(pl.BlockSpec(memory_space=pl.ANY))
        operands.append(grad)
    groups = rows // GROUP
    return pl.pallas_call(
        functools.partial(shards_kernel, counts, grad is not None),
        out_shape=(
            jax.ShapeDtypeStruct((tokens, width), jnp.bfloat16),
            jax.ShapeDtypeStruct((tokens, total * rows), jnp.bfloat16),
            jax.ShapeDtypeStruct((total, groups, cols), jnp.float32),
        ),
        grid_spec=pltpu.PrefetchScalarGridSpec(
            num_scalar_prefetch=1,
            grid=(total,),
            in_specs=in_specs,
            out_specs=(
                pl.BlockSpec((tokens, rows), lambda i, t: (0, t[i])),
                pl.BlockSpec((tokens, rows), lambda i, t: (0, i)),
                pl.BlockSpec((1, groups, cols), lambda i, t: (i, 0, 0)),
            ),
        ),
        input_output_aliases=aliases,
        cost_estimate=pl.CostEstimate(
            flops=8 * total * rows * cols * tokens,
            bytes_accessed=total * rows * (cols * 2 + tokens * 8),
            transcendentals=0,
        ),
        compiler_params=pltpu.CompilerParams(vmem_limit_bytes=VMEM),
        name="shards",
    )(table, *operands)


def place_kernel(table, block_ref, grad_in, grad_ref):
    grad_ref[...] = block_ref[...]


def place(table, blocks, grad, rows):
    tokens = grad.shape[0]
    return pl.pallas_call(
        place_kernel,
        out_shape=jax.ShapeDtypeStruct(grad.shape, grad.dtype),
        grid_spec=pltpu.PrefetchScalarGridSpec(
            num_scalar_prefetch=1,
            grid=(blocks.shape[1] // rows,),
            in_specs=[
                pl.BlockSpec((tokens, rows), lambda i, t: (0, i)),
                pl.BlockSpec(memory_space=pl.ANY),
            ],
            out_specs=pl.BlockSpec((tokens, rows), lambda i, t: (0, t[i])),
        ),
        input_output_aliases={2: 0},
        cost_estimate=pl.CostEstimate(
            flops=0, bytes_accessed=2 * blocks.size * 2, transcendentals=0
        ),
        compiler_params=pltpu.CompilerParams(vmem_limit_bytes=VMEM),
        name="place",
    )(table, blocks, grad)


def spread_kernel(table, *refs):
    *sums, all_ref = refs
    all_ref[...] = jnp.zeros_like(all_ref)
    unit = 0
    for ref in sums:
        for row in range(ref.shape[0]):
            all_ref[table[unit]] = ref[row].astype(all_ref.dtype)
            unit += 1


def spread(table, sums, devices):
    return pl.pallas_call(
        spread_kernel,
        out_shape=jax.ShapeDtypeStruct((devices, *sums[0].shape[1:]), jnp.bfloat16),
        in_specs=[pl.BlockSpec(memory_space=pltpu.SMEM)]
        + [pl.BlockSpec(memory_space=pltpu.VMEM)] * len(sums),
        out_specs=pl.BlockSpec(memory_space=pltpu.VMEM),
        compiler_params=pltpu.CompilerParams(vmem_limit_bytes=VMEM),
        name="spread",
    )(table, *sums)


def unit_table(x, y, core):
    sign = 2 * core - 1

    def owner(dx, dy, half):
        return (((y + sign * dy) % NYL) * NX + (x + sign * dx) % NX) * 2 + half

    return (
        [owner(0, 0, core)]
        + [owner(1, 0, 0), owner(1, 0, 1)]
        + [owner(0, 1, 0), owner(0, 1, 1)]
        + [owner(1, 1, 0), owner(1, 1, 1)]
        + [owner(-1, 1, 0), owner(-1, 1, 1)]
        + [owner(2, 1, 0), owner(2, 1, 1), owner(2, 0, core)]
        + [owner(1, 2, 0), owner(1, 2, 1), owner(0, 2, core)]
        + [owner(2, 2, core)]
    )


def per_device(activations, key_cotangent, doc_lengths, weight_codes, zero_points, step_sizes):
    tokens = activations.shape[0]
    rows = weight_codes.shape[0]
    place_in = lax.axis_index("tensor")
    devices = NX * NYL * 2
    core = place_in % 2
    x = (place_in // 2) % NX
    y = place_in // (2 * NX)
    table = jnp.stack(unit_table(x, y, core)).astype(jnp.int32)
    theirs = jnp.stack(unit_table(x, y, 1 - core)).astype(jnp.int32)

    weight = dequant(weight_codes, zero_points, step_sizes)
    pairs = [[2 * chip, 2 * chip + 1] for chip in range(NX * NYL)]
    chip_weight = lax.all_gather(weight, "tensor", axis=0, tiled=True, axis_index_groups=pairs)

    from_x = send(chip_weight, 1, 0)
    from_y = send(chip_weight, 0, 1)

    indices = place_in * tokens + jnp.arange(tokens, dtype=jnp.int32)
    mine = rope_back(key_cotangent, token_positions(doc_lengths[0], indices))
    rot = jnp.concatenate([mine, swap(mine)], axis=0)
    others = swap(activations)

    from_xy = send(from_y, 1, 0)
    from_yx = send(from_x, 0, 1, cross=True)

    grad, sent_near, sums_near = shards(
        table[:5], activations, others, rot, [weight, from_x, from_y], rows
    )
    got_near = swap(sent_near)

    def my_half(value):
        return lax.dynamic_slice_in_dim(value, core * rows, rows, axis=0)

    far_x = send(jnp.concatenate([from_xy, my_half(from_x)], axis=0), 1, 0)
    far_y = send(jnp.concatenate([from_xy, my_half(from_y)], axis=0), 0, 1)
    far = send(my_half(from_xy), 1, 1)

    grad, sent_mid, sums_mid = shards(
        table[5:9], activations, others, rot, [from_xy, from_yx], rows, grad
    )
    got_mid = swap(sent_mid)
    grad = place(theirs[:5], got_near, grad, rows)
    grad = place(theirs[5:9], got_mid, grad, rows)

    grad, sent_far, sums_far = shards(
        table[9:], activations, others, rot, [far_x, far_y, far], rows, grad
    )
    got_far = swap(sent_far)

    sums = spread(table, [sums_near, sums_mid, sums_far], devices)
    shares = lax.all_to_all(sums, "tensor", split_axis=0, concat_axis=0, tiled=True)
    share = jnp.sum(shares.astype(jnp.float32), axis=0).astype(jnp.bfloat16)
    copies = lax.axis_size("dp")
    totals = lax.all_to_all(
        jnp.broadcast_to(share[None], (copies, *share.shape)),
        "dp",
        split_axis=0,
        concat_axis=0,
        tiled=True,
    )
    seq_tokens = tokens * devices
    total = jnp.sum(totals.astype(jnp.float32), axis=0)
    step_grad = total / (seq_tokens * step_sizes)
    grad = place(theirs[9:], got_far, grad, rows)
    return (grad, step_grad)


def solution(mesh):
    in_specs = (
        P(("dp", "tensor"), None),
        P(("dp", "tensor"), None),
        P("dp", None),
        P("tensor", None),
        P("tensor", None),
        P("tensor", None),
    )
    out_specs = (P(("dp", "tensor"), None), P("tensor", None))
    return jax.shard_map(
        per_device, mesh=mesh, in_specs=in_specs, out_specs=out_specs, check_vma=False
    )
```

```python
import functools
import math

import jax
import jax.numpy as jnp
from jax import lax
from jax.experimental import pallas as pl
from jax.experimental.pallas import tpu as pltpu
from jax.sharding import PartitionSpec as P

HEAD = 128
GROUP = 64
AXES = ("dp", "tensor")
NX, NY, NYL, NZ = 4, 8, 4, 8
VMEM = 24 * 1024 * 1024
DEQUANT_VMEM = 56 * 1024 * 1024


def device_at(x, y, z, core):
    x, y, z = x % NX, y % NY, z % NZ
    dp = z * (NY // NYL) + y // NYL
    return dp * (NX * NYL * 2) + ((y % NYL) * NX + x) * 2 + core


def permutation(target):
    return [
        (device_at(x, y, z, core), device_at(*target(x, y, z, core)))
        for x in range(NX)
        for y in range(NY)
        for z in range(NZ)
        for core in range(2)
    ]


def send(value, dx, dy, cross=False):
    def target(x, y, z, core):
        sign = 1 if (core == 0) != cross else -1
        return x + sign * dx, y + sign * dy, z, core ^ int(cross)

    return lax.ppermute(value, AXES, permutation(target))


def swap(value):
    return lax.ppermute(value, AXES, permutation(lambda x, y, z, core: (x, y, z, core ^ 1)))


def token_positions(lengths, indices):
    count = lengths.shape[0]
    order = jnp.arange(count, dtype=jnp.int32)
    ends = jnp.sum(jnp.where(order[:, None] <= order[None, :], lengths[:, None], 0), axis=0)
    starts = jnp.where(ends[None, :] <= indices[:, None], ends[None, :], 0)
    return indices - jnp.max(starts, axis=1)


def rope_back(cotangent, positions):
    count = cotangent.shape[0]
    split = cotangent.astype(jnp.float32).reshape(count, -1, HEAD)
    middle = HEAD // 2
    freqs = jnp.exp(jnp.arange(middle, dtype=jnp.float32) * (-2.0 * math.log(10000.0) / HEAD))
    angles = positions.astype(jnp.float32)[:, None] * freqs[None, :]
    cosine = jnp.cos(angles)[:, None, :]
    sine = jnp.sin(angles)[:, None, :]
    first = split[..., :middle]
    second = split[..., middle:]
    lower = first * cosine + second * sine
    upper = second * cosine - first * sine
    return jnp.concatenate([lower, upper], axis=-1).reshape(count, -1).astype(jnp.bfloat16)


def dequant_kernel(codes_hbm, zeros_hbm, steps_hbm, weight_ref, codes, zeros, steps, sems):
    groups = zeros.shape[0]
    copies = [
        pltpu.make_async_copy(zeros_hbm, zeros, sems.at[0]),
        pltpu.make_async_copy(steps_hbm, steps, sems.at[1]),
    ]
    for group in range(groups):
        rows = pl.ds(group * GROUP, GROUP)
        copies.append(pltpu.make_async_copy(codes_hbm.at[rows], codes.at[rows], sems.at[2 + group]))
    for copy in copies:
        copy.start()
    copies[0].wait()
    copies[1].wait()
    for group in range(groups):
        rows = pl.ds(group * GROUP, GROUP)
        copies[2 + group].wait()
        levels = (codes[rows, :] - zeros[group : group + 1, :]).astype(jnp.float32)
        weight_ref[rows, :] = (steps[group : group + 1, :] * levels).astype(jnp.bfloat16)


def dequant(codes, zeros, steps):
    return pl.pallas_call(
        dequant_kernel,
        out_shape=jax.ShapeDtypeStruct(codes.shape, jnp.bfloat16),
        in_specs=[pl.BlockSpec(memory_space=pl.ANY)] * 3,
        out_specs=pl.BlockSpec(memory_space=pltpu.VMEM),
        scratch_shapes=[
            pltpu.VMEM(codes.shape, codes.dtype),
            pltpu.VMEM(zeros.shape, zeros.dtype),
            pltpu.VMEM(steps.shape, steps.dtype),
            pltpu.SemaphoreType.DMA((2 + zeros.shape[0],)),
        ],
        compiler_params=pltpu.CompilerParams(vmem_limit_bytes=DEQUANT_VMEM),
        name="dequant",
    )(codes, zeros, steps)


def units_of(weights, rows):
    return [(ref, at) for ref in weights for at in range(0, ref.shape[0], rows)]


def columns_of(table, unit, rows):
    return pl.ds(pl.multiple_of(table[unit] * rows, rows), rows)


def group_sums(table, unit, weight, mine_ref, other_ref, rot_ref):
    rows, cols = weight.shape
    columns = columns_of(table, unit, rows)
    feats = jnp.concatenate([mine_ref[:, columns], other_ref[:, columns]], axis=0)
    weight_grad = lax.dot_general(
        feats, rot_ref[...], (((0,), (0,)), ((), ())), preferred_element_type=jnp.float32
    )
    product = weight_grad * weight.astype(jnp.float32)
    return product.reshape(rows // GROUP, GROUP, cols).sum(axis=1)


def put_grad(table, unit, weight, rot_ref, own, sent_ref, grad_ref, sems):
    rows = weight.shape[0]
    tokens = own.shape[0]
    grad = lax.dot_general(
        rot_ref[...], weight, (((1,), (1,)), ((), ())), preferred_element_type=jnp.float32
    ).astype(jnp.bfloat16)
    block = pl.ds(unit * rows, rows)
    own[:, block] = grad[:tokens]
    sent_ref[:, block] = grad[tokens:]
    copy = pltpu.make_async_copy(
        own.at[:, block], grad_ref.at[:, columns_of(table, unit, rows)], sems.at[unit]
    )
    copy.start()
    return copy


def near_kernel(rows, count, table, mine_ref, other_ref, rot_ref, *refs):
    weights, (grad_ref, sent_ref, sums_ref, own, sems) = refs[:count], refs[count:]
    copies = []
    for unit, (ref, at) in enumerate(units_of(weights, rows)):
        weight = ref[at : at + rows, :]
        copies.append(put_grad(table, unit, weight, rot_ref, own, sent_ref, grad_ref, sems))
        sums_ref[unit] = group_sums(table, unit, weight, mine_ref, other_ref, rot_ref)
    for copy in copies:
        copy.wait()


def far_sums_kernel(rows, count, near, table, mine_ref, other_ref, rot_ref, *refs):
    weights, (near_ref, all_ref) = refs[:count], refs[count:]
    all_ref[...] = jnp.zeros_like(all_ref)
    for unit in range(near):
        all_ref[table[unit]] = near_ref[unit].astype(all_ref.dtype)
    for unit, (ref, at) in enumerate(units_of(weights, rows), near):
        weight = ref[at : at + rows, :]
        sums = group_sums(table, unit, weight, mine_ref, other_ref, rot_ref)
        all_ref[table[unit]] = sums.astype(all_ref.dtype)


def far_grad_kernel(rows, count, table, rot_ref, *refs):
    weights, (_, grad_ref, sent_ref, own, sems) = refs[:count], refs[count:]
    copies = []
    for unit, (ref, at) in enumerate(units_of(weights, rows)):
        weight = ref[at : at + rows, :]
        copies.append(put_grad(table, unit, weight, rot_ref, own, sent_ref, grad_ref, sems))
    for copy in copies:
        copy.wait()


def place_kernel(count, table, blocks_ref, grad_in, grad_ref, sems):
    rows = blocks_ref.shape[1] // count
    copies = [
        pltpu.make_async_copy(
            blocks_ref.at[:, pl.ds(unit * rows, rows)],
            grad_ref.at[:, columns_of(table, unit, rows)],
            sems.at[unit],
        )
        for unit in range(count)
    ]
    for copy in copies:
        copy.start()
    for copy in copies:
        copy.wait()


SMEM_SPEC = pl.BlockSpec(memory_space=pltpu.SMEM)
VMEM_SPEC = pl.BlockSpec(memory_space=pltpu.VMEM)
ANY_SPEC = pl.BlockSpec(memory_space=pl.ANY)


def cost(units, rows, cols, tokens, dots):
    return pl.CostEstimate(
        flops=4 * dots * units * rows * cols * tokens,
        bytes_accessed=units * rows * (cols * 2 + tokens * 4),
        transcendentals=0,
    )


def near_shards(table, mine, other, rot, weights, rows):
    tokens, width = mine.shape
    cols = rot.shape[1]
    total = sum(weight.shape[0] for weight in weights) // rows
    return pl.pallas_call(
        functools.partial(near_kernel, rows, len(weights)),
        out_shape=(
            jax.ShapeDtypeStruct((tokens, width), jnp.bfloat16),
            jax.ShapeDtypeStruct((tokens, total * rows), jnp.bfloat16),
            jax.ShapeDtypeStruct((total, rows // GROUP, cols), jnp.float32),
        ),
        in_specs=[SMEM_SPEC] + [VMEM_SPEC] * (3 + len(weights)),
        out_specs=(ANY_SPEC, VMEM_SPEC, VMEM_SPEC),
        scratch_shapes=[
            pltpu.VMEM((tokens, total * rows), jnp.bfloat16),
            pltpu.SemaphoreType.DMA((total,)),
        ],
        cost_estimate=cost(total, rows, cols, tokens, 2),
        compiler_params=pltpu.CompilerParams(vmem_limit_bytes=VMEM),
        name="near_shards",
    )(table, mine, other, rot, *weights)


def far_sums(table, mine, other, rot, weights, near_sums, rows, devices):
    tokens = mine.shape[0]
    groups, cols = near_sums.shape[1:]
    return pl.pallas_call(
        functools.partial(far_sums_kernel, rows, len(weights), near_sums.shape[0]),
        out_shape=jax.ShapeDtypeStruct((devices, groups, cols), jnp.bfloat16),
        in_specs=[SMEM_SPEC] + [VMEM_SPEC] * (4 + len(weights)),
        out_specs=VMEM_SPEC,
        cost_estimate=cost(devices // 4, rows, cols, tokens, 1),
        compiler_params=pltpu.CompilerParams(vmem_limit_bytes=VMEM),
        name="far_sums",
    )(table, mine, other, rot, *weights, near_sums)


def far_grad(table, rot, weights, grad, rows):
    tokens = grad.shape[0]
    cols = rot.shape[1]
    total = sum(weight.shape[0] for weight in weights) // rows
    return pl.pallas_call(
        functools.partial(far_grad_kernel, rows, len(weights)),
        out_shape=(
            jax.ShapeDtypeStruct(grad.shape, grad.dtype),
            jax.ShapeDtypeStruct((tokens, total * rows), jnp.bfloat16),
        ),
        in_specs=[SMEM_SPEC] + [VMEM_SPEC] * (1 + len(weights)) + [ANY_SPEC],
        out_specs=(ANY_SPEC, VMEM_SPEC),
        scratch_shapes=[
            pltpu.VMEM((tokens, total * rows), jnp.bfloat16),
            pltpu.SemaphoreType.DMA((total,)),
        ],
        input_output_aliases={2 + len(weights): 0},
        cost_estimate=cost(total, rows, cols, tokens, 1),
        compiler_params=pltpu.CompilerParams(vmem_limit_bytes=VMEM),
        name="far_grad",
    )(table, rot, *weights, grad)


def place(table, blocks, grad, rows):
    count = blocks.shape[1] // rows
    return pl.pallas_call(
        functools.partial(place_kernel, count),
        out_shape=jax.ShapeDtypeStruct(grad.shape, grad.dtype),
        in_specs=[SMEM_SPEC, ANY_SPEC, ANY_SPEC],
        out_specs=ANY_SPEC,
        scratch_shapes=[pltpu.SemaphoreType.DMA((count,))],
        input_output_aliases={2: 0},
        cost_estimate=pl.CostEstimate(
            flops=0, bytes_accessed=2 * blocks.size * 2, transcendentals=0
        ),
        compiler_params=pltpu.CompilerParams(vmem_limit_bytes=VMEM),
        name="place",
    )(table, blocks, grad)


def unit_table(x, y, core):
    sign = 2 * core - 1

    def owner(dx, dy, half):
        return (((y + sign * dy) % NYL) * NX + (x + sign * dx) % NX) * 2 + half

    return (
        [owner(0, 0, core)]
        + [owner(1, 0, 0), owner(1, 0, 1)]
        + [owner(0, 1, 0), owner(0, 1, 1)]
        + [owner(1, 1, 0), owner(1, 1, 1)]
        + [owner(-1, 1, 0), owner(-1, 1, 1)]
        + [owner(2, 0, core), owner(0, 2, core)]
        + [owner(2, 1, 0), owner(2, 1, 1)]
        + [owner(1, 2, 0), owner(1, 2, 1)]
        + [owner(2, 2, core)]
    )


def per_device(activations, key_cotangent, doc_lengths, weight_codes, zero_points, step_sizes):
    tokens = activations.shape[0]
    rows = weight_codes.shape[0]
    place_in = lax.axis_index("tensor")
    devices = NX * NYL * 2
    core = place_in % 2
    x = (place_in // 2) % NX
    y = place_in // (2 * NX)
    table = jnp.stack(unit_table(x, y, core)).astype(jnp.int32)
    theirs = jnp.stack(unit_table(x, y, 1 - core)).astype(jnp.int32)

    weight = dequant(weight_codes, zero_points, step_sizes)
    pairs = [[2 * chip, 2 * chip + 1] for chip in range(NX * NYL)]
    chip_weight = lax.all_gather(weight, "tensor", axis=0, tiled=True, axis_index_groups=pairs)

    from_x = send(chip_weight, 1, 0)
    from_y = send(chip_weight, 0, 1)

    indices = place_in * tokens + jnp.arange(tokens, dtype=jnp.int32)
    mine = rope_back(key_cotangent, token_positions(doc_lengths[0], indices))
    rot = jnp.concatenate([mine, swap(mine)], axis=0)
    others = swap(activations)
    from_x, from_y, rot = lax.optimization_barrier((from_x, from_y, rot))

    def my_half(value):
        return lax.dynamic_slice_in_dim(value, core * rows, rows, axis=0)

    from_xy = send(from_y, 1, 0)
    from_yx = send(from_x, 0, 1, cross=True)
    half_x, half_y = my_half(from_x), my_half(from_y)
    far_xx = send(half_x, 1, 0)
    far_yy = send(half_y, 0, 1)
    from_xy, far_xx, _ = lax.optimization_barrier((from_xy, far_xx, half_y))

    far_x = send(from_xy, 1, 0)
    far_y = send(from_xy, 0, 1)
    far = send(my_half(from_xy), 1, 1)

    near = [weight, from_x, from_y, from_xy, from_yx]
    grad, sent_near, sums_near = near_shards(table[:9], activations, others, rot, near, rows)
    got_near = swap(sent_near)
    grad = place(theirs[:9], got_near, grad, rows)

    fars = [far_xx, far_yy, far_x, far_y, far]
    sums = far_sums(table, activations, others, rot, fars, sums_near, rows, devices)
    shares = lax.all_to_all(sums, "tensor", split_axis=0, concat_axis=0, tiled=True)

    grad, sent_far = far_grad(table[9:], rot, fars, grad, rows)
    got_far = swap(sent_far)

    share = jnp.sum(shares.astype(jnp.float32), axis=0).astype(jnp.bfloat16)
    copies = lax.axis_size("dp")
    totals = lax.all_to_all(
        jnp.broadcast_to(share[None], (copies, *share.shape)),
        "dp",
        split_axis=0,
        concat_axis=0,
        tiled=True,
    )
    seq_tokens = tokens * devices
    total = jnp.sum(totals.astype(jnp.float32), axis=0)
    step_grad = total / (seq_tokens * step_sizes)
    grad = place(theirs[9:], got_far, grad, rows)
    return (grad, step_grad)


def solution(mesh):
    in_specs = (
        P(("dp", "tensor"), None),
        P(("dp", "tensor"), None),
        P("dp", None),
        P("tensor", None),
        P("tensor", None),
        P("tensor", None),
    )
    out_specs = (P(("dp", "tensor"), None), P("tensor", None))
    return jax.shard_map(
        per_device, mesh=mesh, in_specs=in_specs, out_specs=out_specs, check_vma=False
    )
```

```python
import functools
import math

import jax
import jax.numpy as jnp
from jax import lax
from jax.experimental import pallas as pl
from jax.experimental.pallas import tpu as pltpu
from jax.sharding import PartitionSpec as P

HEAD = 128
GROUP = 64
AXES = ("dp", "tensor")
NX, NY, NYL, NZ = 4, 8, 4, 8
VMEM = 12 * 1024 * 1024


def device_at(x, y, z, core):
    x, y, z = x % NX, y % NY, z % NZ
    dp = z * (NY // NYL) + y // NYL
    return dp * (NX * NYL * 2) + ((y % NYL) * NX + x) * 2 + core


def permutation(target):
    return [
        (device_at(x, y, z, core), device_at(*target(x, y, z, core)))
        for x in range(NX)
        for y in range(NY)
        for z in range(NZ)
        for core in range(2)
    ]


def send(value, dx, dy, cross=False):
    def target(x, y, z, core):
        sign = 1 if (core == 0) != cross else -1
        return x + sign * dx, y + sign * dy, z, core ^ int(cross)

    return lax.ppermute(value, AXES, permutation(target))


def swap(value):
    return lax.ppermute(value, AXES, permutation(lambda x, y, z, core: (x, y, z, core ^ 1)))


def token_positions(lengths, indices):
    count = lengths.shape[0]
    order = jnp.arange(count, dtype=jnp.int32)
    ends = jnp.sum(jnp.where(order[:, None] <= order[None, :], lengths[:, None], 0), axis=0)
    starts = jnp.where(ends[None, :] <= indices[:, None], ends[None, :], 0)
    return indices - jnp.max(starts, axis=1)


def rope_back(cotangent, positions):
    count = cotangent.shape[0]
    split = cotangent.astype(jnp.float32).reshape(count, -1, HEAD)
    middle = HEAD // 2
    freqs = jnp.exp(jnp.arange(middle, dtype=jnp.float32) * (-2.0 * math.log(10000.0) / HEAD))
    angles = positions.astype(jnp.float32)[:, None] * freqs[None, :]
    cosine = jnp.cos(angles)[:, None, :]
    sine = jnp.sin(angles)[:, None, :]
    first = split[..., :middle]
    second = split[..., middle:]
    lower = first * cosine + second * sine
    upper = second * cosine - first * sine
    return jnp.concatenate([lower, upper], axis=-1).reshape(count, -1).astype(jnp.bfloat16)


def dequant(codes, zeros, steps):
    groups, cols = zeros.shape
    levels = (codes.reshape(groups, GROUP, cols) - zeros[:, None, :]).astype(jnp.float32)
    return (steps[:, None, :] * levels).astype(jnp.bfloat16).reshape(codes.shape)


def columns_of(table, unit, rows):
    return pl.ds(pl.multiple_of(table[unit] * rows, rows), rows)


class Units:
    def __init__(self, rows, table, weights, held, sems, first=0):
        self.rows, self.table, self.held, self.first = rows, table, held, first
        self.copies = []
        for ref in weights:
            for at in range(0, ref.shape[0], rows):
                unit = len(self.copies)
                copy = pltpu.make_async_copy(
                    ref.at[pl.ds(at, rows)], held.at[pl.ds(unit * rows, rows)], sems.at[unit]
                )
                copy.start()
                self.copies.append(copy)
        self.count = len(self.copies)

    def load_features(self, mine, other, feats, sems):
        self.feats, self.feat_copies = feats, []
        tokens = mine.shape[0]
        for unit in range(self.count):
            columns = columns_of(self.table, self.first + unit, self.rows)
            block = pl.ds(unit * self.rows, self.rows)
            pair = [
                pltpu.make_async_copy(
                    ref.at[:, columns],
                    feats.at[pl.ds(core * tokens, tokens), block],
                    sems.at[2 * unit + core],
                )
                for core, ref in enumerate((mine, other))
            ]
            for copy in pair:
                copy.start()
            self.feat_copies.append(pair)

    def weight(self, unit):
        self.copies[unit].wait()
        return self.held[pl.ds(unit * self.rows, self.rows), :]

    def group_sums(self, unit, weight, rot):
        for copy in self.feat_copies[unit]:
            copy.wait()
        feats = self.feats[:, pl.ds(unit * self.rows, self.rows)]
        weight_grad = lax.dot_general(
            feats, rot, (((0,), (0,)), ((), ())), preferred_element_type=jnp.float32
        )
        product = weight_grad * weight.astype(jnp.float32)
        return product.reshape(self.rows // GROUP, GROUP, rot.shape[1]).sum(axis=1)

    def put_grad(self, unit, weight, rot, own, sent_ref, grad_ref, sems):
        tokens = own.shape[0]
        grad = lax.dot_general(
            rot, weight, (((1,), (1,)), ((), ())), preferred_element_type=jnp.float32
        ).astype(jnp.bfloat16)
        block = pl.ds(unit * self.rows, self.rows)
        own[:, block] = grad[:tokens]
        sent_ref[:, block] = grad[tokens:]
        columns = columns_of(self.table, self.first + unit, self.rows)
        copy = pltpu.make_async_copy(own.at[:, block], grad_ref.at[:, columns], sems.at[unit])
        copy.start()
        return copy


def near_kernel(rows, count, table, rot_ref, mine_ref, other_ref, *refs):
    weights, refs = refs[:count], refs[count:]
    grad_ref, sent_ref, sums_ref, held, feats, own, held_sems, feat_sems, own_sems = refs
    units = Units(rows, table, weights, held, held_sems)
    units.load_features(mine_ref, other_ref, feats, feat_sems)
    rot = rot_ref[...]
    copies = []
    for unit in range(units.count):
        weight = units.weight(unit)
        copies.append(units.put_grad(unit, weight, rot, own, sent_ref, grad_ref, own_sems))
        sums_ref[unit] = units.group_sums(unit, weight, rot)
    for copy in copies:
        copy.wait()


def far_sums_kernel(rows, count, near, table, rot_ref, near_ref, mine_ref, other_ref, *refs):
    weights, (all_ref, held, feats, held_sems, feat_sems) = refs[:count], refs[count:]
    units = Units(rows, table, weights, held, held_sems, near)
    units.load_features(mine_ref, other_ref, feats, feat_sems)
    all_ref[...] = jnp.zeros_like(all_ref)
    for unit in range(near):
        all_ref[table[unit]] = near_ref[unit].astype(all_ref.dtype)
    rot = rot_ref[...]
    for unit in range(units.count):
        sums = units.group_sums(unit, units.weight(unit), rot)
        all_ref[table[near + unit]] = sums.astype(all_ref.dtype)


def far_grad_kernel(rows, count, near, table, rot_ref, *refs):
    weights, refs = refs[:count], refs[count:]
    _, grad_ref, sent_ref, held, own, held_sems, own_sems = refs
    units = Units(rows, table, weights, held, held_sems, near)
    rot = rot_ref[...]
    copies = [
        units.put_grad(unit, units.weight(unit), rot, own, sent_ref, grad_ref, own_sems)
        for unit in range(units.count)
    ]
    for copy in copies:
        copy.wait()


SMEM_SPEC = pl.BlockSpec(memory_space=pltpu.SMEM)
VMEM_SPEC = pl.BlockSpec(memory_space=pltpu.VMEM)
ANY_SPEC = pl.BlockSpec(memory_space=pl.ANY)


def cost(units, rows, cols, tokens, dots):
    return pl.CostEstimate(
        flops=4 * dots * units * rows * cols * tokens,
        bytes_accessed=units * rows * (cols * 2 + tokens * 4),
        transcendentals=0,
    )


def scratch(units, rows, cols, tokens, feats, own):
    held = pltpu.VMEM((units * rows, cols), jnp.bfloat16)
    of_feats = pltpu.VMEM((2 * tokens, units * rows), jnp.bfloat16)
    of_own = pltpu.VMEM((tokens, units * rows), jnp.bfloat16)
    buffers = [held] + [of_feats] * feats + [of_own] * own
    sems = [units] + [2 * units] * feats + [units] * own
    return buffers + [pltpu.SemaphoreType.DMA((count,)) for count in sems]


def near_shards(table, mine, other, rot, weights, rows):
    tokens, width = mine.shape
    cols = rot.shape[1]
    total = sum(weight.shape[0] for weight in weights) // rows
    return pl.pallas_call(
        functools.partial(near_kernel, rows, len(weights)),
        out_shape=(
            jax.ShapeDtypeStruct((tokens, width), jnp.bfloat16),
            jax.ShapeDtypeStruct((tokens, total * rows), jnp.bfloat16),
            jax.ShapeDtypeStruct((total, rows // GROUP, cols), jnp.float32),
        ),
        in_specs=[SMEM_SPEC, VMEM_SPEC] + [ANY_SPEC] * (2 + len(weights)),
        out_specs=(ANY_SPEC, VMEM_SPEC, VMEM_SPEC),
        scratch_shapes=scratch(total, rows, cols, tokens, 1, 1),
        cost_estimate=cost(total, rows, cols, tokens, 2),
        compiler_params=pltpu.CompilerParams(vmem_limit_bytes=VMEM),
        name="near_shards",
    )(table, rot, mine, other, *weights)


def far_sums(table, mine, other, rot, weights, near_sums, rows, devices):
    tokens = mine.shape[0]
    near, groups, cols = near_sums.shape
    total = sum(weight.shape[0] for weight in weights) // rows
    return pl.pallas_call(
        functools.partial(far_sums_kernel, rows, len(weights), near),
        out_shape=jax.ShapeDtypeStruct((devices, groups, cols), jnp.bfloat16),
        in_specs=[SMEM_SPEC, VMEM_SPEC, VMEM_SPEC] + [ANY_SPEC] * (2 + len(weights)),
        out_specs=VMEM_SPEC,
        scratch_shapes=scratch(total, rows, cols, tokens, 1, 0),
        cost_estimate=cost(total, rows, cols, tokens, 1),
        compiler_params=pltpu.CompilerParams(vmem_limit_bytes=VMEM),
        name="far_sums",
    )(table, rot, near_sums, mine, other, *weights)


def far_grad(table, rot, weights, grad, rows, near):
    tokens = grad.shape[0]
    cols = rot.shape[1]
    total = sum(weight.shape[0] for weight in weights) // rows
    return pl.pallas_call(
        functools.partial(far_grad_kernel, rows, len(weights), near),
        out_shape=(
            jax.ShapeDtypeStruct(grad.shape, grad.dtype),
            jax.ShapeDtypeStruct((tokens, total * rows), jnp.bfloat16),
        ),
        in_specs=[SMEM_SPEC, VMEM_SPEC] + [ANY_SPEC] * (len(weights) + 1),
        out_specs=(ANY_SPEC, VMEM_SPEC),
        scratch_shapes=scratch(total, rows, cols, tokens, 0, 1),
        input_output_aliases={2 + len(weights): 0},
        cost_estimate=cost(total, rows, cols, tokens, 1),
        compiler_params=pltpu.CompilerParams(vmem_limit_bytes=VMEM),
        name="far_grad",
    )(table, rot, *weights, grad)


def place_kernel(count, first, table, blocks_ref, grad_in, grad_ref, sems):
    rows = blocks_ref.shape[1] // count
    copies = [
        pltpu.make_async_copy(
            blocks_ref.at[:, pl.ds(unit * rows, rows)],
            grad_ref.at[:, columns_of(table, first + unit, rows)],
            sems.at[unit],
        )
        for unit in range(count)
    ]
    for copy in copies:
        copy.start()
    for copy in copies:
        copy.wait()


def place(table, blocks, grad, rows, first):
    count = blocks.shape[1] // rows
    return pl.pallas_call(
        functools.partial(place_kernel, count, first),
        out_shape=jax.ShapeDtypeStruct(grad.shape, grad.dtype),
        in_specs=[SMEM_SPEC, VMEM_SPEC, ANY_SPEC],
        out_specs=ANY_SPEC,
        scratch_shapes=[pltpu.SemaphoreType.DMA((count,))],
        input_output_aliases={2: 0},
        cost_estimate=pl.CostEstimate(
            flops=0, bytes_accessed=2 * blocks.size * 2, transcendentals=0
        ),
        compiler_params=pltpu.CompilerParams(vmem_limit_bytes=VMEM),
        name="place",
    )(table, blocks, grad)


def unit_table(x, y, core):
    sign = 2 * core - 1

    def owner(dx, dy, half):
        return (((y + sign * dy) % NYL) * NX + (x + sign * dx) % NX) * 2 + half

    return (
        [owner(0, 0, core)]
        + [owner(1, 0, 0), owner(1, 0, 1)]
        + [owner(0, 1, 0), owner(0, 1, 1)]
        + [owner(1, 1, 0), owner(1, 1, 1)]
        + [owner(-1, 1, 0), owner(-1, 1, 1)]
        + [owner(2, 0, core), owner(0, 2, core)]
        + [owner(2, 1, 0), owner(2, 1, 1)]
        + [owner(-1, 2, 0), owner(-1, 2, 1)]
        + [owner(2, 2, core)]
    )


def per_device(activations, key_cotangent, doc_lengths, weight_codes, zero_points, step_sizes):
    tokens = activations.shape[0]
    rows = weight_codes.shape[0]
    place_in = lax.axis_index("tensor")
    devices = NX * NYL * 2
    core = place_in % 2
    x = (place_in // 2) % NX
    y = place_in // (2 * NX)
    table = jnp.stack(unit_table(x, y, core)).astype(jnp.int32)
    theirs = jnp.stack(unit_table(x, y, 1 - core)).astype(jnp.int32)

    weight = dequant(weight_codes, zero_points, step_sizes)
    pairs = [[2 * chip, 2 * chip + 1] for chip in range(NX * NYL)]
    chip_weight = lax.all_gather(weight, "tensor", axis=0, tiled=True, axis_index_groups=pairs)

    from_x = send(chip_weight, 1, 0)
    from_y = send(chip_weight, 0, 1)

    indices = place_in * tokens + jnp.arange(tokens, dtype=jnp.int32)
    mine = rope_back(key_cotangent, token_positions(doc_lengths[0], indices))
    rot = jnp.concatenate([mine, swap(mine)], axis=0)
    others = swap(activations)
    from_x, from_y, rot = lax.optimization_barrier((from_x, from_y, rot))

    def my_half(value):
        return lax.dynamic_slice_in_dim(value, core * rows, rows, axis=0)

    from_xy = send(from_y, 1, 0)
    from_yx = send(from_x, 0, 1, cross=True)
    far_xx = send(my_half(from_x), 1, 0)
    far_yy = send(my_half(from_y), 0, 1)
    from_xy, from_yx, _, _ = lax.optimization_barrier((from_xy, from_yx, far_xx, far_yy))

    far_x = send(from_xy, 1, 0)
    far_y = send(from_yx, 0, 1)
    far = send(my_half(from_xy), 1, 1)

    near = [weight, from_x, from_y, from_xy, from_yx]
    grad, sent_near, sums_near = near_shards(table, activations, others, rot, near, rows)
    got_near = swap(sent_near)
    grad = place(theirs, got_near, grad, rows, 0)

    fars = [far_xx, far_yy, far_x, far_y, far]
    at_hand = sums_near.shape[0]
    sums = far_sums(table, activations, others, rot, fars, sums_near, rows, devices)
    shares = lax.all_to_all(sums, "tensor", split_axis=0, concat_axis=0, tiled=True)

    grad, sent_far = far_grad(table, rot, fars, grad, rows, at_hand)
    got_far = swap(sent_far)

    share = jnp.sum(shares.astype(jnp.float32), axis=0).astype(jnp.bfloat16)
    copies = lax.axis_size("dp")
    totals = lax.all_to_all(
        jnp.broadcast_to(share[None], (copies, *share.shape)),
        "dp",
        split_axis=0,
        concat_axis=0,
        tiled=True,
    )
    seq_tokens = tokens * devices
    total = jnp.sum(totals.astype(jnp.float32), axis=0)
    step_grad = total / (seq_tokens * step_sizes)
    grad = place(theirs, got_far, grad, rows, at_hand)
    return (grad, step_grad)


def solution(mesh):
    in_specs = (
        P(("dp", "tensor"), None),
        P(("dp", "tensor"), None),
        P("dp", None),
        P("tensor", None),
        P("tensor", None),
        P("tensor", None),
    )
    out_specs = (P(("dp", "tensor"), None), P("tensor", None))
    return jax.shard_map(
        per_device, mesh=mesh, in_specs=in_specs, out_specs=out_specs, check_vma=False
    )
```

```python
import functools
import math

import jax
import jax.numpy as jnp
from jax import lax
from jax.experimental import pallas as pl
from jax.experimental.pallas import tpu as pltpu
from jax.sharding import PartitionSpec as P

HEAD = 128
GROUP = 64
AXES = ("dp", "tensor")
NX, NY, NYL, NZ = 4, 8, 4, 8
VMEM = 12 * 1024 * 1024


def device_at(x, y, z, core):
    x, y, z = x % NX, y % NY, z % NZ
    dp = z * (NY // NYL) + y // NYL
    return dp * (NX * NYL * 2) + ((y % NYL) * NX + x) * 2 + core


def permutation(target):
    return [
        (device_at(x, y, z, core), device_at(*target(x, y, z, core)))
        for x in range(NX)
        for y in range(NY)
        for z in range(NZ)
        for core in range(2)
    ]


def send(value, dx, dy, cross=False):
    def target(x, y, z, core):
        sign = 1 if (core == 0) != cross else -1
        return x + sign * dx, y + sign * dy, z, core ^ int(cross)

    return lax.ppermute(value, AXES, permutation(target))


def swap(value):
    return lax.ppermute(value, AXES, permutation(lambda x, y, z, core: (x, y, z, core ^ 1)))


def token_positions(lengths, indices):
    count = lengths.shape[0]
    order = jnp.arange(count, dtype=jnp.int32)
    ends = jnp.sum(jnp.where(order[:, None] <= order[None, :], lengths[:, None], 0), axis=0)
    starts = jnp.where(ends[None, :] <= indices[:, None], ends[None, :], 0)
    return indices - jnp.max(starts, axis=1)


def rope_back(cotangent, positions):
    count = cotangent.shape[0]
    split = cotangent.astype(jnp.float32).reshape(count, -1, HEAD)
    middle = HEAD // 2
    freqs = jnp.exp(jnp.arange(middle, dtype=jnp.float32) * (-2.0 * math.log(10000.0) / HEAD))
    angles = positions.astype(jnp.float32)[:, None] * freqs[None, :]
    cosine = jnp.cos(angles)[:, None, :]
    sine = jnp.sin(angles)[:, None, :]
    first = split[..., :middle]
    second = split[..., middle:]
    lower = first * cosine + second * sine
    upper = second * cosine - first * sine
    return jnp.concatenate([lower, upper], axis=-1).reshape(count, -1).astype(jnp.bfloat16)


def dequant(codes, zeros, steps):
    groups, cols = zeros.shape
    levels = (codes.reshape(groups, GROUP, cols) - zeros[:, None, :]).astype(jnp.float32)
    return (steps[:, None, :] * levels).astype(jnp.bfloat16).reshape(codes.shape)


def columns_of(table, unit, rows):
    return pl.ds(pl.multiple_of(table[unit] * rows, rows), rows)


class Units:
    def __init__(self, rows, table, weights, held, sems, first=0):
        self.rows, self.table, self.held, self.first = rows, table, held, first
        self.copies = []
        for ref in weights:
            for at in range(0, ref.shape[0], rows):
                unit = len(self.copies)
                copy = pltpu.make_async_copy(
                    ref.at[pl.ds(at, rows)], held.at[pl.ds(unit * rows, rows)], sems.at[unit]
                )
                copy.start()
                self.copies.append(copy)
        self.count = len(self.copies)

    def weight(self, unit):
        self.copies[unit].wait()
        return self.held[pl.ds(unit * self.rows, self.rows), :]

    def group_sums(self, unit, weight, rot, mine, other):
        block = pl.ds((self.first + unit) * self.rows, self.rows)
        feats = jnp.concatenate([mine[:, block], other[:, block]], axis=0)
        weight_grad = lax.dot_general(
            feats, rot, (((0,), (0,)), ((), ())), preferred_element_type=jnp.float32
        )
        product = weight_grad * weight.astype(jnp.float32)
        return product.reshape(self.rows // GROUP, GROUP, rot.shape[1]).sum(axis=1)

    def put_grad(self, unit, weight, rot, own, sent_ref, grad_ref, sems):
        tokens = own.shape[0]
        grad = lax.dot_general(
            rot, weight, (((1,), (1,)), ((), ())), preferred_element_type=jnp.float32
        ).astype(jnp.bfloat16)
        block = pl.ds(unit * self.rows, self.rows)
        own[:, block] = grad[:tokens]
        sent_ref[:, block] = grad[tokens:]
        columns = columns_of(self.table, self.first + unit, self.rows)
        copy = pltpu.make_async_copy(own.at[:, block], grad_ref.at[:, columns], sems.at[unit])
        copy.start()
        return copy


def pack_kernel(rows, table, theirs, feats_ref, mine_ref, sent_ref):
    for unit in range(mine_ref.shape[1] // rows):
        block = pl.ds(unit * rows, rows)
        mine_ref[:, block] = feats_ref[:, columns_of(table, unit, rows)]
        sent_ref[:, block] = feats_ref[:, columns_of(theirs, unit, rows)]


def near_kernel(rows, count, table, rot_ref, mine_ref, other_ref, *refs):
    weights, refs = refs[:count], refs[count:]
    grad_ref, sent_ref, sums_ref, held, own, held_sems, own_sems = refs
    units = Units(rows, table, weights, held, held_sems)
    rot = rot_ref[...]
    copies = []
    for unit in range(units.count):
        weight = units.weight(unit)
        copies.append(units.put_grad(unit, weight, rot, own, sent_ref, grad_ref, own_sems))
        sums_ref[unit] = units.group_sums(unit, weight, rot, mine_ref, other_ref)
    for copy in copies:
        copy.wait()


def far_sums_kernel(rows, count, near, table, rot_ref, near_ref, mine_ref, other_ref, *refs):
    weights, (all_ref, held, held_sems) = refs[:count], refs[count:]
    units = Units(rows, table, weights, held, held_sems, near)
    all_ref[...] = jnp.zeros_like(all_ref)
    for unit in range(near):
        all_ref[table[unit]] = near_ref[unit].astype(all_ref.dtype)
    rot = rot_ref[...]
    for unit in range(units.count):
        sums = units.group_sums(unit, units.weight(unit), rot, mine_ref, other_ref)
        all_ref[table[near + unit]] = sums.astype(all_ref.dtype)


def far_grad_kernel(rows, count, near, table, rot_ref, *refs):
    weights, refs = refs[:count], refs[count:]
    _, grad_ref, sent_ref, held, own, held_sems, own_sems = refs
    units = Units(rows, table, weights, held, held_sems, near)
    rot = rot_ref[...]
    copies = [
        units.put_grad(unit, units.weight(unit), rot, own, sent_ref, grad_ref, own_sems)
        for unit in range(units.count)
    ]
    for copy in copies:
        copy.wait()


SMEM_SPEC = pl.BlockSpec(memory_space=pltpu.SMEM)
VMEM_SPEC = pl.BlockSpec(memory_space=pltpu.VMEM)
ANY_SPEC = pl.BlockSpec(memory_space=pl.ANY)


def cost(units, rows, cols, tokens, dots):
    return pl.CostEstimate(
        flops=4 * dots * units * rows * cols * tokens,
        bytes_accessed=units * rows * (cols * 2 + tokens * 4),
        transcendentals=0,
    )


def scratch(units, rows, cols, tokens, own):
    buffers = [pltpu.VMEM((units * rows, cols), jnp.bfloat16)]
    buffers += [pltpu.VMEM((tokens, units * rows), jnp.bfloat16)] * own
    return buffers + [pltpu.SemaphoreType.DMA((units,))] * (1 + own)


def pack(table, theirs, feats, rows):
    packed = jax.ShapeDtypeStruct((feats.shape[0], table.shape[0] * rows), feats.dtype)
    return pl.pallas_call(
        functools.partial(pack_kernel, rows),
        out_shape=(packed, packed),
        in_specs=[SMEM_SPEC, SMEM_SPEC, VMEM_SPEC],
        out_specs=(VMEM_SPEC, VMEM_SPEC),
        cost_estimate=pl.CostEstimate(
            flops=0, bytes_accessed=3 * feats.size * 2, transcendentals=0
        ),
        compiler_params=pltpu.CompilerParams(vmem_limit_bytes=VMEM),
        name="pack",
    )(table, theirs, feats)


def near_shards(table, mine, other, rot, weights, rows, width):
    tokens = mine.shape[0]
    cols = rot.shape[1]
    total = sum(weight.shape[0] for weight in weights) // rows
    return pl.pallas_call(
        functools.partial(near_kernel, rows, len(weights)),
        out_shape=(
            jax.ShapeDtypeStruct((tokens, width), jnp.bfloat16),
            jax.ShapeDtypeStruct((tokens, total * rows), jnp.bfloat16),
            jax.ShapeDtypeStruct((total, rows // GROUP, cols), jnp.float32),
        ),
        in_specs=[SMEM_SPEC] + [VMEM_SPEC] * 3 + [ANY_SPEC] * len(weights),
        out_specs=(ANY_SPEC, VMEM_SPEC, VMEM_SPEC),
        scratch_shapes=scratch(total, rows, cols, tokens, 1),
        cost_estimate=cost(total, rows, cols, tokens, 2),
        compiler_params=pltpu.CompilerParams(vmem_limit_bytes=VMEM),
        name="near_shards",
    )(table, rot, mine, other, *weights)


def far_sums(table, mine, other, rot, weights, near_sums, rows, devices):
    tokens = mine.shape[0]
    near, groups, cols = near_sums.shape
    total = sum(weight.shape[0] for weight in weights) // rows
    return pl.pallas_call(
        functools.partial(far_sums_kernel, rows, len(weights), near),
        out_shape=jax.ShapeDtypeStruct((devices, groups, cols), jnp.bfloat16),
        in_specs=[SMEM_SPEC] + [VMEM_SPEC] * 4 + [ANY_SPEC] * len(weights),
        out_specs=VMEM_SPEC,
        scratch_shapes=scratch(total, rows, cols, tokens, 0),
        cost_estimate=cost(total, rows, cols, tokens, 1),
        compiler_params=pltpu.CompilerParams(vmem_limit_bytes=VMEM),
        name="far_sums",
    )(table, rot, near_sums, mine, other, *weights)


def far_grad(table, rot, weights, grad, rows, near):
    tokens = grad.shape[0]
    cols = rot.shape[1]
    total = sum(weight.shape[0] for weight in weights) // rows
    return pl.pallas_call(
        functools.partial(far_grad_kernel, rows, len(weights), near),
        out_shape=(
            jax.ShapeDtypeStruct(grad.shape, grad.dtype),
            jax.ShapeDtypeStruct((tokens, total * rows), jnp.bfloat16),
        ),
        in_specs=[SMEM_SPEC, VMEM_SPEC] + [ANY_SPEC] * (len(weights) + 1),
        out_specs=(ANY_SPEC, VMEM_SPEC),
        scratch_shapes=scratch(total, rows, cols, tokens, 1),
        input_output_aliases={2 + len(weights): 0},
        cost_estimate=cost(total, rows, cols, tokens, 1),
        compiler_params=pltpu.CompilerParams(vmem_limit_bytes=VMEM),
        name="far_grad",
    )(table, rot, *weights, grad)


def place_kernel(count, first, table, blocks_ref, grad_in, grad_ref, sems):
    rows = blocks_ref.shape[1] // count
    copies = [
        pltpu.make_async_copy(
            blocks_ref.at[:, pl.ds(unit * rows, rows)],
            grad_ref.at[:, columns_of(table, first + unit, rows)],
            sems.at[unit],
        )
        for unit in range(count)
    ]
    for copy in copies:
        copy.start()
    for copy in copies:
        copy.wait()


def place(table, blocks, grad, rows, first):
    count = blocks.shape[1] // rows
    return pl.pallas_call(
        functools.partial(place_kernel, count, first),
        out_shape=jax.ShapeDtypeStruct(grad.shape, grad.dtype),
        in_specs=[SMEM_SPEC, VMEM_SPEC, ANY_SPEC],
        out_specs=ANY_SPEC,
        scratch_shapes=[pltpu.SemaphoreType.DMA((count,))],
        input_output_aliases={2: 0},
        cost_estimate=pl.CostEstimate(
            flops=0, bytes_accessed=2 * blocks.size * 2, transcendentals=0
        ),
        compiler_params=pltpu.CompilerParams(vmem_limit_bytes=VMEM),
        name="place",
    )(table, blocks, grad)


def unit_table(x, y, core):
    sign = 2 * core - 1

    def owner(dx, dy, half):
        return (((y + sign * dy) % NYL) * NX + (x + sign * dx) % NX) * 2 + half

    return (
        [owner(0, 0, core)]
        + [owner(1, 0, 0), owner(1, 0, 1)]
        + [owner(0, 1, 0), owner(0, 1, 1)]
        + [owner(1, 1, 0), owner(1, 1, 1)]
        + [owner(-1, 1, 0), owner(-1, 1, 1)]
        + [owner(2, 0, core), owner(0, 2, core)]
        + [owner(2, 1, 0), owner(2, 1, 1)]
        + [owner(-1, 2, 0), owner(-1, 2, 1)]
        + [owner(2, 2, core)]
    )


def per_device(activations, key_cotangent, doc_lengths, weight_codes, zero_points, step_sizes):
    tokens = activations.shape[0]
    rows = weight_codes.shape[0]
    place_in = lax.axis_index("tensor")
    devices = NX * NYL * 2
    core = place_in % 2
    x = (place_in // 2) % NX
    y = place_in // (2 * NX)
    table = jnp.stack(unit_table(x, y, core)).astype(jnp.int32)
    theirs = jnp.stack(unit_table(x, y, 1 - core)).astype(jnp.int32)

    weight = dequant(weight_codes, zero_points, step_sizes)
    pairs = [[2 * chip, 2 * chip + 1] for chip in range(NX * NYL)]
    chip_weight = lax.all_gather(weight, "tensor", axis=0, tiled=True, axis_index_groups=pairs)

    from_x = send(chip_weight, 1, 0)
    from_y = send(chip_weight, 0, 1)

    indices = place_in * tokens + jnp.arange(tokens, dtype=jnp.int32)
    mine = rope_back(key_cotangent, token_positions(doc_lengths[0], indices))
    rot = jnp.concatenate([mine, swap(mine)], axis=0)
    mine_feats, their_feats = pack(table, theirs, activations, rows)
    feats = (mine_feats, swap(their_feats))
    from_x, from_y, rot, _ = lax.optimization_barrier((from_x, from_y, rot, their_feats))

    def my_half(value):
        return lax.dynamic_slice_in_dim(value, core * rows, rows, axis=0)

    from_xy = send(from_y, 1, 0)
    from_yx = send(from_x, 0, 1, cross=True)
    far_xx = send(my_half(from_x), 1, 0)
    far_yy = send(my_half(from_y), 0, 1)
    from_xy, from_yx, _, _ = lax.optimization_barrier((from_xy, from_yx, far_xx, far_yy))

    far_x = send(from_xy, 1, 0)
    far_y = send(from_yx, 0, 1)
    far = send(my_half(from_xy), 1, 1)

    near = [weight, from_x, from_y, from_xy, from_yx]
    grad, sent_near, sums_near = near_shards(table, *feats, rot, near, rows, activations.shape[1])
    got_near = swap(sent_near)
    grad = place(theirs, got_near, grad, rows, 0)

    fars = [far_xx, far_yy, far_x, far_y, far]
    at_hand = sums_near.shape[0]
    sums = far_sums(table, *feats, rot, fars, sums_near, rows, devices)
    shares = lax.all_to_all(sums, "tensor", split_axis=0, concat_axis=0, tiled=True)

    grad, sent_far = far_grad(table, rot, fars, grad, rows, at_hand)
    shares, grad, sent_far = lax.optimization_barrier((shares, grad, sent_far))
    share = jnp.sum(shares.astype(jnp.float32), axis=0).astype(jnp.bfloat16)
    copies = lax.axis_size("dp")
    totals = lax.all_to_all(
        jnp.broadcast_to(share[None], (copies, *share.shape)),
        "dp",
        split_axis=0,
        concat_axis=0,
        tiled=True,
    )
    grad = place(theirs, swap(sent_far), grad, rows, at_hand)
    totals, grad = lax.optimization_barrier((totals, grad))
    seq_tokens = tokens * devices
    total = jnp.sum(totals.astype(jnp.float32), axis=0)
    step_grad = total / (seq_tokens * step_sizes)
    return (grad, step_grad)


def solution(mesh):
    in_specs = (
        P(("dp", "tensor"), None),
        P(("dp", "tensor"), None),
        P("dp", None),
        P("tensor", None),
        P("tensor", None),
        P("tensor", None),
    )
    out_specs = (P(("dp", "tensor"), None), P("tensor", None))
    return jax.shard_map(
        per_device, mesh=mesh, in_specs=in_specs, out_specs=out_specs, check_vma=False
    )
```

```python
import functools
import math

import jax
import jax.numpy as jnp
from jax import lax
from jax.experimental import pallas as pl
from jax.experimental.pallas import tpu as pltpu
from jax.sharding import PartitionSpec as P

HEAD = 128
GROUP = 64
AXES = ("dp", "tensor")
NX, NY, NYL, NZ = 4, 8, 4, 8
HALF = 128
DEVICES = 4
VMEM = 16 * 1024 * 1024


def device_at(x, y, z, core):
    x, y, z = x % NX, y % NY, z % NZ
    dp = z * (NY // NYL) + y // NYL
    return dp * (NX * NYL * 2) + ((y % NYL) * NX + x) * 2 + core


def permutation(target):
    return [
        (device_at(x, y, z, core), device_at(*target(x, y, z, core)))
        for x in range(NX)
        for y in range(NY)
        for z in range(NZ)
        for core in range(2)
    ]


def send(value, dx, dy, cross=False):
    def target(x, y, z, core):
        sign = 1 if (core == 0) != cross else -1
        return x + sign * dx, y + sign * dy, z, core ^ int(cross)

    return lax.ppermute(value, AXES, permutation(target))


def swap(value, core, plane):
    def target(x, y, z, own):
        return x, y, z ^ plane, own ^ core

    return lax.ppermute(value, AXES, permutation(target))


def token_positions(lengths, indices):
    count = lengths.shape[0]
    order = jnp.arange(count, dtype=jnp.int32)
    ends = jnp.sum(jnp.where(order[:, None] <= order[None, :], lengths[:, None], 0), axis=0)
    starts = jnp.where(ends[None, :] <= indices[:, None], ends[None, :], 0)
    return indices - jnp.max(starts, axis=1)


def rope_back(cotangent, positions):
    count = cotangent.shape[0]
    split = cotangent.astype(jnp.float32).reshape(count, -1, HEAD)
    middle = HEAD // 2
    freqs = jnp.exp(jnp.arange(middle, dtype=jnp.float32) * (-2.0 * math.log(10000.0) / HEAD))
    angles = positions.astype(jnp.float32)[:, None] * freqs[None, :]
    cosine = jnp.cos(angles)[:, None, :]
    sine = jnp.sin(angles)[:, None, :]
    first = split[..., :middle]
    second = split[..., middle:]
    lower = first * cosine + second * sine
    upper = second * cosine - first * sine
    return jnp.concatenate([lower, upper], axis=-1).reshape(count, -1).astype(jnp.bfloat16)


def dequant(codes, zeros, steps):
    groups, cols = zeros.shape
    levels = (codes.reshape(groups, GROUP, cols) - zeros[:, None, :]).astype(jnp.float32)
    return (steps[:, None, :] * levels).astype(jnp.bfloat16).reshape(codes.shape)


def columns_of(tables, device, unit, rows):
    return pl.ds(pl.multiple_of(tables[device, unit] * HALF, HALF), rows)


def blocks_of(sizes):
    return [pl.ds(sum(sizes[:unit]), size) for unit, size in enumerate(sizes)]


def load(weights, held, sems):
    blocks = blocks_of([ref.shape[0] for ref in weights])
    copies = [
        pltpu.make_async_copy(ref, held.at[block], sems.at[unit])
        for unit, (ref, block) in enumerate(zip(weights, blocks))
    ]
    for copy in copies:
        copy.start()
    for copy in copies:
        copy.wait()
    return blocks


def group_sums(feats, weight, rot):
    weight_grad = lax.dot_general(
        feats, rot, (((0,), (0,)), ((), ())), preferred_element_type=jnp.float32
    )
    product = weight_grad * weight.astype(jnp.float32)
    rows, cols = weight.shape
    return product.reshape(rows // HALF, HALF // GROUP, GROUP, cols).sum(axis=2)


def put_grads(tables, first, blocks, held, rot, grads, sent, grad_ref, sems):
    for block in blocks:
        grads[:, block] = lax.dot_general(
            rot, held[block, :], (((1,), (1,)), ((), ())), preferred_element_type=jnp.float32
        ).astype(jnp.bfloat16)
    tokens = grad_ref.shape[0]
    copies = [
        pltpu.make_async_copy(
            grads.at[pl.ds(0, tokens), block],
            grad_ref.at[:, columns_of(tables, 0, first + unit, block.size)],
            sems.at[unit],
        )
        for unit, block in enumerate(blocks)
    ]
    copies += [
        pltpu.make_async_copy(
            grads.at[pl.ds(part * tokens, tokens)], ref, sems.at[len(blocks) + part - 1]
        )
        for part, ref in enumerate(sent, 1)
    ]
    for copy in copies:
        copy.start()
    return copies


def pack_kernel(sizes, tables, feats_ref, rot_ref, mine_ref, core_ref, plane_ref):
    width = sum(sizes)
    outs = ((mine_ref, 0), (core_ref, 0), (plane_ref, 0), (plane_ref, width))
    for device, (ref, at) in enumerate(outs):
        for unit, block in enumerate(blocks_of(sizes)):
            columns = columns_of(tables, device, unit, block.size)
            ref[:, pl.ds(at + block.start, block.size)] = feats_ref[:, columns]
    core_ref[:, width:] = rot_ref[...]
    plane_ref[:, 2 * width :] = rot_ref[...]


def near_kernel(count, tables, *refs):
    feats = refs[:1] + refs[2 : DEVICES + 1]
    rots, refs = refs[1 : DEVICES + 1], refs[DEVICES + 1 :]
    weights, refs = refs[:count], refs[count:]
    grad_ref, sums_ref, rot_ref, feats_ref, *sent, held, grads, held_sems, grad_sems = refs
    blocks = load(weights, held, held_sems)
    cols = held.shape[1]
    rot = jnp.concatenate([ref[:, ref.shape[1] - cols :] for ref in rots], axis=0)
    near, far = held.shape[0], feats_ref.shape[1]
    copies = put_grads(tables, 0, blocks, held, rot, grads, sent, grad_ref, grad_sems)
    for block in blocks:
        columns = jnp.concatenate([ref[:, block] for ref in feats], axis=0)
        at = block.start // HALF
        sums_ref[at : at + block.size // HALF] = group_sums(columns, held[block, :], rot)
    rot_ref[...] = rot
    for part, ref in enumerate(feats):
        tokens = pl.ds(part * ref.shape[0], ref.shape[0])
        feats_ref[tokens, :] = ref[:, near : near + far]
    for copy in copies:
        copy.wait()


def far_sums_kernel(near, count, tables, rot_ref, feats_ref, near_ref, *refs):
    weights, (all_ref, held, sems) = refs[:count], refs[count:]
    blocks = load(weights, held, sems)
    all_ref[...] = jnp.zeros_like(all_ref)
    rot = rot_ref[...]
    sums = [near_ref[...]]
    sums += [group_sums(feats_ref[:, block], held[block, :], rot) for block in blocks]
    sizes = near + tuple(block.size for block in blocks)
    sums = jnp.concatenate(sums, axis=0).astype(all_ref.dtype)
    at = 0
    for unit, size in enumerate(sizes):
        for half in range(size // HALF):
            all_ref[tables[0, unit] + half] = sums[at]
            at += 1


def far_grad_kernel(near, count, tables, rot_ref, *refs):
    weights, refs = refs[:count], refs[count:]
    _, grad_ref, *sent, held, grads, held_sems, grad_sems = refs
    blocks = load(weights, held, held_sems)
    rot = rot_ref[...]
    copies = put_grads(tables, near, blocks, held, rot, grads, sent, grad_ref, grad_sems)
    for copy in copies:
        copy.wait()


def place_kernel(sizes, first, tables, *refs):
    *parts, _, grad_ref, sems = refs
    copies = [
        pltpu.make_async_copy(
            ref.at[:, block],
            grad_ref.at[:, columns_of(tables, device, first + unit, block.size)],
            sems.at[device - 1, unit],
        )
        for device, ref in enumerate(parts, 1)
        for unit, block in enumerate(blocks_of(sizes))
    ]
    for copy in copies:
        copy.start()
    for copy in copies:
        copy.wait()


SMEM_SPEC = pl.BlockSpec(memory_space=pltpu.SMEM)
VMEM_SPEC = pl.BlockSpec(memory_space=pltpu.VMEM)
ANY_SPEC = pl.BlockSpec(memory_space=pl.ANY)
PARAMS = pltpu.CompilerParams(vmem_limit_bytes=VMEM)


def cost(rows, cols, tokens, dots):
    return pl.CostEstimate(
        flops=2 * DEVICES * dots * rows * cols * tokens,
        bytes_accessed=rows * (cols * 2 + tokens * 2 * DEVICES),
        transcendentals=0,
    )


def scratch(weights, tokens, own):
    rows, cols = sum(weight.shape[0] for weight in weights), weights[0].shape[1]
    buffers = [pltpu.VMEM((rows, cols), jnp.bfloat16)]
    sems = [pltpu.SemaphoreType.DMA((len(weights),))]
    if own:
        buffers.append(pltpu.VMEM((DEVICES * tokens, rows), jnp.bfloat16))
        sems.append(pltpu.SemaphoreType.DMA((len(weights) + DEVICES - 1,)))
    return buffers + sems


def pack(tables, feats, rot, sizes):
    tokens, width, cols = feats.shape[0], sum(sizes), rot.shape[1]
    widths = (width, width + cols, 2 * width + cols)
    return pl.pallas_call(
        functools.partial(pack_kernel, sizes),
        out_shape=tuple(jax.ShapeDtypeStruct((tokens, size), feats.dtype) for size in widths),
        in_specs=[SMEM_SPEC, VMEM_SPEC, VMEM_SPEC],
        out_specs=(VMEM_SPEC,) * 3,
        cost_estimate=pl.CostEstimate(
            flops=0, bytes_accessed=2 * feats.size * 2, transcendentals=0
        ),
        compiler_params=PARAMS,
        name="pack",
    )(tables, feats, rot)


def near_shards(tables, feats, rot, weights, width, far):
    tokens, cols = rot.shape
    rows = sum(weight.shape[0] for weight in weights)
    return pl.pallas_call(
        functools.partial(near_kernel, len(weights)),
        out_shape=(
            jax.ShapeDtypeStruct((tokens, width), jnp.bfloat16),
            jax.ShapeDtypeStruct((rows // HALF, HALF // GROUP, cols), jnp.float32),
            jax.ShapeDtypeStruct((DEVICES * tokens, cols), jnp.bfloat16),
            jax.ShapeDtypeStruct((DEVICES * tokens, far), jnp.bfloat16),
        )
        + (jax.ShapeDtypeStruct((tokens, rows), jnp.bfloat16),) * (DEVICES - 1),
        in_specs=[SMEM_SPEC] + [VMEM_SPEC] * (DEVICES + 1) + [ANY_SPEC] * len(weights),
        out_specs=(ANY_SPEC,) + (VMEM_SPEC,) * 3 + (ANY_SPEC,) * (DEVICES - 1),
        scratch_shapes=scratch(weights, tokens, 1),
        cost_estimate=cost(rows, cols, tokens, 2),
        compiler_params=PARAMS,
        name="near_shards",
    )(tables, feats[0], rot, *feats[1:], *weights)


def far_sums(tables, rot, feats, weights, near_sums, near_sizes, halves):
    tokens, cols = rot.shape
    rows = feats.shape[1]
    return pl.pallas_call(
        functools.partial(far_sums_kernel, near_sizes, len(weights)),
        out_shape=jax.ShapeDtypeStruct((halves, HALF // GROUP, cols), jnp.bfloat16),
        in_specs=[SMEM_SPEC] + [VMEM_SPEC] * 3 + [ANY_SPEC] * len(weights),
        out_specs=VMEM_SPEC,
        scratch_shapes=scratch(weights, tokens, 0),
        cost_estimate=cost(rows, cols, tokens // DEVICES, 1),
        compiler_params=PARAMS,
        name="far_sums",
    )(tables, rot, feats, near_sums, *weights)


def far_grad(tables, rot, weights, grad, near):
    tokens, cols = grad.shape[0], rot.shape[1]
    rows = sum(weight.shape[0] for weight in weights)
    return pl.pallas_call(
        functools.partial(far_grad_kernel, near, len(weights)),
        out_shape=(jax.ShapeDtypeStruct(grad.shape, grad.dtype),)
        + (jax.ShapeDtypeStruct((tokens, rows), jnp.bfloat16),) * (DEVICES - 1),
        in_specs=[SMEM_SPEC, VMEM_SPEC] + [ANY_SPEC] * (len(weights) + 1),
        out_specs=(ANY_SPEC,) * DEVICES,
        scratch_shapes=scratch(weights, tokens, 1),
        input_output_aliases={2 + len(weights): 0},
        cost_estimate=cost(rows, cols, tokens, 1),
        compiler_params=PARAMS,
        name="far_grad",
    )(tables, rot, *weights, grad)


def place(tables, blocks, grad, sizes, first):
    return pl.pallas_call(
        functools.partial(place_kernel, sizes, first),
        out_shape=jax.ShapeDtypeStruct(grad.shape, grad.dtype),
        in_specs=[SMEM_SPEC] + [VMEM_SPEC] * len(blocks) + [ANY_SPEC],
        out_specs=ANY_SPEC,
        scratch_shapes=[pltpu.SemaphoreType.DMA((len(blocks), len(sizes)))],
        input_output_aliases={1 + len(blocks): 0},
        cost_estimate=pl.CostEstimate(
            flops=0, bytes_accessed=4 * len(blocks) * blocks[0].size, transcendentals=0
        ),
        compiler_params=PARAMS,
        name="place",
    )(tables, *blocks, grad)


def unit_table(x, y, core, plane):
    sign = 2 * core - 1

    def owner(dx, dy, half=0):
        chip = ((y + sign * dy) % NYL) * NX + (x + sign * dx) % NX
        return (chip * 2 + plane) * 2 + half

    near = [owner(0, 0, core), owner(1, 0), owner(0, 1), owner(1, 1), owner(-1, 1)]
    far = [owner(2, 0, core), owner(0, 2, core), owner(2, 1), owner(-1, 2), owner(2, 2, core)]
    return jnp.stack(near + far).astype(jnp.int32)


def per_device(activations, key_cotangent, doc_lengths, weight_codes, zero_points, step_sizes):
    tokens, width = activations.shape
    rows = weight_codes.shape[0]
    devices = NX * NYL * 2
    place_in = lax.axis_index("tensor")
    core = place_in % 2
    x = (place_in // 2) % NX
    y = place_in // (2 * NX)
    plane = (lax.axis_index("dp") // (NY // NYL)) % 2
    others = [(core, plane), (1 - core, plane), (core, 1 - plane), (1 - core, 1 - plane)]
    tables = jnp.stack([unit_table(x, y, *at) for at in others])
    near_sizes = (HALF, rows, rows, rows, rows)
    far_sizes = (HALF, HALF, rows, rows, HALF)
    sizes = near_sizes + far_sizes

    weight = dequant(weight_codes, zero_points, step_sizes)
    pairs = [[2 * chip, 2 * chip + 1] for chip in range(NX * NYL)]
    both = lax.all_gather(weight, "tensor", axis=0, tiled=True, axis_index_groups=pairs)
    chip_weight = lax.dynamic_slice_in_dim(both, plane * rows, rows, axis=0)

    def my_half(value):
        return lax.dynamic_slice_in_dim(value, core * HALF, HALF, axis=0)

    chip_weight, key_cotangent, activations = lax.optimization_barrier(
        (chip_weight, key_cotangent, activations)
    )
    from_x = send(chip_weight, 1, 0)
    from_y = send(chip_weight, 0, 1)

    indices = place_in * tokens + jnp.arange(tokens, dtype=jnp.int32)
    mine = rope_back(key_cotangent, token_positions(doc_lengths[0], indices))
    feats, for_core, for_plane = pack(tables, activations, mine, sizes)
    from_plane = swap(for_plane, 0, 1)
    from_core = swap(for_core, 1, 0)
    from_x, from_y, _ = lax.optimization_barrier((from_x, from_y, for_plane))

    from_xy = send(from_y, 1, 0)
    from_yx = send(from_x, 0, 1, cross=True)
    far_xx = send(my_half(from_x), 1, 0)
    far_yy = send(my_half(from_y), 0, 1)
    from_xy, from_yx, _, _ = lax.optimization_barrier((from_xy, from_yx, far_xx, far_yy))

    far_x = send(from_xy, 1, 0)
    far_y = send(from_yx, 0, 1)
    half_xy = my_half(from_xy)
    far = send(half_xy, 1, 1)

    for_both, _, _ = lax.optimization_barrier((from_plane, half_xy, from_yx))
    from_both = swap(for_both[:, sum(sizes) :], 1, 0)
    tokens_feats = [feats, from_core, from_plane, from_both]
    near = [my_half(chip_weight), from_x, from_y, from_xy, from_yx]
    grad, near_sums, rot, far_feats, *near_sent = near_shards(
        tables, tokens_feats, mine, near, width, sum(far_sizes)
    )
    near_got = [swap(near_sent[0], 1, 0), swap(near_sent[1], 0, 1), swap(near_sent[2], 1, 1)]
    grad = place(tables, near_got, grad, near_sizes, 0)

    fars = [far_xx, far_yy, far_x, far_y, far]
    halves = devices * rows // HALF
    sums = far_sums(tables, rot, far_feats, fars, near_sums, near_sizes, halves)
    shares = lax.all_to_all(sums, "tensor", split_axis=0, concat_axis=0, tiled=True)

    grad, *far_sent = far_grad(tables, rot, fars, grad, len(near))
    shares, grad, *far_sent = lax.optimization_barrier((shares, grad, *far_sent))
    shares = shares.astype(jnp.float32).reshape(devices, rows // GROUP, -1)
    share = jnp.sum(shares, axis=0).astype(jnp.bfloat16)
    copies = lax.axis_size("dp")
    totals = lax.all_to_all(
        jnp.broadcast_to(share[None], (copies, *share.shape)),
        "dp",
        split_axis=0,
        concat_axis=0,
        tiled=True,
    )
    far_got = [swap(far_sent[0], 1, 0), swap(far_sent[1], 0, 1), swap(far_sent[2], 1, 1)]
    grad = place(tables, far_got, grad, far_sizes, len(near))
    totals, grad = lax.optimization_barrier((totals, grad))
    seq_tokens = tokens * devices
    total = jnp.sum(totals.astype(jnp.float32), axis=0)
    step_grad = total / (seq_tokens * step_sizes)
    return (grad, step_grad)


def solution(mesh):
    in_specs = (
        P(("dp", "tensor"), None),
        P(("dp", "tensor"), None),
        P("dp", None),
        P("tensor", None),
        P("tensor", None),
        P("tensor", None),
    )
    out_specs = (P(("dp", "tensor"), None), P("tensor", None))
    return jax.shard_map(
        per_device, mesh=mesh, in_specs=in_specs, out_specs=out_specs, check_vma=False
    )
```

```python
import functools
import math

import jax
import jax.numpy as jnp
from jax import lax
from jax.experimental import pallas as pl
from jax.experimental.pallas import tpu as pltpu
from jax.sharding import PartitionSpec as P

HEAD = 128
GROUP = 64
AXES = ("dp", "tensor")
SPLIT_Y = 2
CHUNK = 512
VMEM = 56 * 1024 * 1024
PARAMS = pltpu.CompilerParams(vmem_limit_bytes=VMEM)
SMEM_SPEC = pl.BlockSpec(memory_space=pltpu.SMEM)
VMEM_SPEC = pl.BlockSpec(memory_space=pltpu.VMEM)
ANY_SPEC = pl.BlockSpec(memory_space=pl.ANY)


def swap(value):
    count = lax.axis_size("dp")
    pairs = [(dp, (dp // SPLIT_Y ^ 1) * SPLIT_Y + dp % SPLIT_Y) for dp in range(count)]
    return lax.ppermute(value, "dp", pairs)


def token_positions(lengths, indices):
    count = lengths.shape[0]
    order = jnp.arange(count, dtype=jnp.int32)
    ends = jnp.sum(jnp.where(order[:, None] <= order[None, :], lengths[:, None], 0), axis=0)
    starts = jnp.where(ends[None, :] <= indices[:, None], ends[None, :], 0)
    return indices - jnp.max(starts, axis=1)


def rope_back(cotangent, positions):
    count = cotangent.shape[0]
    split = cotangent.astype(jnp.float32).reshape(count, -1, HEAD)
    middle = HEAD // 2
    freqs = jnp.exp(jnp.arange(middle, dtype=jnp.float32) * (-2.0 * math.log(10000.0) / HEAD))
    angles = positions.astype(jnp.float32)[:, None] * freqs[None, :]
    cosine = jnp.cos(angles)[:, None, :]
    sine = jnp.sin(angles)[:, None, :]
    first = split[..., :middle]
    second = split[..., middle:]
    lower = first * cosine + second * sine
    upper = second * cosine - first * sine
    return jnp.concatenate([lower, upper], axis=-1).reshape(count, -1).astype(jnp.bfloat16)


def dequant(codes, zeros, steps):
    groups, cols = zeros.shape
    levels = (codes.reshape(groups, GROUP, cols) - zeros[:, None, :]).astype(jnp.float32)
    return (steps[:, None, :] * levels).astype(jnp.bfloat16).reshape(codes.shape)


def columns_of(plane, unit, rows):
    return pl.ds(pl.multiple_of(unit * 2 * rows + plane * rows, rows), rows)


def pack_kernel(rows, plane_ref, feats_ref, rot_ref, mine_ref, other_ref):
    plane = plane_ref[0]
    width = mine_ref.shape[1]
    for unit in range(width // rows):
        block = pl.ds(unit * rows, rows)
        mine_ref[:, block] = feats_ref[:, columns_of(plane, unit, rows)]
        other_ref[:, block] = feats_ref[:, columns_of(1 - plane, unit, rows)]
    other_ref[:, width:] = rot_ref[...]


def pack(plane, feats, rot, rows):
    tokens, width = feats.shape
    cols = rot.shape[1]
    return pl.pallas_call(
        functools.partial(pack_kernel, rows),
        out_shape=(
            jax.ShapeDtypeStruct((tokens, width // 2), feats.dtype),
            jax.ShapeDtypeStruct((tokens, width // 2 + cols), feats.dtype),
        ),
        in_specs=[SMEM_SPEC, VMEM_SPEC, VMEM_SPEC],
        out_specs=(VMEM_SPEC, VMEM_SPEC),
        cost_estimate=pl.CostEstimate(
            flops=0, bytes_accessed=4 * feats.size, transcendentals=0
        ),
        compiler_params=PARAMS,
        name="pack",
    )(plane, feats, rot)


def load(weight_ref, held, sems):
    copies = []
    for at in range(0, held.shape[0], CHUNK):
        rows = pl.ds(at, CHUNK)
        copy = pltpu.make_async_copy(weight_ref.at[rows], held.at[rows], sems.at[at // CHUNK])
        copy.start()
        copies.append((rows, copy))
    return copies


def sums_kernel(mine_ref, rot_ref, other_ref, weight_ref, sums_ref, held, sems):
    width, cols = held.shape
    rot = jnp.concatenate([rot_ref[...], other_ref[:, width:]], axis=0)
    units, groups = sums_ref.shape[:2]
    per_chunk = CHUNK // (groups * GROUP)
    for rows, copy in load(weight_ref, held, sems):
        copy.wait()
        feats = jnp.concatenate([mine_ref[:, rows], other_ref[:, rows]], axis=0)
        weight_grad = lax.dot_general(
            feats, rot, (((0,), (0,)), ((), ())), preferred_element_type=jnp.float32
        )
        product = weight_grad * held[rows, :].astype(jnp.float32)
        sums = product.reshape(per_chunk, groups, GROUP, cols).sum(axis=2)
        first = rows.start // (groups * GROUP)
        sums_ref[first : first + per_chunk] = sums.astype(sums_ref.dtype)


def group_sums(mine, rot, other, weight, rows):
    tokens, cols = rot.shape
    width = weight.shape[0]
    return pl.pallas_call(
        sums_kernel,
        out_shape=jax.ShapeDtypeStruct((width // rows, rows // GROUP, cols), jnp.bfloat16),
        in_specs=[VMEM_SPEC] * 3 + [ANY_SPEC],
        out_specs=VMEM_SPEC,
        scratch_shapes=[
            pltpu.VMEM(weight.shape, weight.dtype),
            pltpu.SemaphoreType.DMA((width // CHUNK,)),
        ],
        cost_estimate=pl.CostEstimate(
            flops=4 * width * cols * tokens, bytes_accessed=weight.size * 2, transcendentals=0
        ),
        compiler_params=PARAMS,
        name="group_sums",
    )(mine, rot, other, weight)


def grads_kernel(rot_ref, other_ref, weight_ref, mine_ref, sent_ref, held, sems):
    width = held.shape[0]
    tokens = rot_ref.shape[0]
    rot = jnp.concatenate([rot_ref[...], other_ref[:, width:]], axis=0)
    for rows, copy in load(weight_ref, held, sems):
        copy.wait()
        grad = lax.dot_general(
            rot, held[rows, :], (((1,), (1,)), ((), ())), preferred_element_type=jnp.float32
        ).astype(jnp.bfloat16)
        mine_ref[:, rows] = grad[:tokens]
        sent_ref[:, rows] = grad[tokens:]


def grads(rot, other, weight):
    tokens, cols = rot.shape
    width = weight.shape[0]
    part = jax.ShapeDtypeStruct((tokens, width), jnp.bfloat16)
    return pl.pallas_call(
        grads_kernel,
        out_shape=(part, part),
        in_specs=[VMEM_SPEC] * 2 + [ANY_SPEC],
        out_specs=(VMEM_SPEC, VMEM_SPEC),
        scratch_shapes=[
            pltpu.VMEM(weight.shape, weight.dtype),
            pltpu.SemaphoreType.DMA((width // CHUNK,)),
        ],
        cost_estimate=pl.CostEstimate(
            flops=4 * width * cols * tokens, bytes_accessed=weight.size * 2, transcendentals=0
        ),
        compiler_params=PARAMS,
        name="grads",
    )(rot, other, weight)


def merge_kernel(rows, plane_ref, mine_ref, other_ref, grad_ref):
    plane = plane_ref[0]
    for unit in range(mine_ref.shape[1] // rows):
        block = pl.ds(unit * rows, rows)
        grad_ref[:, columns_of(plane, unit, rows)] = mine_ref[:, block]
        grad_ref[:, columns_of(1 - plane, unit, rows)] = other_ref[:, block]


def merge(plane, mine, other, rows):
    tokens, width = mine.shape
    return pl.pallas_call(
        functools.partial(merge_kernel, rows),
        out_shape=jax.ShapeDtypeStruct((tokens, 2 * width), mine.dtype),
        in_specs=[SMEM_SPEC, VMEM_SPEC, VMEM_SPEC],
        out_specs=VMEM_SPEC,
        cost_estimate=pl.CostEstimate(
            flops=0, bytes_accessed=8 * mine.size, transcendentals=0
        ),
        compiler_params=PARAMS,
        name="merge",
    )(plane, mine, other)


def per_device(activations, key_cotangent, doc_lengths, weight_codes, zero_points, step_sizes):
    tokens = activations.shape[0]
    groups, cols = step_sizes.shape
    rows = weight_codes.shape[0] // 2
    devices, copies = lax.axis_size("tensor"), lax.axis_size("dp")
    plane = (lax.axis_index("dp") // SPLIT_Y) % 2
    plane_at = plane.astype(jnp.int32).reshape(1)

    def plane_half(value):
        count = value.shape[0] // 2
        return lax.dynamic_slice_in_dim(value, plane * count, count, axis=0)

    weight = dequant(plane_half(weight_codes), plane_half(zero_points), plane_half(step_sizes))
    weight = lax.all_gather(weight, "tensor", axis=0, tiled=True)

    indices = lax.axis_index("tensor") * tokens + jnp.arange(tokens, dtype=jnp.int32)
    rot = rope_back(key_cotangent, token_positions(doc_lengths[0], indices))
    feats, to_other = pack(plane_at, activations, rot, rows)
    other = swap(to_other)

    sums = group_sums(feats, rot, other, weight, rows)
    shares = lax.all_to_all(sums, "tensor", split_axis=0, concat_axis=0, tiled=True)
    mine, sent = grads(rot, other, weight)
    got = swap(sent)
    share = jnp.sum(shares.astype(jnp.float32), axis=0).astype(jnp.bfloat16)
    totals = lax.all_to_all(
        jnp.broadcast_to(share[None], (copies, *share.shape)),
        "dp",
        split_axis=0,
        concat_axis=0,
        tiled=True,
    )
    totals = totals.astype(jnp.float32).reshape(-1, 2, SPLIT_Y, groups // 2, cols)
    total = jnp.sum(totals, axis=(0, 2)).reshape(groups, cols)
    step_grad = total / (tokens * devices * step_sizes)
    return (merge(plane_at, mine, got, rows), step_grad)


def solution(mesh):
    in_specs = (
        P(("dp", "tensor"), None),
        P(("dp", "tensor"), None),
        P("dp", None),
        P("tensor", None),
        P("tensor", None),
        P("tensor", None),
    )
    out_specs = (P(("dp", "tensor"), None), P("tensor", None))
    return jax.shard_map(
        per_device, mesh=mesh, in_specs=in_specs, out_specs=out_specs, check_vma=False
    )
```

```python
import functools
import math

import jax
import jax.numpy as jnp
from jax import lax
from jax.experimental import pallas as pl
from jax.experimental.pallas import tpu as pltpu
from jax.sharding import PartitionSpec as P

HEAD = 128
GROUP = 64
AXES = ("dp", "tensor")
NX, NY, NYL, NZ = 4, 8, 4, 8
VMEM = 12 * 1024 * 1024


def device_at(x, y, z, core):
    x, y, z = x % NX, y % NY, z % NZ
    dp = z * (NY // NYL) + y // NYL
    return dp * (NX * NYL * 2) + ((y % NYL) * NX + x) * 2 + core


def permutation(target):
    return [
        (device_at(x, y, z, core), device_at(*target(x, y, z, core)))
        for x in range(NX)
        for y in range(NY)
        for z in range(NZ)
        for core in range(2)
    ]


def send(value, dx, dy, cross=False):
    def target(x, y, z, core):
        sign = 1 if (core == 0) != cross else -1
        return x + sign * dx, y + sign * dy, z, core ^ int(cross)

    return lax.ppermute(value, AXES, permutation(target))


def swap(value):
    return lax.ppermute(value, AXES, permutation(lambda x, y, z, core: (x, y, z, core ^ 1)))


def token_positions(lengths, indices):
    count = lengths.shape[0]
    order = jnp.arange(count, dtype=jnp.int32)
    ends = jnp.sum(jnp.where(order[:, None] <= order[None, :], lengths[:, None], 0), axis=0)
    starts = jnp.where(ends[None, :] <= indices[:, None], ends[None, :], 0)
    return indices - jnp.max(starts, axis=1)


def rope_back(cotangent, positions):
    count = cotangent.shape[0]
    split = cotangent.astype(jnp.float32).reshape(count, -1, HEAD)
    middle = HEAD // 2
    freqs = jnp.exp(jnp.arange(middle, dtype=jnp.float32) * (-2.0 * math.log(10000.0) / HEAD))
    angles = positions.astype(jnp.float32)[:, None] * freqs[None, :]
    cosine = jnp.cos(angles)[:, None, :]
    sine = jnp.sin(angles)[:, None, :]
    first = split[..., :middle]
    second = split[..., middle:]
    lower = first * cosine + second * sine
    upper = second * cosine - first * sine
    return jnp.concatenate([lower, upper], axis=-1).reshape(count, -1).astype(jnp.bfloat16)


def dequant(codes, zeros, steps):
    groups, cols = zeros.shape
    levels = (codes.reshape(groups, GROUP, cols) - zeros[:, None, :]).astype(jnp.float32)
    return (steps[:, None, :] * levels).astype(jnp.bfloat16).reshape(codes.shape)


def columns_of(table, unit, rows):
    return pl.ds(pl.multiple_of(table[unit] * rows, rows), rows)


def load(weights, held, sems):
    copies, at = [], 0
    for unit, ref in enumerate(weights):
        rows = pl.ds(at, ref.shape[0])
        copies.append(pltpu.make_async_copy(ref, held.at[rows], sems.at[unit]))
        at += ref.shape[0]
    for copy in copies:
        copy.start()
    for copy in copies:
        copy.wait()


def group_sums(feats, weight, rot):
    weight_grad = lax.dot_general(
        feats, rot, (((0,), (0,)), ((), ())), preferred_element_type=jnp.float32
    )
    product = weight_grad * weight.astype(jnp.float32)
    rows, cols = weight.shape
    return product.reshape(rows // GROUP, GROUP, cols).sum(axis=1)


def put_grads(table, first, rows, held, rot, own, sent_ref, grad_ref, sems):
    tokens, width = own.shape
    copies = []
    for unit in range(width // rows):
        block = pl.ds(unit * rows, rows)
        grad = lax.dot_general(
            rot, held[block, :], (((1,), (1,)), ((), ())), preferred_element_type=jnp.float32
        ).astype(jnp.bfloat16)
        own[:, block] = grad[:tokens]
        sent_ref[:, block] = grad[tokens:]
        columns = columns_of(table, first + unit, rows)
        copies.append(
            pltpu.make_async_copy(own.at[:, block], grad_ref.at[:, columns], sems.at[unit])
        )
    for copy in copies:
        copy.start()
    return copies


def pack_kernel(rows, table, theirs, feats_ref, mine_ref, sent_ref):
    for unit in range(mine_ref.shape[1] // rows):
        block = pl.ds(unit * rows, rows)
        mine_ref[:, block] = feats_ref[:, columns_of(table, unit, rows)]
        sent_ref[:, block] = feats_ref[:, columns_of(theirs, unit, rows)]


def near_kernel(rows, count, table, rot_ref, mine_ref, other_ref, *refs):
    weights, refs = refs[:count], refs[count:]
    grad_ref, sent_ref, sums_ref, held, own, held_sems, own_sems = refs
    load(weights, held, held_sems)
    rot = rot_ref[...]
    copies = put_grads(table, 0, rows, held, rot, own, sent_ref, grad_ref, own_sems)
    for unit in range(sums_ref.shape[0]):
        block = pl.ds(unit * rows, rows)
        feats = jnp.concatenate([mine_ref[:, block], other_ref[:, block]], axis=0)
        sums_ref[unit] = group_sums(feats, held[block, :], rot)
    for copy in copies:
        copy.wait()


def far_sums_kernel(rows, count, near, table, rot_ref, near_ref, mine_ref, other_ref, *refs):
    weights, (all_ref, held, held_sems) = refs[:count], refs[count:]
    load(weights, held, held_sems)
    rot = rot_ref[...]
    sums = [near_ref[unit] for unit in range(near)]
    for unit in range(held.shape[0] // rows):
        block = pl.ds((near + unit) * rows, rows)
        feats = jnp.concatenate([mine_ref[:, block], other_ref[:, block]], axis=0)
        sums.append(group_sums(feats, held[pl.ds(unit * rows, rows), :], rot))
    all_ref[...] = jnp.zeros_like(all_ref)
    for unit, of_unit in enumerate(sums):
        all_ref[table[unit]] = of_unit.astype(all_ref.dtype)


def far_grad_kernel(rows, count, near, table, rot_ref, *refs):
    weights, refs = refs[:count], refs[count:]
    _, grad_ref, sent_ref, held, own, held_sems, own_sems = refs
    load(weights, held, held_sems)
    copies = put_grads(table, near, rows, held, rot_ref[...], own, sent_ref, grad_ref, own_sems)
    for copy in copies:
        copy.wait()


SMEM_SPEC = pl.BlockSpec(memory_space=pltpu.SMEM)
VMEM_SPEC = pl.BlockSpec(memory_space=pltpu.VMEM)
ANY_SPEC = pl.BlockSpec(memory_space=pl.ANY)


def cost(units, rows, cols, tokens, dots):
    return pl.CostEstimate(
        flops=4 * dots * units * rows * cols * tokens,
        bytes_accessed=units * rows * (cols * 2 + tokens * 4),
        transcendentals=0,
    )


def scratch(units, rows, cols, tokens, own):
    buffers = [pltpu.VMEM((units * rows, cols), jnp.bfloat16)]
    buffers += [pltpu.VMEM((tokens, units * rows), jnp.bfloat16)] * own
    return buffers + [pltpu.SemaphoreType.DMA((units,))] * (1 + own)


def pack(table, theirs, feats, rows):
    packed = jax.ShapeDtypeStruct((feats.shape[0], table.shape[0] * rows), feats.dtype)
    return pl.pallas_call(
        functools.partial(pack_kernel, rows),
        out_shape=(packed, packed),
        in_specs=[SMEM_SPEC, SMEM_SPEC, VMEM_SPEC],
        out_specs=(VMEM_SPEC, VMEM_SPEC),
        cost_estimate=pl.CostEstimate(
            flops=0, bytes_accessed=3 * feats.size * 2, transcendentals=0
        ),
        compiler_params=pltpu.CompilerParams(vmem_limit_bytes=VMEM),
        name="pack",
    )(table, theirs, feats)


def near_shards(table, mine, other, rot, weights, rows, width):
    tokens = mine.shape[0]
    cols = rot.shape[1]
    total = sum(weight.shape[0] for weight in weights) // rows
    return pl.pallas_call(
        functools.partial(near_kernel, rows, len(weights)),
        out_shape=(
            jax.ShapeDtypeStruct((tokens, width), jnp.bfloat16),
            jax.ShapeDtypeStruct((tokens, total * rows), jnp.bfloat16),
            jax.ShapeDtypeStruct((total, rows // GROUP, cols), jnp.float32),
        ),
        in_specs=[SMEM_SPEC] + [VMEM_SPEC] * 3 + [ANY_SPEC] * len(weights),
        out_specs=(ANY_SPEC, VMEM_SPEC, VMEM_SPEC),
        scratch_shapes=scratch(total, rows, cols, tokens, 1),
        cost_estimate=cost(total, rows, cols, tokens, 2),
        compiler_params=pltpu.CompilerParams(vmem_limit_bytes=VMEM),
        name="near_shards",
    )(table, rot, mine, other, *weights)


def far_sums(table, mine, other, rot, weights, near_sums, rows, devices):
    tokens = mine.shape[0]
    near, groups, cols = near_sums.shape
    total = sum(weight.shape[0] for weight in weights) // rows
    return pl.pallas_call(
        functools.partial(far_sums_kernel, rows, len(weights), near),
        out_shape=jax.ShapeDtypeStruct((devices, groups, cols), jnp.bfloat16),
        in_specs=[SMEM_SPEC] + [VMEM_SPEC] * 4 + [ANY_SPEC] * len(weights),
        out_specs=VMEM_SPEC,
        scratch_shapes=scratch(total, rows, cols, tokens, 0),
        cost_estimate=cost(total, rows, cols, tokens, 1),
        compiler_params=pltpu.CompilerParams(vmem_limit_bytes=VMEM),
        name="far_sums",
    )(table, rot, near_sums, mine, other, *weights)


def far_grad(table, rot, weights, grad, rows, near):
    tokens = grad.shape[0]
    cols = rot.shape[1]
    total = sum(weight.shape[0] for weight in weights) // rows
    return pl.pallas_call(
        functools.partial(far_grad_kernel, rows, len(weights), near),
        out_shape=(
            jax.ShapeDtypeStruct(grad.shape, grad.dtype),
            jax.ShapeDtypeStruct((tokens, total * rows), jnp.bfloat16),
        ),
        in_specs=[SMEM_SPEC, VMEM_SPEC] + [ANY_SPEC] * (len(weights) + 1),
        out_specs=(ANY_SPEC, VMEM_SPEC),
        scratch_shapes=scratch(total, rows, cols, tokens, 1),
        input_output_aliases={2 + len(weights): 0},
        cost_estimate=cost(total, rows, cols, tokens, 1),
        compiler_params=pltpu.CompilerParams(vmem_limit_bytes=VMEM),
        name="far_grad",
    )(table, rot, *weights, grad)


def place_kernel(count, first, table, blocks_ref, grad_in, grad_ref, sems):
    rows = blocks_ref.shape[1] // count
    copies = [
        pltpu.make_async_copy(
            blocks_ref.at[:, pl.ds(unit * rows, rows)],
            grad_ref.at[:, columns_of(table, first + unit, rows)],
            sems.at[unit],
        )
        for unit in range(count)
    ]
    for copy in copies:
        copy.start()
    for copy in copies:
        copy.wait()


def place(table, blocks, grad, rows, first):
    count = blocks.shape[1] // rows
    return pl.pallas_call(
        functools.partial(place_kernel, count, first),
        out_shape=jax.ShapeDtypeStruct(grad.shape, grad.dtype),
        in_specs=[SMEM_SPEC, VMEM_SPEC, ANY_SPEC],
        out_specs=ANY_SPEC,
        scratch_shapes=[pltpu.SemaphoreType.DMA((count,))],
        input_output_aliases={2: 0},
        cost_estimate=pl.CostEstimate(
            flops=0, bytes_accessed=2 * blocks.size * 2, transcendentals=0
        ),
        compiler_params=pltpu.CompilerParams(vmem_limit_bytes=VMEM),
        name="place",
    )(table, blocks, grad)


def unit_table(x, y, core):
    sign = 2 * core - 1

    def owner(dx, dy, half):
        return (((y + sign * dy) % NYL) * NX + (x + sign * dx) % NX) * 2 + half

    return (
        [owner(0, 0, core)]
        + [owner(1, 0, 0), owner(1, 0, 1)]
        + [owner(0, 1, 0), owner(0, 1, 1)]
        + [owner(1, 1, 0), owner(1, 1, 1)]
        + [owner(-1, 1, 0), owner(-1, 1, 1)]
        + [owner(2, 0, core), owner(0, 2, core)]
        + [owner(2, 1, 0), owner(2, 1, 1)]
        + [owner(-1, 2, 0), owner(-1, 2, 1)]
        + [owner(2, 2, core)]
    )


def per_device(activations, key_cotangent, doc_lengths, weight_codes, zero_points, step_sizes):
    tokens = activations.shape[0]
    rows = weight_codes.shape[0]
    place_in = lax.axis_index("tensor")
    devices = NX * NYL * 2
    core = place_in % 2
    x = (place_in // 2) % NX
    y = place_in // (2 * NX)
    table = jnp.stack(unit_table(x, y, core)).astype(jnp.int32)
    theirs = jnp.stack(unit_table(x, y, 1 - core)).astype(jnp.int32)

    weight = dequant(weight_codes, zero_points, step_sizes)
    pairs = [[2 * chip, 2 * chip + 1] for chip in range(NX * NYL)]
    chip_weight = lax.all_gather(weight, "tensor", axis=0, tiled=True, axis_index_groups=pairs)

    from_x = send(chip_weight, 1, 0)
    from_y = send(chip_weight, 0, 1)

    indices = place_in * tokens + jnp.arange(tokens, dtype=jnp.int32)
    mine = rope_back(key_cotangent, token_positions(doc_lengths[0], indices))
    rot = jnp.concatenate([mine, swap(mine)], axis=0)
    mine_feats, their_feats = pack(table, theirs, activations, rows)
    feats = (mine_feats, swap(their_feats))
    from_x, from_y, rot, _ = lax.optimization_barrier((from_x, from_y, rot, their_feats))

    def my_half(value):
        return lax.dynamic_slice_in_dim(value, core * rows, rows, axis=0)

    from_xy = send(from_y, 1, 0)
    from_yx = send(from_x, 0, 1, cross=True)
    half_x, half_y = my_half(from_x), my_half(from_y)
    from_xy, _, _ = lax.optimization_barrier((from_xy, half_x, half_y))

    far_x = send(from_xy, 1, 0)
    far_y = send(from_yx, 0, 1)
    half_xy = my_half(from_xy)
    far = send(half_xy, 1, 1)
    half_x, half_y, _ = lax.optimization_barrier((half_x, half_y, half_xy))
    far_xx = send(half_x, 1, 0)
    far_yy = send(half_y, 0, 1)

    near = [weight, from_x, from_y, from_xy, from_yx]
    grad, sent_near, sums_near = near_shards(table, *feats, rot, near, rows, activations.shape[1])
    fars = [far_xx, far_yy, far_x, far_y, far]
    at_hand = sums_near.shape[0]
    sums = far_sums(table, *feats, rot, fars, sums_near, rows, devices)
    shares = lax.all_to_all(sums, "tensor", split_axis=0, concat_axis=0, tiled=True)

    grad, sent_far = far_grad(table, rot, fars, grad, rows, at_hand)
    sent_near, _ = lax.optimization_barrier((sent_near, sums))
    got_near = swap(sent_near)
    shares, sent_far = lax.optimization_barrier((shares, sent_far))
    share = jnp.sum(shares.astype(jnp.float32), axis=0).astype(jnp.bfloat16)
    copies = lax.axis_size("dp")
    totals = lax.all_to_all(
        jnp.broadcast_to(share[None], (copies, *share.shape)),
        "dp",
        split_axis=0,
        concat_axis=0,
        tiled=True,
    )
    grad = place(theirs, got_near, grad, rows, 0)
    grad = place(theirs, swap(sent_far), grad, rows, at_hand)
    totals, grad = lax.optimization_barrier((totals, grad))
    seq_tokens = tokens * devices
    total = jnp.sum(totals.astype(jnp.float32), axis=0)
    step_grad = total / (seq_tokens * step_sizes)
    return (grad, step_grad)


def solution(mesh):
    in_specs = (
        P(("dp", "tensor"), None),
        P(("dp", "tensor"), None),
        P("dp", None),
        P("tensor", None),
        P("tensor", None),
        P("tensor", None),
    )
    out_specs = (P(("dp", "tensor"), None), P("tensor", None))
    return jax.shard_map(
        per_device, mesh=mesh, in_specs=in_specs, out_specs=out_specs, check_vma=False
    )
```

```python
import functools
import math

import jax
import jax.numpy as jnp
from jax import lax
from jax.experimental import pallas as pl
from jax.experimental.pallas import tpu as pltpu
from jax.sharding import PartitionSpec as P

HEAD = 128
GROUP = 64
AXES = ("dp", "tensor")
NX, NY, NYL, NZ = 4, 8, 4, 8
VMEM = 12 * 1024 * 1024


def device_at(x, y, z, core):
    x, y, z = x % NX, y % NY, z % NZ
    dp = z * (NY // NYL) + y // NYL
    return dp * (NX * NYL * 2) + ((y % NYL) * NX + x) * 2 + core


def permutation(target):
    return [
        (device_at(x, y, z, core), device_at(*target(x, y, z, core)))
        for x in range(NX)
        for y in range(NY)
        for z in range(NZ)
        for core in range(2)
    ]


def send(value, dx, dy, cross=False):
    def target(x, y, z, core):
        sign = 1 if (core == 0) != cross else -1
        return x + sign * dx, y + sign * dy, z, core ^ int(cross)

    return lax.ppermute(value, AXES, permutation(target))


def swap(value):
    return lax.ppermute(value, AXES, permutation(lambda x, y, z, core: (x, y, z, core ^ 1)))


def token_positions(lengths, indices):
    count = lengths.shape[0]
    order = jnp.arange(count, dtype=jnp.int32)
    ends = jnp.sum(jnp.where(order[:, None] <= order[None, :], lengths[:, None], 0), axis=0)
    starts = jnp.where(ends[None, :] <= indices[:, None], ends[None, :], 0)
    return indices - jnp.max(starts, axis=1)


def rotation(positions):
    middle = HEAD // 2
    freqs = jnp.exp(jnp.arange(middle, dtype=jnp.float32) * (-2.0 * math.log(10000.0) / HEAD))
    angles = positions.astype(jnp.float32)[:, None] * freqs[None, :]
    cosine, sine = jnp.cos(angles), jnp.sin(angles)
    even = jnp.concatenate([cosine, cosine], axis=1)
    return even, jnp.concatenate([sine, -sine], axis=1)


def dequant(codes, zeros, steps):
    groups, cols = zeros.shape
    levels = (codes.reshape(groups, GROUP, cols) - zeros[:, None, :]).astype(jnp.float32)
    return (steps[:, None, :] * levels).astype(jnp.bfloat16).reshape(codes.shape)


def columns_of(table, unit, rows):
    return pl.ds(pl.multiple_of(table[unit] * rows, rows), rows)


def load(weights, held, sems):
    copies, at = [], 0
    for unit, ref in enumerate(weights):
        rows = pl.ds(at, ref.shape[0])
        copies.append(pltpu.make_async_copy(ref, held.at[rows], sems.at[unit]))
        at += ref.shape[0]
    for copy in copies:
        copy.start()
    for copy in copies:
        copy.wait()


def group_sums(feats, weight, rot):
    weight_grad = lax.dot_general(
        feats, rot, (((0,), (0,)), ((), ())), preferred_element_type=jnp.float32
    )
    product = weight_grad * weight.astype(jnp.float32)
    rows, cols = weight.shape
    return product.reshape(rows // GROUP, GROUP, cols).sum(axis=1)


def put_grads(table, first, rows, held, rot, own, sent_ref, grad_ref, sems):
    tokens, width = own.shape
    copies = []
    for unit in range(width // rows):
        block = pl.ds(unit * rows, rows)
        grad = lax.dot_general(
            rot, held[block, :], (((1,), (1,)), ((), ())), preferred_element_type=jnp.float32
        ).astype(jnp.bfloat16)
        own[:, block] = grad[:tokens]
        sent_ref[:, block] = grad[tokens:]
        columns = columns_of(table, first + unit, rows)
        copies.append(
            pltpu.make_async_copy(own.at[:, block], grad_ref.at[:, columns], sems.at[unit])
        )
    for copy in copies:
        copy.start()
    return copies


def pack_kernel(rows, table, theirs, even_ref, odd_ref, cot_ref, feats_ref, *outs):
    rot_ref, mine_ref, sent_ref = outs
    width = mine_ref.shape[1]
    even, odd = even_ref[...], odd_ref[...]
    for at in range(0, cot_ref.shape[1], HEAD):
        head = cot_ref[:, at : at + HEAD].astype(jnp.float32)
        turned = head * even + pltpu.roll(head, HEAD // 2, 1) * odd
        rot_ref[:, at : at + HEAD] = turned.astype(rot_ref.dtype)
        sent_ref[:, width + at : width + at + HEAD] = turned.astype(rot_ref.dtype)
    for unit in range(width // rows):
        block = pl.ds(unit * rows, rows)
        mine_ref[:, block] = feats_ref[:, columns_of(table, unit, rows)]
        sent_ref[:, block] = feats_ref[:, columns_of(theirs, unit, rows)]


def near_kernel(rows, count, table, rot_ref, mine_ref, other_ref, *refs):
    weights, refs = refs[:count], refs[count:]
    grad_ref, sent_ref, sums_ref, *both, held, own, held_sems, own_sems = refs
    load(weights, held, held_sems)
    rot = jnp.concatenate([rot_ref[...], other_ref[:, mine_ref.shape[1] :]], axis=0)
    for ref in both:
        ref[...] = rot
    copies = put_grads(table, 0, rows, held, rot, own, sent_ref, grad_ref, own_sems)
    for unit in range(sums_ref.shape[0]):
        block = pl.ds(unit * rows, rows)
        feats = jnp.concatenate([mine_ref[:, block], other_ref[:, block]], axis=0)
        sums_ref[unit] = group_sums(feats, held[block, :], rot)
    for copy in copies:
        copy.wait()


def far_sums_kernel(rows, count, near, table, rot_ref, near_ref, mine_ref, other_ref, *refs):
    weights, (all_ref, held, held_sems) = refs[:count], refs[count:]
    load(weights, held, held_sems)
    rot = rot_ref[...]
    sums = [near_ref[unit] for unit in range(near)]
    for unit in range(held.shape[0] // rows):
        block = pl.ds((near + unit) * rows, rows)
        feats = jnp.concatenate([mine_ref[:, block], other_ref[:, block]], axis=0)
        sums.append(group_sums(feats, held[pl.ds(unit * rows, rows), :], rot))
    all_ref[...] = jnp.zeros_like(all_ref)
    for unit, of_unit in enumerate(sums):
        all_ref[table[unit]] = of_unit.astype(all_ref.dtype)


def far_grad_kernel(rows, count, near, table, rot_ref, *refs):
    weights, refs = refs[:count], refs[count:]
    _, grad_ref, sent_ref, held, own, held_sems, own_sems = refs
    load(weights, held, held_sems)
    copies = put_grads(table, near, rows, held, rot_ref[...], own, sent_ref, grad_ref, own_sems)
    for copy in copies:
        copy.wait()


SMEM_SPEC = pl.BlockSpec(memory_space=pltpu.SMEM)
VMEM_SPEC = pl.BlockSpec(memory_space=pltpu.VMEM)
ANY_SPEC = pl.BlockSpec(memory_space=pl.ANY)


def cost(units, rows, cols, tokens, dots):
    return pl.CostEstimate(
        flops=4 * dots * units * rows * cols * tokens,
        bytes_accessed=units * rows * (cols * 2 + tokens * 4),
        transcendentals=0,
    )


def scratch(units, rows, cols, tokens, own):
    buffers = [pltpu.VMEM((units * rows, cols), jnp.bfloat16)]
    buffers += [pltpu.VMEM((tokens, units * rows), jnp.bfloat16)] * own
    return buffers + [pltpu.SemaphoreType.DMA((units,))] * (1 + own)


def pack(table, theirs, turn, cotangent, feats, rows):
    tokens, cols = cotangent.shape
    width = table.shape[0] * rows
    return pl.pallas_call(
        functools.partial(pack_kernel, rows),
        out_shape=tuple(
            jax.ShapeDtypeStruct((tokens, size), feats.dtype)
            for size in (cols, width, width + cols)
        ),
        in_specs=[SMEM_SPEC, SMEM_SPEC] + [VMEM_SPEC] * 4,
        out_specs=(VMEM_SPEC,) * 3,
        cost_estimate=pl.CostEstimate(
            flops=0, bytes_accessed=3 * feats.size * 2, transcendentals=0
        ),
        compiler_params=pltpu.CompilerParams(vmem_limit_bytes=VMEM),
        name="pack",
    )(table, theirs, *turn, cotangent, feats)


def near_shards(table, mine, other, rot, weights, rows, width):
    tokens = mine.shape[0]
    cols = rot.shape[1]
    total = sum(weight.shape[0] for weight in weights) // rows
    return pl.pallas_call(
        functools.partial(near_kernel, rows, len(weights)),
        out_shape=(
            jax.ShapeDtypeStruct((tokens, width), jnp.bfloat16),
            jax.ShapeDtypeStruct((tokens, total * rows), jnp.bfloat16),
            jax.ShapeDtypeStruct((total, rows // GROUP, cols), jnp.float32),
        )
        + (jax.ShapeDtypeStruct((2 * tokens, cols), jnp.bfloat16),) * 2,
        in_specs=[SMEM_SPEC] + [VMEM_SPEC] * 3 + [ANY_SPEC] * len(weights),
        out_specs=(ANY_SPEC,) + (VMEM_SPEC,) * 4,
        scratch_shapes=scratch(total, rows, cols, tokens, 1),
        cost_estimate=cost(total, rows, cols, tokens, 2),
        compiler_params=pltpu.CompilerParams(vmem_limit_bytes=VMEM),
        name="near_shards",
    )(table, rot, mine, other, *weights)


def far_sums(table, mine, other, rot, weights, near_sums, rows, devices):
    tokens = mine.shape[0]
    near, groups, cols = near_sums.shape
    total = sum(weight.shape[0] for weight in weights) // rows
    return pl.pallas_call(
        functools.partial(far_sums_kernel, rows, len(weights), near),
        out_shape=jax.ShapeDtypeStruct((devices, groups, cols), jnp.bfloat16),
        in_specs=[SMEM_SPEC] + [VMEM_SPEC] * 4 + [ANY_SPEC] * len(weights),
        out_specs=VMEM_SPEC,
        scratch_shapes=scratch(total, rows, cols, tokens, 0),
        cost_estimate=cost(total, rows, cols, tokens, 1),
        compiler_params=pltpu.CompilerParams(vmem_limit_bytes=VMEM),
        name="far_sums",
    )(table, rot, near_sums, mine, other, *weights)


def far_grad(table, rot, weights, grad, rows, near):
    tokens = grad.shape[0]
    cols = rot.shape[1]
    total = sum(weight.shape[0] for weight in weights) // rows
    return pl.pallas_call(
        functools.partial(far_grad_kernel, rows, len(weights), near),
        out_shape=(
            jax.ShapeDtypeStruct(grad.shape, grad.dtype),
            jax.ShapeDtypeStruct((tokens, total * rows), jnp.bfloat16),
        ),
        in_specs=[SMEM_SPEC, VMEM_SPEC] + [ANY_SPEC] * (len(weights) + 1),
        out_specs=(ANY_SPEC, VMEM_SPEC),
        scratch_shapes=scratch(total, rows, cols, tokens, 1),
        input_output_aliases={2 + len(weights): 0},
        cost_estimate=cost(total, rows, cols, tokens, 1),
        compiler_params=pltpu.CompilerParams(vmem_limit_bytes=VMEM),
        name="far_grad",
    )(table, rot, *weights, grad)


def place_kernel(count, first, table, blocks_ref, grad_in, grad_ref, sems):
    rows = blocks_ref.shape[1] // count
    copies = [
        pltpu.make_async_copy(
            blocks_ref.at[:, pl.ds(unit * rows, rows)],
            grad_ref.at[:, columns_of(table, first + unit, rows)],
            sems.at[unit],
        )
        for unit in range(count)
    ]
    for copy in copies:
        copy.start()
    for copy in copies:
        copy.wait()


def place(table, blocks, grad, rows, first):
    count = blocks.shape[1] // rows
    return pl.pallas_call(
        functools.partial(place_kernel, count, first),
        out_shape=jax.ShapeDtypeStruct(grad.shape, grad.dtype),
        in_specs=[SMEM_SPEC, VMEM_SPEC, ANY_SPEC],
        out_specs=ANY_SPEC,
        scratch_shapes=[pltpu.SemaphoreType.DMA((count,))],
        input_output_aliases={2: 0},
        cost_estimate=pl.CostEstimate(
            flops=0, bytes_accessed=2 * blocks.size * 2, transcendentals=0
        ),
        compiler_params=pltpu.CompilerParams(vmem_limit_bytes=VMEM),
        name="place",
    )(table, blocks, grad)


def unit_table(x, y, core):
    sign = 2 * core - 1

    def owner(dx, dy, half):
        return (((y + sign * dy) % NYL) * NX + (x + sign * dx) % NX) * 2 + half

    return (
        [owner(0, 0, core)]
        + [owner(1, 0, 0), owner(1, 0, 1)]
        + [owner(0, 1, 0), owner(0, 1, 1)]
        + [owner(1, 1, 0), owner(1, 1, 1)]
        + [owner(-1, 1, 0), owner(-1, 1, 1)]
        + [owner(2, 0, core), owner(0, 2, core)]
        + [owner(2, 1, 0), owner(2, 1, 1)]
        + [owner(-1, 2, 0), owner(-1, 2, 1)]
        + [owner(2, 2, core)]
    )


def per_device(activations, key_cotangent, doc_lengths, weight_codes, zero_points, step_sizes):
    tokens = activations.shape[0]
    rows = weight_codes.shape[0]
    place_in = lax.axis_index("tensor")
    devices = NX * NYL * 2
    core = place_in % 2
    x = (place_in // 2) % NX
    y = place_in // (2 * NX)
    table = jnp.stack(unit_table(x, y, core)).astype(jnp.int32)
    theirs = jnp.stack(unit_table(x, y, 1 - core)).astype(jnp.int32)

    weight = dequant(weight_codes, zero_points, step_sizes)
    pairs = [[2 * chip, 2 * chip + 1] for chip in range(NX * NYL)]
    chip_weight = lax.all_gather(weight, "tensor", axis=0, tiled=True, axis_index_groups=pairs)

    from_x = send(chip_weight, 1, 0)
    from_y = send(chip_weight, 0, 1)

    indices = place_in * tokens + jnp.arange(tokens, dtype=jnp.int32)
    turn = rotation(token_positions(doc_lengths[0], indices))
    mine, mine_feats, to_other = pack(table, theirs, turn, key_cotangent, activations, rows)
    feats = (mine_feats, swap(to_other))
    from_x, from_y, _ = lax.optimization_barrier((from_x, from_y, to_other))

    def my_half(value):
        return lax.dynamic_slice_in_dim(value, core * rows, rows, axis=0)

    from_xy = send(from_y, 1, 0)
    from_yx = send(from_x, 0, 1, cross=True)
    half_x, half_y = my_half(from_x), my_half(from_y)
    from_xy, _, _ = lax.optimization_barrier((from_xy, half_x, half_y))

    far_x = send(from_xy, 1, 0)
    far_y = send(from_yx, 0, 1)
    far_xx = send(half_x, 1, 0)
    far_yy = send(half_y, 0, 1)
    half_xy, _, _ = lax.optimization_barrier((my_half(from_xy), far_xx, far_yy))
    far = send(half_xy, 1, 1)

    near = [weight, from_x, from_y, from_xy, from_yx]
    grad, sent_near, sums_near, rot, rot_again = near_shards(
        table, *feats, mine, near, rows, activations.shape[1]
    )
    fars = [far_xx, far_yy, far_x, far_y, far]
    at_hand = sums_near.shape[0]
    sums = far_sums(table, *feats, rot, fars, sums_near, rows, devices)
    shares = lax.all_to_all(sums, "tensor", split_axis=0, concat_axis=0, tiled=True)

    grad, sent_far = far_grad(table, rot_again, fars, grad, rows, at_hand)
    got_near = swap(sent_near)
    share = jnp.sum(shares.astype(jnp.float32), axis=0).astype(jnp.bfloat16)
    share = jnp.broadcast_to(share[None], (lax.axis_size("dp"), *share.shape))
    share, sent_far = lax.optimization_barrier((share, sent_far))
    totals = lax.all_to_all(share, "dp", split_axis=0, concat_axis=0, tiled=True)
    grad = place(theirs, got_near, grad, rows, 0)
    grad = place(theirs, swap(sent_far), grad, rows, at_hand)
    totals, grad = lax.optimization_barrier((totals, grad))
    seq_tokens = tokens * devices
    total = jnp.sum(totals.astype(jnp.float32), axis=0)
    step_grad = total / (seq_tokens * step_sizes)
    return (grad, step_grad)


def solution(mesh):
    in_specs = (
        P(("dp", "tensor"), None),
        P(("dp", "tensor"), None),
        P("dp", None),
        P("tensor", None),
        P("tensor", None),
        P("tensor", None),
    )
    out_specs = (P(("dp", "tensor"), None), P("tensor", None))
    return jax.shard_map(
        per_device, mesh=mesh, in_specs=in_specs, out_specs=out_specs, check_vma=False
    )
```

```python
import functools
import math

import jax
import jax.numpy as jnp
from jax import lax
from jax.experimental import pallas as pl
from jax.experimental.pallas import tpu as pltpu
from jax.sharding import PartitionSpec as P

HEAD = 128
GROUP = 64
AXES = ("dp", "tensor")
NX, NY, NYL, NZ = 4, 8, 4, 8
VMEM = 48 * 1024 * 1024


def device_at(x, y, z, core):
    x, y, z = x % NX, y % NY, z % NZ
    dp = z * (NY // NYL) + y // NYL
    return dp * (NX * NYL * 2) + ((y % NYL) * NX + x) * 2 + core


def permutation(target):
    return [
        (device_at(x, y, z, core), device_at(*target(x, y, z, core)))
        for x in range(NX)
        for y in range(NY)
        for z in range(NZ)
        for core in range(2)
    ]


def send(value, dx, dy, cross=False):
    def target(x, y, z, core):
        sign = 1 if (core == 0) != cross else -1
        return x + sign * dx, y + sign * dy, z, core ^ int(cross)

    return lax.ppermute(value, AXES, permutation(target))


def swap(value):
    return lax.ppermute(value, AXES, permutation(lambda x, y, z, core: (x, y, z, core ^ 1)))


def token_positions(lengths, indices):
    count = lengths.shape[0]
    order = jnp.arange(count, dtype=jnp.int32)
    ends = jnp.sum(jnp.where(order[:, None] <= order[None, :], lengths[:, None], 0), axis=0)
    starts = jnp.where(ends[None, :] <= indices[:, None], ends[None, :], 0)
    return indices - jnp.max(starts, axis=1)


def rotation(positions):
    middle = HEAD // 2
    freqs = jnp.exp(jnp.arange(middle, dtype=jnp.float32) * (-2.0 * math.log(10000.0) / HEAD))
    angles = positions.astype(jnp.float32)[:, None] * freqs[None, :]
    cosine, sine = jnp.cos(angles), jnp.sin(angles)
    even = jnp.concatenate([cosine, cosine], axis=1)
    return even, jnp.concatenate([sine, -sine], axis=1)


def dequant(codes, zeros, steps):
    groups, cols = zeros.shape
    levels = (codes.reshape(groups, GROUP, cols) - zeros[:, None, :]).astype(jnp.float32)
    return (steps[:, None, :] * levels).astype(jnp.bfloat16).reshape(codes.shape)


def columns_of(table, unit, rows):
    return pl.ds(pl.multiple_of(table[unit] * rows, rows), rows)


def load(weights, held, sems):
    copies, at = [], 0
    for unit, ref in enumerate(weights):
        rows = pl.ds(at, ref.shape[0])
        copies.append(pltpu.make_async_copy(ref, held.at[rows], sems.at[unit]))
        at += ref.shape[0]
    for copy in copies:
        copy.start()
    for copy in copies:
        copy.wait()


def group_sums(feats, weight, rot):
    weight_grad = lax.dot_general(
        feats, rot, (((0,), (0,)), ((), ())), preferred_element_type=jnp.float32
    )
    product = weight_grad * weight.astype(jnp.float32)
    rows, cols = weight.shape
    return product.reshape(rows // GROUP, GROUP, cols).sum(axis=1)


def put_grads(table, first, rows, held, rot, own, sent_ref, grad_ref, sems):
    tokens, width = own.shape
    copies = []
    for unit in range(width // rows):
        block = pl.ds(unit * rows, rows)
        grad = lax.dot_general(
            rot, held[block, :], (((1,), (1,)), ((), ())), preferred_element_type=jnp.float32
        ).astype(jnp.bfloat16)
        own[:, block] = grad[:tokens]
        sent_ref[:, block] = grad[tokens:]
        columns = columns_of(table, first + unit, rows)
        copies.append(
            pltpu.make_async_copy(own.at[:, block], grad_ref.at[:, columns], sems.at[unit])
        )
    for copy in copies:
        copy.start()
    return copies


def pack_kernel(rows, table, theirs, even_ref, odd_ref, cot_ref, feats_ref, *outs):
    rot_ref, mine_ref, sent_ref = outs
    width = mine_ref.shape[1]
    even, odd = even_ref[...], odd_ref[...]
    for at in range(0, cot_ref.shape[1], HEAD):
        head = cot_ref[:, at : at + HEAD].astype(jnp.float32)
        turned = head * even + pltpu.roll(head, HEAD // 2, 1) * odd
        rot_ref[:, at : at + HEAD] = turned.astype(rot_ref.dtype)
        sent_ref[:, width + at : width + at + HEAD] = turned.astype(rot_ref.dtype)
    for unit in range(width // rows):
        block = pl.ds(unit * rows, rows)
        mine_ref[:, block] = feats_ref[:, columns_of(table, unit, rows)]
        sent_ref[:, block] = feats_ref[:, columns_of(theirs, unit, rows)]


def near_kernel(rows, count, table, rot_ref, mine_ref, other_ref, *refs):
    weights, refs = refs[:count], refs[count:]
    grad_ref, sent_ref, sums_ref, *both, held, own, held_sems, own_sems = refs
    load(weights, held, held_sems)
    rot = jnp.concatenate([rot_ref[...], other_ref[:, mine_ref.shape[1] :]], axis=0)
    for ref in both:
        ref[...] = rot
    copies = put_grads(table, 0, rows, held, rot, own, sent_ref, grad_ref, own_sems)
    for unit in range(sums_ref.shape[0]):
        block = pl.ds(unit * rows, rows)
        feats = jnp.concatenate([mine_ref[:, block], other_ref[:, block]], axis=0)
        sums_ref[unit] = group_sums(feats, held[block, :], rot)
    for copy in copies:
        copy.wait()


def far_sums_kernel(rows, count, near, table, rot_ref, near_ref, mine_ref, other_ref, *refs):
    weights, (all_ref, held, held_sems) = refs[:count], refs[count:]
    load(weights, held, held_sems)
    rot = rot_ref[...]
    sums = [near_ref[unit] for unit in range(near)]
    for unit in range(held.shape[0] // rows):
        block = pl.ds((near + unit) * rows, rows)
        feats = jnp.concatenate([mine_ref[:, block], other_ref[:, block]], axis=0)
        sums.append(group_sums(feats, held[pl.ds(unit * rows, rows), :], rot))
    all_ref[...] = jnp.zeros_like(all_ref)
    for unit, of_unit in enumerate(sums):
        all_ref[table[unit]] = of_unit.astype(all_ref.dtype)


def far_grad_kernel(rows, count, near, table, rot_ref, *refs):
    weights, refs = refs[:count], refs[count:]
    _, grad_ref, sent_ref, held, own, held_sems, own_sems = refs
    load(weights, held, held_sems)
    copies = put_grads(table, near, rows, held, rot_ref[...], own, sent_ref, grad_ref, own_sems)
    for copy in copies:
        copy.wait()


SMEM_SPEC = pl.BlockSpec(memory_space=pltpu.SMEM)
VMEM_SPEC = pl.BlockSpec(memory_space=pltpu.VMEM)
ANY_SPEC = pl.BlockSpec(memory_space=pl.ANY)


def cost(units, rows, cols, tokens, dots):
    return pl.CostEstimate(
        flops=4 * dots * units * rows * cols * tokens,
        bytes_accessed=units * rows * (cols * 2 + tokens * 4),
        transcendentals=0,
    )


def scratch(units, rows, cols, tokens, own):
    buffers = [pltpu.VMEM((units * rows, cols), jnp.bfloat16)]
    buffers += [pltpu.VMEM((tokens, units * rows), jnp.bfloat16)] * own
    return buffers + [pltpu.SemaphoreType.DMA((units,))] * (1 + own)


def pack(table, theirs, turn, cotangent, feats, rows):
    tokens, cols = cotangent.shape
    width = table.shape[0] * rows
    return pl.pallas_call(
        functools.partial(pack_kernel, rows),
        out_shape=tuple(
            jax.ShapeDtypeStruct((tokens, size), feats.dtype)
            for size in (cols, width, width + cols)
        ),
        in_specs=[SMEM_SPEC, SMEM_SPEC] + [VMEM_SPEC] * 4,
        out_specs=(VMEM_SPEC,) * 3,
        cost_estimate=pl.CostEstimate(
            flops=0, bytes_accessed=3 * feats.size * 2, transcendentals=0
        ),
        compiler_params=pltpu.CompilerParams(vmem_limit_bytes=VMEM),
        name="pack",
    )(table, theirs, *turn, cotangent, feats)


def near_shards(table, mine, other, rot, weights, rows, width):
    tokens = mine.shape[0]
    cols = rot.shape[1]
    total = sum(weight.shape[0] for weight in weights) // rows
    return pl.pallas_call(
        functools.partial(near_kernel, rows, len(weights)),
        out_shape=(
            jax.ShapeDtypeStruct((tokens, width), jnp.bfloat16),
            jax.ShapeDtypeStruct((tokens, total * rows), jnp.bfloat16),
            jax.ShapeDtypeStruct((total, rows // GROUP, cols), jnp.float32),
        )
        + (jax.ShapeDtypeStruct((2 * tokens, cols), jnp.bfloat16),) * 2,
        in_specs=[SMEM_SPEC] + [VMEM_SPEC] * 3 + [ANY_SPEC] * len(weights),
        out_specs=(ANY_SPEC,) + (VMEM_SPEC,) * 4,
        scratch_shapes=scratch(total, rows, cols, tokens, 1),
        cost_estimate=cost(total, rows, cols, tokens, 2),
        compiler_params=pltpu.CompilerParams(vmem_limit_bytes=VMEM),
        name="near_shards",
    )(table, rot, mine, other, *weights)


def far_sums(table, mine, other, rot, weights, near_sums, rows, devices):
    tokens = mine.shape[0]
    near, groups, cols = near_sums.shape
    total = sum(weight.shape[0] for weight in weights) // rows
    return pl.pallas_call(
        functools.partial(far_sums_kernel, rows, len(weights), near),
        out_shape=jax.ShapeDtypeStruct((devices, groups, cols), jnp.bfloat16),
        in_specs=[SMEM_SPEC] + [VMEM_SPEC] * 4 + [ANY_SPEC] * len(weights),
        out_specs=VMEM_SPEC,
        scratch_shapes=scratch(total, rows, cols, tokens, 0),
        cost_estimate=cost(total, rows, cols, tokens, 1),
        compiler_params=pltpu.CompilerParams(vmem_limit_bytes=VMEM),
        name="far_sums",
    )(table, rot, near_sums, mine, other, *weights)


def far_grad(table, rot, weights, grad, rows, near):
    tokens = grad.shape[0]
    cols = rot.shape[1]
    total = sum(weight.shape[0] for weight in weights) // rows
    return pl.pallas_call(
        functools.partial(far_grad_kernel, rows, len(weights), near),
        out_shape=(
            jax.ShapeDtypeStruct(grad.shape, grad.dtype),
            jax.ShapeDtypeStruct((tokens, total * rows), jnp.bfloat16),
        ),
        in_specs=[SMEM_SPEC, VMEM_SPEC] + [ANY_SPEC] * (len(weights) + 1),
        out_specs=(ANY_SPEC, VMEM_SPEC),
        scratch_shapes=scratch(total, rows, cols, tokens, 1),
        input_output_aliases={2 + len(weights): 0},
        cost_estimate=cost(total, rows, cols, tokens, 1),
        compiler_params=pltpu.CompilerParams(vmem_limit_bytes=VMEM),
        name="far_grad",
    )(table, rot, *weights, grad)


def place_kernel(count, first, table, blocks_ref, grad_in, grad_ref, sems):
    rows = blocks_ref.shape[1] // count
    copies = [
        pltpu.make_async_copy(
            blocks_ref.at[:, pl.ds(unit * rows, rows)],
            grad_ref.at[:, columns_of(table, first + unit, rows)],
            sems.at[unit],
        )
        for unit in range(count)
    ]
    for copy in copies:
        copy.start()
    for copy in copies:
        copy.wait()


def place(table, blocks, grad, rows, first):
    count = blocks.shape[1] // rows
    return pl.pallas_call(
        functools.partial(place_kernel, count, first),
        out_shape=jax.ShapeDtypeStruct(grad.shape, grad.dtype),
        in_specs=[SMEM_SPEC, VMEM_SPEC, ANY_SPEC],
        out_specs=ANY_SPEC,
        scratch_shapes=[pltpu.SemaphoreType.DMA((count,))],
        input_output_aliases={2: 0},
        cost_estimate=pl.CostEstimate(
            flops=0, bytes_accessed=2 * blocks.size * 2, transcendentals=0
        ),
        compiler_params=pltpu.CompilerParams(vmem_limit_bytes=VMEM),
        name="place",
    )(table, blocks, grad)


def unit_table(x, y, core):
    sign = 2 * core - 1

    def owner(dx, dy, half):
        return (((y + sign * dy) % NYL) * NX + (x + sign * dx) % NX) * 2 + half

    return (
        [owner(0, 0, core)]
        + [owner(1, 0, 0), owner(1, 0, 1)]
        + [owner(0, 1, 0), owner(0, 1, 1)]
        + [owner(1, 1, 0), owner(1, 1, 1)]
        + [owner(-1, 1, 0), owner(-1, 1, 1)]
        + [owner(2, 0, core), owner(0, 2, core)]
        + [owner(2, 1, 0), owner(2, 1, 1)]
        + [owner(-1, 2, 0), owner(-1, 2, 1)]
        + [owner(2, 2, core)]
    )


def per_device(activations, key_cotangent, doc_lengths, weight_codes, zero_points, step_sizes):
    tokens = activations.shape[0]
    rows = weight_codes.shape[0]
    place_in = lax.axis_index("tensor")
    devices = NX * NYL * 2
    core = place_in % 2
    x = (place_in // 2) % NX
    y = place_in // (2 * NX)
    table = jnp.stack(unit_table(x, y, core)).astype(jnp.int32)
    theirs = jnp.stack(unit_table(x, y, 1 - core)).astype(jnp.int32)

    weight = dequant(weight_codes, zero_points, step_sizes)
    pairs = [[2 * chip, 2 * chip + 1] for chip in range(NX * NYL)]
    chip_weight = lax.all_gather(weight, "tensor", axis=0, tiled=True, axis_index_groups=pairs)

    from_x = send(chip_weight, 1, 0)
    from_y = send(chip_weight, 0, 1)

    indices = place_in * tokens + jnp.arange(tokens, dtype=jnp.int32)
    turn = rotation(token_positions(doc_lengths[0], indices))
    mine, mine_feats, to_other = pack(table, theirs, turn, key_cotangent, activations, rows)
    feats = (mine_feats, swap(to_other))
    from_x, from_y, _ = lax.optimization_barrier((from_x, from_y, to_other))

    def my_half(value):
        return lax.dynamic_slice_in_dim(value, core * rows, rows, axis=0)

    from_xy = send(from_y, 1, 0)
    from_yx = send(from_x, 0, 1, cross=True)
    half_x, half_y, _ = lax.optimization_barrier((my_half(from_x), my_half(from_y), feats[1]))
    from_xy, _, _ = lax.optimization_barrier((from_xy, half_x, half_y))

    far_x = send(from_xy, 1, 0)
    far_y = send(from_yx, 0, 1)
    far_xx = send(half_x, 1, 0)
    far_yy = send(half_y, 0, 1)
    half_xy, _, _ = lax.optimization_barrier((my_half(from_xy), far_xx, far_yy))
    far = send(half_xy, 1, 1)

    near = [weight, from_x, from_y, from_xy, from_yx]
    grad, sent_near, sums_near, rot, rot_again = near_shards(
        table, *feats, mine, near, rows, activations.shape[1]
    )
    fars = [far_xx, far_yy, far_x, far_y, far]
    at_hand = sums_near.shape[0]
    sums = far_sums(table, *feats, rot, fars, sums_near, rows, devices)
    shares = lax.all_to_all(sums, "tensor", split_axis=0, concat_axis=0, tiled=True)

    grad, sent_far = far_grad(table, rot_again, fars, grad, rows, at_hand)
    got_near = swap(sent_near)
    share = jnp.sum(shares.astype(jnp.float32), axis=0).astype(jnp.bfloat16)
    share = jnp.broadcast_to(share[None], (lax.axis_size("dp"), *share.shape))
    share, sent_far = lax.optimization_barrier((share, sent_far))
    totals = lax.all_to_all(share, "dp", split_axis=0, concat_axis=0, tiled=True)
    grad = place(theirs, got_near, grad, rows, 0)
    grad = place(theirs, swap(sent_far), grad, rows, at_hand)
    totals, grad = lax.optimization_barrier((totals, grad))
    seq_tokens = tokens * devices
    total = jnp.sum(totals.astype(jnp.float32), axis=0)
    step_grad = total / (seq_tokens * step_sizes)
    return (grad, step_grad)


def solution(mesh):
    in_specs = (
        P(("dp", "tensor"), None),
        P(("dp", "tensor"), None),
        P("dp", None),
        P("tensor", None),
        P("tensor", None),
        P("tensor", None),
    )
    out_specs = (P(("dp", "tensor"), None), P("tensor", None))
    return jax.shard_map(
        per_device, mesh=mesh, in_specs=in_specs, out_specs=out_specs, check_vma=False
    )
```

```python
import functools
import math

import jax
import jax.numpy as jnp
from jax import lax
from jax.experimental import pallas as pl
from jax.experimental.pallas import tpu as pltpu
from jax.sharding import PartitionSpec as P

HEAD = 128
GROUP = 64
AXES = ("dp", "tensor")
NX, NY, NYL, NZ = 4, 8, 4, 8
VMEM = 48 * 1024 * 1024


def device_at(x, y, z, core):
    x, y, z = x % NX, y % NY, z % NZ
    dp = z * (NY // NYL) + y // NYL
    return dp * (NX * NYL * 2) + ((y % NYL) * NX + x) * 2 + core


def permutation(target):
    return [
        (device_at(x, y, z, core), device_at(*target(x, y, z, core)))
        for x in range(NX)
        for y in range(NY)
        for z in range(NZ)
        for core in range(2)
    ]


def send(value, dx, dy, cross=False):
    def target(x, y, z, core):
        sign = 1 if (core == 0) != cross else -1
        return x + sign * dx, y + sign * dy, z, core ^ int(cross)

    return lax.ppermute(value, AXES, permutation(target))


def swap(value):
    return lax.ppermute(value, AXES, permutation(lambda x, y, z, core: (x, y, z, core ^ 1)))


def token_positions(lengths, indices):
    count = lengths.shape[0]
    order = jnp.arange(count, dtype=jnp.int32)
    ends = jnp.sum(jnp.where(order[:, None] <= order[None, :], lengths[:, None], 0), axis=0)
    starts = jnp.where(ends[None, :] <= indices[:, None], ends[None, :], 0)
    return indices - jnp.max(starts, axis=1)


def rotation(positions):
    middle = HEAD // 2
    freqs = jnp.exp(jnp.arange(middle, dtype=jnp.float32) * (-2.0 * math.log(10000.0) / HEAD))
    angles = positions.astype(jnp.float32)[:, None] * freqs[None, :]
    cosine, sine = jnp.cos(angles), jnp.sin(angles)
    even = jnp.concatenate([cosine, cosine], axis=1)
    return even, jnp.concatenate([sine, -sine], axis=1)


def dequant(codes, zeros, steps):
    groups, cols = zeros.shape
    levels = (codes.reshape(groups, GROUP, cols) - zeros[:, None, :]).astype(jnp.float32)
    return (steps[:, None, :] * levels).astype(jnp.bfloat16).reshape(codes.shape)


def columns_of(table, unit, rows):
    return pl.ds(pl.multiple_of(table[unit] * rows, rows), rows)


def load(weights, held, sems):
    copies, at = [], 0
    for unit, ref in enumerate(weights):
        rows = pl.ds(at, ref.shape[0])
        copies.append(pltpu.make_async_copy(ref, held.at[rows], sems.at[unit]))
        at += ref.shape[0]
    for copy in copies:
        copy.start()
    for copy in copies:
        copy.wait()


def group_sums(feats, weight, rot):
    weight_grad = lax.dot_general(
        feats, rot, (((0,), (0,)), ((), ())), preferred_element_type=jnp.float32
    )
    product = weight_grad * weight.astype(jnp.float32)
    rows, cols = weight.shape
    return product.reshape(rows // GROUP, GROUP, cols).sum(axis=1)


def put_grads(table, first, rows, held, rot, own, sent_ref, grad_ref, sems):
    tokens, width = own.shape
    copies = []
    for unit in range(width // rows):
        block = pl.ds(unit * rows, rows)
        grad = lax.dot_general(
            rot, held[block, :], (((1,), (1,)), ((), ())), preferred_element_type=jnp.float32
        ).astype(jnp.bfloat16)
        own[:, block] = grad[:tokens]
        sent_ref[:, block] = grad[tokens:]
        columns = columns_of(table, first + unit, rows)
        copies.append(
            pltpu.make_async_copy(own.at[:, block], grad_ref.at[:, columns], sems.at[unit])
        )
    for copy in copies:
        copy.start()
    return copies


def pack_kernel(rows, table, theirs, even_ref, odd_ref, cot_ref, feats_ref, *outs):
    rot_ref, mine_ref, sent_ref = outs
    width = mine_ref.shape[1]
    even, odd = even_ref[...], odd_ref[...]
    for at in range(0, cot_ref.shape[1], HEAD):
        head = cot_ref[:, at : at + HEAD].astype(jnp.float32)
        turned = head * even + pltpu.roll(head, HEAD // 2, 1) * odd
        rot_ref[:, at : at + HEAD] = turned.astype(rot_ref.dtype)
        sent_ref[:, width + at : width + at + HEAD] = turned.astype(rot_ref.dtype)
    for unit in range(width // rows):
        block = pl.ds(unit * rows, rows)
        mine_ref[:, block] = feats_ref[:, columns_of(table, unit, rows)]
        sent_ref[:, block] = feats_ref[:, columns_of(theirs, unit, rows)]


def near_kernel(rows, count, table, rot_ref, mine_ref, other_ref, *refs):
    weights, refs = refs[:count], refs[count:]
    grad_ref, sent_ref, sums_ref, *both, held, own, held_sems, own_sems = refs
    load(weights, held, held_sems)
    rot = jnp.concatenate([rot_ref[...], other_ref[:, mine_ref.shape[1] :]], axis=0)
    for ref in both:
        ref[...] = rot
    copies = put_grads(table, 0, rows, held, rot, own, sent_ref, grad_ref, own_sems)
    for unit in range(sums_ref.shape[0]):
        block = pl.ds(unit * rows, rows)
        feats = jnp.concatenate([mine_ref[:, block], other_ref[:, block]], axis=0)
        sums_ref[unit] = group_sums(feats, held[block, :], rot)
    for copy in copies:
        copy.wait()


def far_sums_kernel(rows, count, near, table, rot_ref, near_ref, mine_ref, other_ref, *refs):
    weights, (all_ref, held, held_sems) = refs[:count], refs[count:]
    load(weights, held, held_sems)
    rot = rot_ref[...]
    sums = [near_ref[unit] for unit in range(near)]
    for unit in range(held.shape[0] // rows):
        block = pl.ds((near + unit) * rows, rows)
        feats = jnp.concatenate([mine_ref[:, block], other_ref[:, block]], axis=0)
        sums.append(group_sums(feats, held[pl.ds(unit * rows, rows), :], rot))
    all_ref[...] = jnp.zeros_like(all_ref)
    for unit, of_unit in enumerate(sums):
        all_ref[table[unit]] = of_unit.astype(all_ref.dtype)


def far_grad_kernel(rows, count, near, table, rot_ref, *refs):
    weights, refs = refs[:count], refs[count:]
    _, grad_ref, sent_ref, held, own, held_sems, own_sems = refs
    load(weights, held, held_sems)
    copies = put_grads(table, near, rows, held, rot_ref[...], own, sent_ref, grad_ref, own_sems)
    for copy in copies:
        copy.wait()


SMEM_SPEC = pl.BlockSpec(memory_space=pltpu.SMEM)
VMEM_SPEC = pl.BlockSpec(memory_space=pltpu.VMEM)
ANY_SPEC = pl.BlockSpec(memory_space=pl.ANY)


def cost(units, rows, cols, tokens, dots):
    return pl.CostEstimate(
        flops=4 * dots * units * rows * cols * tokens,
        bytes_accessed=units * rows * (cols * 2 + tokens * 4),
        transcendentals=0,
    )


def scratch(units, rows, cols, tokens, own):
    buffers = [pltpu.VMEM((units * rows, cols), jnp.bfloat16)]
    buffers += [pltpu.VMEM((tokens, units * rows), jnp.bfloat16)] * own
    return buffers + [pltpu.SemaphoreType.DMA((units,))] * (1 + own)


def pack(table, theirs, turn, cotangent, feats, rows):
    tokens, cols = cotangent.shape
    width = table.shape[0] * rows
    return pl.pallas_call(
        functools.partial(pack_kernel, rows),
        out_shape=tuple(
            jax.ShapeDtypeStruct((tokens, size), feats.dtype)
            for size in (cols, width, width + cols)
        ),
        in_specs=[SMEM_SPEC, SMEM_SPEC] + [VMEM_SPEC] * 4,
        out_specs=(VMEM_SPEC,) * 3,
        cost_estimate=pl.CostEstimate(
            flops=0, bytes_accessed=3 * feats.size * 2, transcendentals=0
        ),
        compiler_params=pltpu.CompilerParams(vmem_limit_bytes=VMEM),
        name="pack",
    )(table, theirs, *turn, cotangent, feats)


def halves_kernel(core, *refs):
    count = len(refs) // 2
    sems = refs[-1]
    copies = []
    for at, (whole, half) in enumerate(zip(refs[:count], refs[count:-1])):
        rows = half.shape[0]
        mine = pl.ds(pl.multiple_of(core[0] * rows, rows), rows)
        copies.append(pltpu.make_async_copy(whole.at[mine], half, sems.at[at]))
    for copy in copies:
        copy.start()
    for copy in copies:
        copy.wait()


def halves(core, arrays, rows):
    half = jax.ShapeDtypeStruct((rows, arrays[0].shape[1]), arrays[0].dtype)
    return pl.pallas_call(
        halves_kernel,
        out_shape=(half,) * len(arrays),
        in_specs=[SMEM_SPEC] + [ANY_SPEC] * len(arrays),
        out_specs=(VMEM_SPEC,) * len(arrays),
        scratch_shapes=[pltpu.SemaphoreType.DMA((len(arrays),))],
        cost_estimate=pl.CostEstimate(
            flops=0, bytes_accessed=4 * len(arrays) * half.size, transcendentals=0
        ),
        compiler_params=pltpu.CompilerParams(vmem_limit_bytes=VMEM),
        name="halves",
    )(core, *arrays)


def near_shards(table, mine, other, rot, weights, rows, width):
    tokens = mine.shape[0]
    cols = rot.shape[1]
    total = sum(weight.shape[0] for weight in weights) // rows
    return pl.pallas_call(
        functools.partial(near_kernel, rows, len(weights)),
        out_shape=(
            jax.ShapeDtypeStruct((tokens, width), jnp.bfloat16),
            jax.ShapeDtypeStruct((tokens, total * rows), jnp.bfloat16),
            jax.ShapeDtypeStruct((total, rows // GROUP, cols), jnp.float32),
        )
        + (jax.ShapeDtypeStruct((2 * tokens, cols), jnp.bfloat16),) * 2,
        in_specs=[SMEM_SPEC] + [VMEM_SPEC] * 3 + [ANY_SPEC] * len(weights),
        out_specs=(ANY_SPEC,) + (VMEM_SPEC,) * 4,
        scratch_shapes=scratch(total, rows, cols, tokens, 1),
        cost_estimate=cost(total, rows, cols, tokens, 2),
        compiler_params=pltpu.CompilerParams(vmem_limit_bytes=VMEM),
        name="near_shards",
    )(table, rot, mine, other, *weights)


def far_sums(table, mine, other, rot, weights, near_sums, rows, devices):
    tokens = mine.shape[0]
    near, groups, cols = near_sums.shape
    total = sum(weight.shape[0] for weight in weights) // rows
    return pl.pallas_call(
        functools.partial(far_sums_kernel, rows, len(weights), near),
        out_shape=jax.ShapeDtypeStruct((devices, groups, cols), jnp.bfloat16),
        in_specs=[SMEM_SPEC] + [VMEM_SPEC] * 4 + [ANY_SPEC] * len(weights),
        out_specs=VMEM_SPEC,
        scratch_shapes=scratch(total, rows, cols, tokens, 0),
        cost_estimate=cost(total, rows, cols, tokens, 1),
        compiler_params=pltpu.CompilerParams(vmem_limit_bytes=VMEM),
        name="far_sums",
    )(table, rot, near_sums, mine, other, *weights)


def far_grad(table, rot, weights, grad, rows, near):
    tokens = grad.shape[0]
    cols = rot.shape[1]
    total = sum(weight.shape[0] for weight in weights) // rows
    return pl.pallas_call(
        functools.partial(far_grad_kernel, rows, len(weights), near),
        out_shape=(
            jax.ShapeDtypeStruct(grad.shape, grad.dtype),
            jax.ShapeDtypeStruct((tokens, total * rows), jnp.bfloat16),
        ),
        in_specs=[SMEM_SPEC, VMEM_SPEC] + [ANY_SPEC] * (len(weights) + 1),
        out_specs=(ANY_SPEC, VMEM_SPEC),
        scratch_shapes=scratch(total, rows, cols, tokens, 1),
        input_output_aliases={2 + len(weights): 0},
        cost_estimate=cost(total, rows, cols, tokens, 1),
        compiler_params=pltpu.CompilerParams(vmem_limit_bytes=VMEM),
        name="far_grad",
    )(table, rot, *weights, grad)


def place_kernel(count, first, table, blocks_ref, grad_in, grad_ref, sems):
    rows = blocks_ref.shape[1] // count
    copies = [
        pltpu.make_async_copy(
            blocks_ref.at[:, pl.ds(unit * rows, rows)],
            grad_ref.at[:, columns_of(table, first + unit, rows)],
            sems.at[unit],
        )
        for unit in range(count)
    ]
    for copy in copies:
        copy.start()
    for copy in copies:
        copy.wait()


def place(table, blocks, grad, rows, first):
    count = blocks.shape[1] // rows
    return pl.pallas_call(
        functools.partial(place_kernel, count, first),
        out_shape=jax.ShapeDtypeStruct(grad.shape, grad.dtype),
        in_specs=[SMEM_SPEC, VMEM_SPEC, ANY_SPEC],
        out_specs=ANY_SPEC,
        scratch_shapes=[pltpu.SemaphoreType.DMA((count,))],
        input_output_aliases={2: 0},
        cost_estimate=pl.CostEstimate(
            flops=0, bytes_accessed=2 * blocks.size * 2, transcendentals=0
        ),
        compiler_params=pltpu.CompilerParams(vmem_limit_bytes=VMEM),
        name="place",
    )(table, blocks, grad)


def unit_table(x, y, core):
    sign = 2 * core - 1

    def owner(dx, dy, half):
        return (((y + sign * dy) % NYL) * NX + (x + sign * dx) % NX) * 2 + half

    return (
        [owner(0, 0, core)]
        + [owner(1, 0, 0), owner(1, 0, 1)]
        + [owner(0, 1, 0), owner(0, 1, 1)]
        + [owner(1, 1, 0), owner(1, 1, 1)]
        + [owner(1, -1, 0), owner(1, -1, 1)]
        + [owner(2, 0, core), owner(0, 2, core)]
        + [owner(1, 2, 0), owner(1, 2, 1)]
        + [owner(2, -1, 0), owner(2, -1, 1)]
        + [owner(2, 2, core)]
    )


def per_device(activations, key_cotangent, doc_lengths, weight_codes, zero_points, step_sizes):
    tokens = activations.shape[0]
    rows = weight_codes.shape[0]
    place_in = lax.axis_index("tensor")
    devices = NX * NYL * 2
    core = place_in % 2
    x = (place_in // 2) % NX
    y = place_in // (2 * NX)
    table = jnp.stack(unit_table(x, y, core)).astype(jnp.int32)
    theirs = jnp.stack(unit_table(x, y, 1 - core)).astype(jnp.int32)

    weight = dequant(weight_codes, zero_points, step_sizes)
    pairs = [[2 * chip, 2 * chip + 1] for chip in range(NX * NYL)]
    chip_weight = lax.all_gather(weight, "tensor", axis=0, tiled=True, axis_index_groups=pairs)

    from_y = send(chip_weight, 0, 1)
    from_x = send(chip_weight, 1, 0)

    indices = place_in * tokens + jnp.arange(tokens, dtype=jnp.int32)
    turn = rotation(token_positions(doc_lengths[0], indices))
    mine, mine_feats, to_other = pack(table, theirs, turn, key_cotangent, activations, rows)
    feats = (mine_feats, swap(to_other))
    from_x, _ = lax.optimization_barrier((from_x, to_other))

    from_xy = send(from_x, 0, 1)
    from_yx = send(from_y, 1, 0, cross=True)
    half_x, half_y = halves(core.reshape(1), [from_x, from_y], rows)
    half_x, half_y, _ = lax.optimization_barrier((half_x, half_y, feats[1]))
    from_xy, _, _ = lax.optimization_barrier((from_xy, half_x, half_y))

    far_y = send(from_xy, 0, 1)
    far_x = send(from_yx, 1, 0)
    far_xx = send(half_x, 1, 0)
    far_yy = send(half_y, 0, 1)
    half_xy = lax.dynamic_slice_in_dim(from_xy, core * rows, rows, axis=0)
    half_xy, _, _ = lax.optimization_barrier((half_xy, far_xx, far_yy))
    far = send(half_xy, 1, 1)

    near = [weight, from_x, from_y, from_xy, from_yx]
    grad, sent_near, sums_near, rot, rot_again = near_shards(
        table, *feats, mine, near, rows, activations.shape[1]
    )
    fars = [far_xx, far_yy, far_y, far_x, far]
    at_hand = sums_near.shape[0]
    sums = far_sums(table, *feats, rot, fars, sums_near, rows, devices)
    shares = lax.all_to_all(sums, "tensor", split_axis=0, concat_axis=0, tiled=True)

    grad, sent_far = far_grad(table, rot_again, fars, grad, rows, at_hand)
    got_near = swap(sent_near)
    share = jnp.sum(shares.astype(jnp.float32), axis=0).astype(jnp.bfloat16)
    share = jnp.broadcast_to(share[None], (lax.axis_size("dp"), *share.shape))
    share, sent_far = lax.optimization_barrier((share, sent_far))
    totals = lax.all_to_all(share, "dp", split_axis=0, concat_axis=0, tiled=True)
    grad = place(theirs, got_near, grad, rows, 0)
    grad = place(theirs, swap(sent_far), grad, rows, at_hand)
    totals, grad = lax.optimization_barrier((totals, grad))
    seq_tokens = tokens * devices
    total = jnp.sum(totals.astype(jnp.float32), axis=0)
    step_grad = total / (seq_tokens * step_sizes)
    return (grad, step_grad)


def solution(mesh):
    in_specs = (
        P(("dp", "tensor"), None),
        P(("dp", "tensor"), None),
        P("dp", None),
        P("tensor", None),
        P("tensor", None),
        P("tensor", None),
    )
    out_specs = (P(("dp", "tensor"), None), P("tensor", None))
    return jax.shard_map(
        per_device, mesh=mesh, in_specs=in_specs, out_specs=out_specs, check_vma=False
    )
```

```python
import functools
import math

import jax
import jax.numpy as jnp
from jax import lax
from jax.experimental import pallas as pl
from jax.experimental.pallas import tpu as pltpu
from jax.sharding import PartitionSpec as P

HEAD = 128
GROUP = 64
AXES = ("dp", "tensor")
NX, NY, NYL, NZ = 4, 8, 4, 8
VMEM = 48 * 1024 * 1024


def device_at(x, y, z, core):
    x, y, z = x % NX, y % NY, z % NZ
    dp = z * (NY // NYL) + y // NYL
    return dp * (NX * NYL * 2) + ((y % NYL) * NX + x) * 2 + core


def permutation(target):
    return [
        (device_at(x, y, z, core), device_at(*target(x, y, z, core)))
        for x in range(NX)
        for y in range(NY)
        for z in range(NZ)
        for core in range(2)
    ]


def send(value, dx, dy, cross=False):
    def target(x, y, z, core):
        sign = 1 if (core == 0) != cross else -1
        return x + sign * dx, y + sign * dy, z, core ^ int(cross)

    return lax.ppermute(value, AXES, permutation(target))


def swap(value):
    return lax.ppermute(value, AXES, permutation(lambda x, y, z, core: (x, y, z, core ^ 1)))


def token_positions(lengths, indices):
    count = lengths.shape[0]
    order = jnp.arange(count, dtype=jnp.int32)
    ends = jnp.sum(jnp.where(order[:, None] <= order[None, :], lengths[:, None], 0), axis=0)
    starts = jnp.where(ends[None, :] <= indices[:, None], ends[None, :], 0)
    return indices - jnp.max(starts, axis=1)


def rotation(positions):
    middle = HEAD // 2
    freqs = jnp.exp(jnp.arange(middle, dtype=jnp.float32) * (-2.0 * math.log(10000.0) / HEAD))
    angles = positions.astype(jnp.float32)[:, None] * freqs[None, :]
    cosine, sine = jnp.cos(angles), jnp.sin(angles)
    even = jnp.concatenate([cosine, cosine], axis=1)
    return even, jnp.concatenate([sine, -sine], axis=1)


def dequant(codes, zeros, steps):
    groups, cols = zeros.shape
    levels = (codes.reshape(groups, GROUP, cols) - zeros[:, None, :]).astype(jnp.float32)
    return (steps[:, None, :] * levels).astype(jnp.bfloat16).reshape(codes.shape)


def columns_of(table, unit, rows):
    return pl.ds(pl.multiple_of(table[unit] * rows, rows), rows)


def load(weights, held, sems):
    copies, at = [], 0
    for unit, ref in enumerate(weights):
        rows = pl.ds(at, ref.shape[0])
        copies.append(pltpu.make_async_copy(ref, held.at[rows], sems.at[unit]))
        at += ref.shape[0]
    for copy in copies:
        copy.start()
    for copy in copies:
        copy.wait()


def group_sums(feats, weight, rot):
    weight_grad = lax.dot_general(
        feats, rot, (((0,), (0,)), ((), ())), preferred_element_type=jnp.float32
    )
    product = weight_grad * weight.astype(jnp.float32)
    rows, cols = weight.shape
    return product.reshape(rows // GROUP, GROUP, cols).sum(axis=1)


def put_grads(table, first, rows, held, rot, own, sent_ref, grad_ref, sems):
    tokens, width = own.shape
    copies = []
    for unit in range(width // rows):
        block = pl.ds(unit * rows, rows)
        grad = lax.dot_general(
            rot, held[block, :], (((1,), (1,)), ((), ())), preferred_element_type=jnp.float32
        ).astype(jnp.bfloat16)
        own[:, block] = grad[:tokens]
        sent_ref[:, block] = grad[tokens:]
        columns = columns_of(table, first + unit, rows)
        copies.append(
            pltpu.make_async_copy(own.at[:, block], grad_ref.at[:, columns], sems.at[unit])
        )
    for copy in copies:
        copy.start()
    return copies


def pack_kernel(rows, table, theirs, even_ref, odd_ref, cot_ref, feats_ref, *outs):
    rot_ref, mine_ref, sent_ref = outs
    width = mine_ref.shape[1]
    even, odd = even_ref[...], odd_ref[...]
    for at in range(0, cot_ref.shape[1], HEAD):
        head = cot_ref[:, at : at + HEAD].astype(jnp.float32)
        turned = head * even + pltpu.roll(head, HEAD // 2, 1) * odd
        rot_ref[:, at : at + HEAD] = turned.astype(rot_ref.dtype)
        sent_ref[:, width + at : width + at + HEAD] = turned.astype(rot_ref.dtype)
    for unit in range(width // rows):
        block = pl.ds(unit * rows, rows)
        mine_ref[:, block] = feats_ref[:, columns_of(table, unit, rows)]
        sent_ref[:, block] = feats_ref[:, columns_of(theirs, unit, rows)]


def near_kernel(rows, count, table, rot_ref, mine_ref, other_ref, *refs):
    weights, refs = refs[:count], refs[count:]
    grad_ref, sent_ref, sums_ref, *both, held, own, held_sems, own_sems = refs
    load(weights, held, held_sems)
    rot = jnp.concatenate([rot_ref[...], other_ref[:, mine_ref.shape[1] :]], axis=0)
    for ref in both:
        ref[...] = rot
    copies = put_grads(table, 0, rows, held, rot, own, sent_ref, grad_ref, own_sems)
    for unit in range(sums_ref.shape[0]):
        block = pl.ds(unit * rows, rows)
        feats = jnp.concatenate([mine_ref[:, block], other_ref[:, block]], axis=0)
        sums_ref[unit] = group_sums(feats, held[block, :], rot)
    for copy in copies:
        copy.wait()


def far_sums_kernel(rows, count, near, table, rot_ref, near_ref, mine_ref, other_ref, *refs):
    weights, (all_ref, held, held_sems) = refs[:count], refs[count:]
    load(weights, held, held_sems)
    rot = rot_ref[...]
    sums = [near_ref[unit] for unit in range(near)]
    for unit in range(held.shape[0] // rows):
        block = pl.ds((near + unit) * rows, rows)
        feats = jnp.concatenate([mine_ref[:, block], other_ref[:, block]], axis=0)
        sums.append(group_sums(feats, held[pl.ds(unit * rows, rows), :], rot))
    all_ref[...] = jnp.zeros_like(all_ref)
    for unit, of_unit in enumerate(sums):
        all_ref[table[unit]] = of_unit.astype(all_ref.dtype)


def far_grad_kernel(rows, count, near, table, rot_ref, *refs):
    weights, refs = refs[:count], refs[count:]
    _, grad_ref, sent_ref, held, own, held_sems, own_sems = refs
    load(weights, held, held_sems)
    copies = put_grads(table, near, rows, held, rot_ref[...], own, sent_ref, grad_ref, own_sems)
    for copy in copies:
        copy.wait()


SMEM_SPEC = pl.BlockSpec(memory_space=pltpu.SMEM)
VMEM_SPEC = pl.BlockSpec(memory_space=pltpu.VMEM)
ANY_SPEC = pl.BlockSpec(memory_space=pl.ANY)


def cost(units, rows, cols, tokens, dots):
    return pl.CostEstimate(
        flops=4 * dots * units * rows * cols * tokens,
        bytes_accessed=units * rows * (cols * 2 + tokens * 4),
        transcendentals=0,
    )


def scratch(units, rows, cols, tokens, own):
    buffers = [pltpu.VMEM((units * rows, cols), jnp.bfloat16)]
    buffers += [pltpu.VMEM((tokens, units * rows), jnp.bfloat16)] * own
    return buffers + [pltpu.SemaphoreType.DMA((units,))] * (1 + own)


def pack(table, theirs, turn, cotangent, feats, rows):
    tokens, cols = cotangent.shape
    width = table.shape[0] * rows
    return pl.pallas_call(
        functools.partial(pack_kernel, rows),
        out_shape=tuple(
            jax.ShapeDtypeStruct((tokens, size), feats.dtype)
            for size in (cols, width, width + cols)
        ),
        in_specs=[SMEM_SPEC, SMEM_SPEC] + [VMEM_SPEC] * 4,
        out_specs=(VMEM_SPEC,) * 3,
        cost_estimate=pl.CostEstimate(
            flops=0, bytes_accessed=3 * feats.size * 2, transcendentals=0
        ),
        compiler_params=pltpu.CompilerParams(vmem_limit_bytes=VMEM),
        name="pack",
    )(table, theirs, *turn, cotangent, feats)


def halves_kernel(core, *refs):
    count = len(refs) // 2
    sems = refs[-1]
    copies = []
    for at, (whole, half) in enumerate(zip(refs[:count], refs[count:-1])):
        rows = half.shape[0]
        mine = pl.ds(pl.multiple_of(core[0] * rows, rows), rows)
        copies.append(pltpu.make_async_copy(whole.at[mine], half, sems.at[at]))
    for copy in copies:
        copy.start()
    for copy in copies:
        copy.wait()


def halves(core, arrays, rows):
    half = jax.ShapeDtypeStruct((rows, arrays[0].shape[1]), arrays[0].dtype)
    return pl.pallas_call(
        halves_kernel,
        out_shape=(half,) * len(arrays),
        in_specs=[SMEM_SPEC] + [ANY_SPEC] * len(arrays),
        out_specs=(VMEM_SPEC,) * len(arrays),
        scratch_shapes=[pltpu.SemaphoreType.DMA((len(arrays),))],
        cost_estimate=pl.CostEstimate(
            flops=0, bytes_accessed=4 * len(arrays) * half.size, transcendentals=0
        ),
        compiler_params=pltpu.CompilerParams(vmem_limit_bytes=VMEM),
        name="halves",
    )(core, *arrays)


def near_shards(table, mine, other, rot, weights, rows, width):
    tokens = mine.shape[0]
    cols = rot.shape[1]
    total = sum(weight.shape[0] for weight in weights) // rows
    return pl.pallas_call(
        functools.partial(near_kernel, rows, len(weights)),
        out_shape=(
            jax.ShapeDtypeStruct((tokens, width), jnp.bfloat16),
            jax.ShapeDtypeStruct((tokens, total * rows), jnp.bfloat16),
            jax.ShapeDtypeStruct((total, rows // GROUP, cols), jnp.float32),
        )
        + (jax.ShapeDtypeStruct((2 * tokens, cols), jnp.bfloat16),) * 2,
        in_specs=[SMEM_SPEC] + [VMEM_SPEC] * 3 + [ANY_SPEC] * len(weights),
        out_specs=(ANY_SPEC,) + (VMEM_SPEC,) * 4,
        scratch_shapes=scratch(total, rows, cols, tokens, 1),
        cost_estimate=cost(total, rows, cols, tokens, 2),
        compiler_params=pltpu.CompilerParams(vmem_limit_bytes=VMEM),
        name="near_shards",
    )(table, rot, mine, other, *weights)


def far_sums(table, mine, other, rot, weights, near_sums, rows, devices):
    tokens = mine.shape[0]
    near, groups, cols = near_sums.shape
    total = sum(weight.shape[0] for weight in weights) // rows
    return pl.pallas_call(
        functools.partial(far_sums_kernel, rows, len(weights), near),
        out_shape=jax.ShapeDtypeStruct((devices, groups, cols), jnp.bfloat16),
        in_specs=[SMEM_SPEC] + [VMEM_SPEC] * 4 + [ANY_SPEC] * len(weights),
        out_specs=VMEM_SPEC,
        scratch_shapes=scratch(total, rows, cols, tokens, 0),
        cost_estimate=cost(total, rows, cols, tokens, 1),
        compiler_params=pltpu.CompilerParams(vmem_limit_bytes=VMEM),
        name="far_sums",
    )(table, rot, near_sums, mine, other, *weights)


def far_grad(table, rot, weights, grad, rows, near):
    tokens = grad.shape[0]
    cols = rot.shape[1]
    total = sum(weight.shape[0] for weight in weights) // rows
    return pl.pallas_call(
        functools.partial(far_grad_kernel, rows, len(weights), near),
        out_shape=(
            jax.ShapeDtypeStruct(grad.shape, grad.dtype),
            jax.ShapeDtypeStruct((tokens, total * rows), jnp.bfloat16),
        ),
        in_specs=[SMEM_SPEC, VMEM_SPEC] + [ANY_SPEC] * (len(weights) + 1),
        out_specs=(ANY_SPEC, VMEM_SPEC),
        scratch_shapes=scratch(total, rows, cols, tokens, 1),
        input_output_aliases={2 + len(weights): 0},
        cost_estimate=cost(total, rows, cols, tokens, 1),
        compiler_params=pltpu.CompilerParams(vmem_limit_bytes=VMEM),
        name="far_grad",
    )(table, rot, *weights, grad)


def place_kernel(count, first, table, blocks_ref, grad_in, grad_ref, sems):
    rows = blocks_ref.shape[1] // count
    copies = [
        pltpu.make_async_copy(
            blocks_ref.at[:, pl.ds(unit * rows, rows)],
            grad_ref.at[:, columns_of(table, first + unit, rows)],
            sems.at[unit],
        )
        for unit in range(count)
    ]
    for copy in copies:
        copy.start()
    for copy in copies:
        copy.wait()


def place(table, blocks, grad, rows, first):
    count = blocks.shape[1] // rows
    return pl.pallas_call(
        functools.partial(place_kernel, count, first),
        out_shape=jax.ShapeDtypeStruct(grad.shape, grad.dtype),
        in_specs=[SMEM_SPEC, VMEM_SPEC, ANY_SPEC],
        out_specs=ANY_SPEC,
        scratch_shapes=[pltpu.SemaphoreType.DMA((count,))],
        input_output_aliases={2: 0},
        cost_estimate=pl.CostEstimate(
            flops=0, bytes_accessed=2 * blocks.size * 2, transcendentals=0
        ),
        compiler_params=pltpu.CompilerParams(vmem_limit_bytes=VMEM),
        name="place",
    )(table, blocks, grad)


def unit_table(x, y, core):
    sign = 2 * core - 1

    def owner(dx, dy, half):
        return (((y + sign * dy) % NYL) * NX + (x + sign * dx) % NX) * 2 + half

    return (
        [owner(0, 0, core)]
        + [owner(1, 0, 0), owner(1, 0, 1)]
        + [owner(0, 1, 0), owner(0, 1, 1)]
        + [owner(1, 1, 0), owner(1, 1, 1)]
        + [owner(1, -1, 0), owner(1, -1, 1)]
        + [owner(2, 0, core), owner(0, 2, core)]
        + [owner(1, 2, 0), owner(1, 2, 1)]
        + [owner(2, -1, 0), owner(2, -1, 1)]
        + [owner(2, 2, core)]
    )


def per_device(activations, key_cotangent, doc_lengths, weight_codes, zero_points, step_sizes):
    tokens = activations.shape[0]
    rows = weight_codes.shape[0]
    place_in = lax.axis_index("tensor")
    devices = NX * NYL * 2
    core = place_in % 2
    x = (place_in // 2) % NX
    y = place_in // (2 * NX)
    table = jnp.stack(unit_table(x, y, core)).astype(jnp.int32)
    theirs = jnp.stack(unit_table(x, y, 1 - core)).astype(jnp.int32)

    weight = dequant(weight_codes, zero_points, step_sizes)
    pairs = [[2 * chip, 2 * chip + 1] for chip in range(NX * NYL)]
    chip_weight = lax.all_gather(weight, "tensor", axis=0, tiled=True, axis_index_groups=pairs)

    from_y = send(chip_weight, 0, 1)
    from_x = send(chip_weight, 1, 0)

    indices = place_in * tokens + jnp.arange(tokens, dtype=jnp.int32)
    turn = rotation(token_positions(doc_lengths[0], indices))
    mine, mine_feats, to_other = pack(table, theirs, turn, key_cotangent, activations, rows)
    own, _ = lax.optimization_barrier((weight, to_other))
    far_xx = send(own, 2, 0)
    from_x, _ = lax.optimization_barrier((from_x, to_other))
    to_other, _ = lax.optimization_barrier((to_other, far_xx))
    feats = (mine_feats, swap(to_other))

    from_xy = send(from_x, 0, 1)
    from_yx = send(from_y, 1, 0, cross=True)
    (half_y,) = halves(core.reshape(1), [from_y], rows)
    from_xy, _ = lax.optimization_barrier((from_xy, half_y))

    far_y = send(from_xy, 0, 1)
    far_x = send(from_yx, 1, 0)
    far_yy = send(half_y, 0, 1)
    half_xy = lax.dynamic_slice_in_dim(from_xy, core * rows, rows, axis=0)
    half_xy, _ = lax.optimization_barrier((half_xy, far_yy))
    far = send(half_xy, 1, 1)

    near = [weight, from_x, from_y, from_xy, from_yx]
    grad, sent_near, sums_near, rot, rot_again = near_shards(
        table, *feats, mine, near, rows, activations.shape[1]
    )
    fars = [far_xx, far_yy, far_y, far_x, far]
    at_hand = sums_near.shape[0]
    sums = far_sums(table, *feats, rot, fars, sums_near, rows, devices)
    shares = lax.all_to_all(sums, "tensor", split_axis=0, concat_axis=0, tiled=True)

    grad, sent_far = far_grad(table, rot_again, fars, grad, rows, at_hand)
    got_near = swap(sent_near)
    share = jnp.sum(shares.astype(jnp.float32), axis=0).astype(jnp.bfloat16)
    share = jnp.broadcast_to(share[None], (lax.axis_size("dp"), *share.shape))
    share, sent_far = lax.optimization_barrier((share, sent_far))
    totals = lax.all_to_all(share, "dp", split_axis=0, concat_axis=0, tiled=True)
    grad = place(theirs, got_near, grad, rows, 0)
    grad = place(theirs, swap(sent_far), grad, rows, at_hand)
    totals, grad = lax.optimization_barrier((totals, grad))
    seq_tokens = tokens * devices
    total = jnp.sum(totals.astype(jnp.float32), axis=0)
    step_grad = total / (seq_tokens * step_sizes)
    return (grad, step_grad)


def solution(mesh):
    in_specs = (
        P(("dp", "tensor"), None),
        P(("dp", "tensor"), None),
        P("dp", None),
        P("tensor", None),
        P("tensor", None),
        P("tensor", None),
    )
    out_specs = (P(("dp", "tensor"), None), P("tensor", None))
    return jax.shard_map(
        per_device, mesh=mesh, in_specs=in_specs, out_specs=out_specs, check_vma=False
    )
```

```python
import functools
import math

import jax
import jax.numpy as jnp
from jax import lax
from jax.experimental import pallas as pl
from jax.experimental.pallas import tpu as pltpu
from jax.sharding import PartitionSpec as P

HEAD = 128
GROUP = 64
AXES = ("dp", "tensor")
NX, NY, NYL, NZ = 4, 8, 4, 8
VMEM = 48 * 1024 * 1024


def device_at(x, y, z, core):
    x, y, z = x % NX, y % NY, z % NZ
    dp = z * (NY // NYL) + y // NYL
    return dp * (NX * NYL * 2) + ((y % NYL) * NX + x) * 2 + core


def permutation(target):
    return [
        (device_at(x, y, z, core), device_at(*target(x, y, z, core)))
        for x in range(NX)
        for y in range(NY)
        for z in range(NZ)
        for core in range(2)
    ]


def send(value, dx, dy, cross=False):
    def target(x, y, z, core):
        sign = 1 if (core == 0) != cross else -1
        return x + sign * dx, y + sign * dy, z, core ^ int(cross)

    return lax.ppermute(value, AXES, permutation(target))


def swap(value):
    return lax.ppermute(value, AXES, permutation(lambda x, y, z, core: (x, y, z, core ^ 1)))


def token_positions(lengths, indices):
    count = lengths.shape[0]
    order = jnp.arange(count, dtype=jnp.int32)
    ends = jnp.sum(jnp.where(order[:, None] <= order[None, :], lengths[:, None], 0), axis=0)
    starts = jnp.where(ends[None, :] <= indices[:, None], ends[None, :], 0)
    return indices - jnp.max(starts, axis=1)


def rotation(positions):
    middle = HEAD // 2
    freqs = jnp.exp(jnp.arange(middle, dtype=jnp.float32) * (-2.0 * math.log(10000.0) / HEAD))
    angles = positions.astype(jnp.float32)[:, None] * freqs[None, :]
    cosine, sine = jnp.cos(angles), jnp.sin(angles)
    even = jnp.concatenate([cosine, cosine], axis=1)
    return even, jnp.concatenate([sine, -sine], axis=1)


def dequant(codes, zeros, steps):
    groups, cols = zeros.shape
    levels = (codes.reshape(groups, GROUP, cols) - zeros[:, None, :]).astype(jnp.float32)
    return (steps[:, None, :] * levels).astype(jnp.bfloat16).reshape(codes.shape)


def columns_of(table, unit, rows):
    return pl.ds(pl.multiple_of(table[unit] * rows, rows), rows)


def load(weights, held, sems):
    copies, at = [], 0
    for unit, ref in enumerate(weights):
        rows = pl.ds(at, ref.shape[0])
        copies.append(pltpu.make_async_copy(ref, held.at[rows], sems.at[unit]))
        at += ref.shape[0]
    for copy in copies:
        copy.start()
    for copy in copies:
        copy.wait()


def group_sums(feats, weight, rot):
    weight_grad = lax.dot_general(
        feats, rot, (((0,), (0,)), ((), ())), preferred_element_type=jnp.float32
    )
    product = weight_grad * weight.astype(jnp.float32)
    rows, cols = weight.shape
    return product.reshape(rows // GROUP, GROUP, cols).sum(axis=1)


def put_grads(table, first, rows, held, rot, own, sent_ref, grad_ref, sems):
    tokens, width = own.shape
    copies = []
    for unit in range(width // rows):
        block = pl.ds(unit * rows, rows)
        grad = lax.dot_general(
            rot, held[block, :], (((1,), (1,)), ((), ())), preferred_element_type=jnp.float32
        ).astype(jnp.bfloat16)
        own[:, block] = grad[:tokens]
        sent_ref[:, block] = grad[tokens:]
        columns = columns_of(table, first + unit, rows)
        copies.append(
            pltpu.make_async_copy(own.at[:, block], grad_ref.at[:, columns], sems.at[unit])
        )
    for copy in copies:
        copy.start()
    return copies


def pack_kernel(rows, table, theirs, even_ref, odd_ref, cot_ref, feats_ref, *outs):
    rot_ref, mine_ref, sent_ref = outs
    width = mine_ref.shape[1]
    even, odd = even_ref[...], odd_ref[...]
    for at in range(0, cot_ref.shape[1], HEAD):
        head = cot_ref[:, at : at + HEAD].astype(jnp.float32)
        turned = head * even + pltpu.roll(head, HEAD // 2, 1) * odd
        rot_ref[:, at : at + HEAD] = turned.astype(rot_ref.dtype)
        sent_ref[:, width + at : width + at + HEAD] = turned.astype(rot_ref.dtype)
    for unit in range(width // rows):
        block = pl.ds(unit * rows, rows)
        mine_ref[:, block] = feats_ref[:, columns_of(table, unit, rows)]
        sent_ref[:, block] = feats_ref[:, columns_of(theirs, unit, rows)]


def near_kernel(rows, count, table, rot_ref, mine_ref, other_ref, *refs):
    weights, refs = refs[:count], refs[count:]
    grad_ref, sent_ref, sums_ref, *both, held, own, held_sems, own_sems = refs
    load(weights, held, held_sems)
    rot = jnp.concatenate([rot_ref[...], other_ref[:, mine_ref.shape[1] :]], axis=0)
    for ref in both:
        ref[...] = rot
    copies = put_grads(table, 0, rows, held, rot, own, sent_ref, grad_ref, own_sems)
    for unit in range(sums_ref.shape[0]):
        block = pl.ds(unit * rows, rows)
        feats = jnp.concatenate([mine_ref[:, block], other_ref[:, block]], axis=0)
        sums_ref[unit] = group_sums(feats, held[block, :], rot)
    for copy in copies:
        copy.wait()


def far_sums_kernel(rows, count, near, table, rot_ref, near_ref, mine_ref, other_ref, *refs):
    weights, (all_ref, held, held_sems) = refs[:count], refs[count:]
    load(weights, held, held_sems)
    rot = rot_ref[...]
    sums = [near_ref[unit] for unit in range(near)]
    for unit in range(held.shape[0] // rows):
        block = pl.ds((near + unit) * rows, rows)
        feats = jnp.concatenate([mine_ref[:, block], other_ref[:, block]], axis=0)
        sums.append(group_sums(feats, held[pl.ds(unit * rows, rows), :], rot))
    all_ref[...] = jnp.zeros_like(all_ref)
    for unit, of_unit in enumerate(sums):
        all_ref[table[unit]] = of_unit.astype(all_ref.dtype)


def far_grad_kernel(rows, count, near, table, rot_ref, *refs):
    weights, refs = refs[:count], refs[count:]
    _, grad_ref, sent_ref, held, own, held_sems, own_sems = refs
    load(weights, held, held_sems)
    copies = put_grads(table, near, rows, held, rot_ref[...], own, sent_ref, grad_ref, own_sems)
    for copy in copies:
        copy.wait()


SMEM_SPEC = pl.BlockSpec(memory_space=pltpu.SMEM)
VMEM_SPEC = pl.BlockSpec(memory_space=pltpu.VMEM)
ANY_SPEC = pl.BlockSpec(memory_space=pl.ANY)


def cost(units, rows, cols, tokens, dots):
    return pl.CostEstimate(
        flops=4 * dots * units * rows * cols * tokens,
        bytes_accessed=units * rows * (cols * 2 + tokens * 4),
        transcendentals=0,
    )


def scratch(units, rows, cols, tokens, own):
    buffers = [pltpu.VMEM((units * rows, cols), jnp.bfloat16)]
    buffers += [pltpu.VMEM((tokens, units * rows), jnp.bfloat16)] * own
    return buffers + [pltpu.SemaphoreType.DMA((units,))] * (1 + own)


def pack(table, theirs, turn, cotangent, feats, rows):
    tokens, cols = cotangent.shape
    width = table.shape[0] * rows
    return pl.pallas_call(
        functools.partial(pack_kernel, rows),
        out_shape=tuple(
            jax.ShapeDtypeStruct((tokens, size), feats.dtype)
            for size in (cols, width, width + cols)
        ),
        in_specs=[SMEM_SPEC, SMEM_SPEC] + [VMEM_SPEC] * 4,
        out_specs=(VMEM_SPEC,) * 3,
        cost_estimate=pl.CostEstimate(
            flops=0, bytes_accessed=3 * feats.size * 2, transcendentals=0
        ),
        compiler_params=pltpu.CompilerParams(vmem_limit_bytes=VMEM),
        name="pack",
    )(table, theirs, *turn, cotangent, feats)


def halves_kernel(core, *refs):
    count = len(refs) // 2
    sems = refs[-1]
    copies = []
    for at, (whole, half) in enumerate(zip(refs[:count], refs[count:-1])):
        rows = half.shape[0]
        mine = pl.ds(pl.multiple_of(core[0] * rows, rows), rows)
        copies.append(pltpu.make_async_copy(whole.at[mine], half, sems.at[at]))
    for copy in copies:
        copy.start()
    for copy in copies:
        copy.wait()


def halves(core, arrays, rows):
    half = jax.ShapeDtypeStruct((rows, arrays[0].shape[1]), arrays[0].dtype)
    return pl.pallas_call(
        halves_kernel,
        out_shape=(half,) * len(arrays),
        in_specs=[SMEM_SPEC] + [ANY_SPEC] * len(arrays),
        out_specs=(VMEM_SPEC,) * len(arrays),
        scratch_shapes=[pltpu.SemaphoreType.DMA((len(arrays),))],
        cost_estimate=pl.CostEstimate(
            flops=0, bytes_accessed=4 * len(arrays) * half.size, transcendentals=0
        ),
        compiler_params=pltpu.CompilerParams(vmem_limit_bytes=VMEM),
        name="halves",
    )(core, *arrays)


def near_shards(table, mine, other, rot, weights, rows, width):
    tokens = mine.shape[0]
    cols = rot.shape[1]
    total = sum(weight.shape[0] for weight in weights) // rows
    return pl.pallas_call(
        functools.partial(near_kernel, rows, len(weights)),
        out_shape=(
            jax.ShapeDtypeStruct((tokens, width), jnp.bfloat16),
            jax.ShapeDtypeStruct((tokens, total * rows), jnp.bfloat16),
            jax.ShapeDtypeStruct((total, rows // GROUP, cols), jnp.float32),
        )
        + (jax.ShapeDtypeStruct((2 * tokens, cols), jnp.bfloat16),) * 2,
        in_specs=[SMEM_SPEC] + [VMEM_SPEC] * 3 + [ANY_SPEC] * len(weights),
        out_specs=(ANY_SPEC,) + (VMEM_SPEC,) * 4,
        scratch_shapes=scratch(total, rows, cols, tokens, 1),
        cost_estimate=cost(total, rows, cols, tokens, 2),
        compiler_params=pltpu.CompilerParams(vmem_limit_bytes=VMEM),
        name="near_shards",
    )(table, rot, mine, other, *weights)


def far_sums(table, mine, other, rot, weights, near_sums, rows, devices):
    tokens = mine.shape[0]
    near, groups, cols = near_sums.shape
    total = sum(weight.shape[0] for weight in weights) // rows
    return pl.pallas_call(
        functools.partial(far_sums_kernel, rows, len(weights), near),
        out_shape=jax.ShapeDtypeStruct((devices, groups, cols), jnp.bfloat16),
        in_specs=[SMEM_SPEC] + [VMEM_SPEC] * 4 + [ANY_SPEC] * len(weights),
        out_specs=VMEM_SPEC,
        scratch_shapes=scratch(total, rows, cols, tokens, 0),
        cost_estimate=cost(total, rows, cols, tokens, 1),
        compiler_params=pltpu.CompilerParams(vmem_limit_bytes=VMEM),
        name="far_sums",
    )(table, rot, near_sums, mine, other, *weights)


def far_grad(table, rot, weights, grad, rows, near):
    tokens = grad.shape[0]
    cols = rot.shape[1]
    total = sum(weight.shape[0] for weight in weights) // rows
    return pl.pallas_call(
        functools.partial(far_grad_kernel, rows, len(weights), near),
        out_shape=(
            jax.ShapeDtypeStruct(grad.shape, grad.dtype),
            jax.ShapeDtypeStruct((tokens, total * rows), jnp.bfloat16),
        ),
        in_specs=[SMEM_SPEC, VMEM_SPEC] + [ANY_SPEC] * (len(weights) + 1),
        out_specs=(ANY_SPEC, VMEM_SPEC),
        scratch_shapes=scratch(total, rows, cols, tokens, 1),
        input_output_aliases={2 + len(weights): 0},
        cost_estimate=cost(total, rows, cols, tokens, 1),
        compiler_params=pltpu.CompilerParams(vmem_limit_bytes=VMEM),
        name="far_grad",
    )(table, rot, *weights, grad)


def place_kernel(count, first, table, blocks_ref, grad_in, grad_ref, sems):
    rows = blocks_ref.shape[1] // count
    copies = [
        pltpu.make_async_copy(
            blocks_ref.at[:, pl.ds(unit * rows, rows)],
            grad_ref.at[:, columns_of(table, first + unit, rows)],
            sems.at[unit],
        )
        for unit in range(count)
    ]
    for copy in copies:
        copy.start()
    for copy in copies:
        copy.wait()


def place(table, blocks, grad, rows, first):
    count = blocks.shape[1] // rows
    return pl.pallas_call(
        functools.partial(place_kernel, count, first),
        out_shape=jax.ShapeDtypeStruct(grad.shape, grad.dtype),
        in_specs=[SMEM_SPEC, VMEM_SPEC, ANY_SPEC],
        out_specs=ANY_SPEC,
        scratch_shapes=[pltpu.SemaphoreType.DMA((count,))],
        input_output_aliases={2: 0},
        cost_estimate=pl.CostEstimate(
            flops=0, bytes_accessed=2 * blocks.size * 2, transcendentals=0
        ),
        compiler_params=pltpu.CompilerParams(vmem_limit_bytes=VMEM),
        name="place",
    )(table, blocks, grad)


def unit_table(x, y, core):
    sign = 2 * core - 1

    def owner(dx, dy, half):
        return (((y + sign * dy) % NYL) * NX + (x + sign * dx) % NX) * 2 + half

    return (
        [owner(0, 0, core)]
        + [owner(1, 0, 0), owner(1, 0, 1)]
        + [owner(0, 1, 0), owner(0, 1, 1)]
        + [owner(1, 1, 0), owner(1, 1, 1)]
        + [owner(1, -1, 0), owner(1, -1, 1)]
        + [owner(2, 0, core), owner(0, 2, core)]
        + [owner(1, 2, 0), owner(1, 2, 1)]
        + [owner(2, -1, 0), owner(2, -1, 1)]
        + [owner(2, 2, core)]
    )


def per_device(activations, key_cotangent, doc_lengths, weight_codes, zero_points, step_sizes):
    tokens = activations.shape[0]
    rows = weight_codes.shape[0]
    place_in = lax.axis_index("tensor")
    devices = NX * NYL * 2
    core = place_in % 2
    x = (place_in // 2) % NX
    y = place_in // (2 * NX)
    table = jnp.stack(unit_table(x, y, core)).astype(jnp.int32)
    theirs = jnp.stack(unit_table(x, y, 1 - core)).astype(jnp.int32)

    weight = dequant(weight_codes, zero_points, step_sizes)
    pairs = [[2 * chip, 2 * chip + 1] for chip in range(NX * NYL)]
    chip_weight = lax.all_gather(weight, "tensor", axis=0, tiled=True, axis_index_groups=pairs)

    from_y = send(chip_weight, 0, 1)
    from_x = send(chip_weight, 1, 0)

    indices = place_in * tokens + jnp.arange(tokens, dtype=jnp.int32)
    turn = rotation(token_positions(doc_lengths[0], indices))
    mine, mine_feats, to_other = pack(table, theirs, turn, key_cotangent, activations, rows)
    own, _ = lax.optimization_barrier((weight, to_other))
    far_xx = send(own, 2, 0)
    from_x, _ = lax.optimization_barrier((from_x, to_other))
    to_other, _ = lax.optimization_barrier((to_other, far_xx))
    feats = (mine_feats, swap(to_other))

    from_xy = send(from_x, 0, 1)
    from_yx = send(from_y, 1, 0, cross=True)
    (half_y,) = halves(core.reshape(1), [from_y], rows)
    from_xy, _ = lax.optimization_barrier((from_xy, half_y))

    far_y = send(from_xy, 0, 1)
    far_x = send(from_yx, 1, 0)
    far_yy = send(half_y, 0, 1)
    half_xy = lax.dynamic_slice_in_dim(from_xy, core * rows, rows, axis=0)
    half_xy, _ = lax.optimization_barrier((half_xy, far_yy))
    far = send(half_xy, 1, 1)

    near = [weight, from_x, from_y, from_xy, from_yx]
    grad, sent_near, sums_near, rot, rot_again = near_shards(
        table, *feats, mine, near, rows, activations.shape[1]
    )
    fars = [far_xx, far_yy, far_y, far_x, far]
    at_hand = sums_near.shape[0]
    sums = far_sums(table, *feats, rot, fars, sums_near, rows, devices)
    shares = lax.all_to_all(sums, "tensor", split_axis=0, concat_axis=0, tiled=True)

    grad, sent_far = far_grad(table, rot_again, fars, grad, rows, at_hand)
    got_near = swap(sent_near)
    share = jnp.sum(shares.astype(jnp.float32), axis=0).astype(jnp.bfloat16)
    share = jnp.broadcast_to(share[None], (lax.axis_size("dp"), *share.shape))
    share, sent_far = lax.optimization_barrier((share, sent_far))
    totals = lax.all_to_all(share, "dp", split_axis=0, concat_axis=0, tiled=True)
    sent_far, got_near = lax.optimization_barrier((sent_far, got_near))
    grad = place(theirs, got_near, grad, rows, 0)
    grad = place(theirs, swap(sent_far), grad, rows, at_hand)
    seq_tokens = tokens * devices
    total = jnp.sum(totals.astype(jnp.float32), axis=0)
    step_grad = total / (seq_tokens * step_sizes)
    return (grad, step_grad)


def solution(mesh):
    in_specs = (
        P(("dp", "tensor"), None),
        P(("dp", "tensor"), None),
        P("dp", None),
        P("tensor", None),
        P("tensor", None),
        P("tensor", None),
    )
    out_specs = (P(("dp", "tensor"), None), P("tensor", None))
    return jax.shard_map(
        per_device, mesh=mesh, in_specs=in_specs, out_specs=out_specs, check_vma=False
    )
```

```python
import functools
import math

import jax
import jax.numpy as jnp
from jax import lax
from jax.experimental import pallas as pl
from jax.experimental.pallas import tpu as pltpu
from jax.sharding import PartitionSpec as P

HEAD = 128
GROUP = 64
AXES = ("dp", "tensor")
NX, NY, NYL, NZ = 4, 8, 4, 8
VMEM = 48 * 1024 * 1024


def device_at(x, y, z, core):
    x, y, z = x % NX, y % NY, z % NZ
    dp = z * (NY // NYL) + y // NYL
    return dp * (NX * NYL * 2) + ((y % NYL) * NX + x) * 2 + core


def permutation(target):
    return [
        (device_at(x, y, z, core), device_at(*target(x, y, z, core)))
        for x in range(NX)
        for y in range(NY)
        for z in range(NZ)
        for core in range(2)
    ]


def send(value, dx, dy, cross=False):
    def target(x, y, z, core):
        sign = 1 if (core == 0) != cross else -1
        return x + sign * dx, y + sign * dy, z, core ^ int(cross)

    return lax.ppermute(value, AXES, permutation(target))


def swap(value):
    return lax.ppermute(value, AXES, permutation(lambda x, y, z, core: (x, y, z, core ^ 1)))


def token_positions(lengths, indices):
    count = lengths.shape[0]
    order = jnp.arange(count, dtype=jnp.int32)
    ends = jnp.sum(jnp.where(order[:, None] <= order[None, :], lengths[:, None], 0), axis=0)
    starts = jnp.where(ends[None, :] <= indices[:, None], ends[None, :], 0)
    return indices - jnp.max(starts, axis=1)


def rotation(positions):
    middle = HEAD // 2
    freqs = jnp.exp(jnp.arange(middle, dtype=jnp.float32) * (-2.0 * math.log(10000.0) / HEAD))
    angles = positions.astype(jnp.float32)[:, None] * freqs[None, :]
    cosine, sine = jnp.cos(angles), jnp.sin(angles)
    even = jnp.concatenate([cosine, cosine], axis=1)
    return even, jnp.concatenate([sine, -sine], axis=1)


def dequant(codes, zeros, steps):
    groups, cols = zeros.shape
    levels = (codes.reshape(groups, GROUP, cols) - zeros[:, None, :]).astype(jnp.float32)
    return (steps[:, None, :] * levels).astype(jnp.bfloat16).reshape(codes.shape)


def columns_of(table, unit, rows):
    return pl.ds(pl.multiple_of(table[unit] * rows, rows), rows)


def load(weights, held, sems):
    copies, at = [], 0
    for unit, ref in enumerate(weights):
        rows = pl.ds(at, ref.shape[0])
        copies.append(pltpu.make_async_copy(ref, held.at[rows], sems.at[unit]))
        at += ref.shape[0]
    for copy in copies:
        copy.start()
    for copy in copies:
        copy.wait()


def group_sums(feats, weight, rot):
    weight_grad = lax.dot_general(
        feats, rot, (((0,), (0,)), ((), ())), preferred_element_type=jnp.float32
    )
    product = weight_grad * weight.astype(jnp.float32)
    rows, cols = weight.shape
    return product.reshape(rows // GROUP, GROUP, cols).sum(axis=1)


def put_grads(table, first, rows, held, rot, own, sent_ref, grad_ref, sems):
    tokens, width = own.shape
    copies = []
    for unit in range(width // rows):
        block = pl.ds(unit * rows, rows)
        grad = lax.dot_general(
            rot, held[block, :], (((1,), (1,)), ((), ())), preferred_element_type=jnp.float32
        ).astype(jnp.bfloat16)
        own[:, block] = grad[:tokens]
        sent_ref[:, block] = grad[tokens:]
        columns = columns_of(table, first + unit, rows)
        copies.append(
            pltpu.make_async_copy(own.at[:, block], grad_ref.at[:, columns], sems.at[unit])
        )
    for copy in copies:
        copy.start()
    return copies


def pack_kernel(rows, table, theirs, even_ref, odd_ref, cot_ref, feats_ref, *outs):
    rot_ref, mine_ref, sent_ref = outs
    width = mine_ref.shape[1]
    even, odd = even_ref[...], odd_ref[...]
    for at in range(0, cot_ref.shape[1], HEAD):
        head = cot_ref[:, at : at + HEAD].astype(jnp.float32)
        turned = head * even + pltpu.roll(head, HEAD // 2, 1) * odd
        rot_ref[:, at : at + HEAD] = turned.astype(rot_ref.dtype)
        sent_ref[:, width + at : width + at + HEAD] = turned.astype(rot_ref.dtype)
    for unit in range(width // rows):
        block = pl.ds(unit * rows, rows)
        mine_ref[:, block] = feats_ref[:, columns_of(table, unit, rows)]
        sent_ref[:, block] = feats_ref[:, columns_of(theirs, unit, rows)]


def near_kernel(rows, count, table, rot_ref, mine_ref, other_ref, *refs):
    weights, refs = refs[:count], refs[count:]
    grad_ref, sent_ref, sums_ref, *both, held, own, held_sems, own_sems = refs
    load(weights, held, held_sems)
    rot = jnp.concatenate([rot_ref[...], other_ref[:, mine_ref.shape[1] :]], axis=0)
    for ref in both:
        ref[...] = rot
    copies = put_grads(table, 0, rows, held, rot, own, sent_ref, grad_ref, own_sems)
    for unit in range(sums_ref.shape[0]):
        block = pl.ds(unit * rows, rows)
        feats = jnp.concatenate([mine_ref[:, block], other_ref[:, block]], axis=0)
        sums_ref[unit] = group_sums(feats, held[block, :], rot)
    for copy in copies:
        copy.wait()


def far_sums_kernel(rows, count, near, table, rot_ref, near_ref, mine_ref, other_ref, *refs):
    weights, (all_ref, held, held_sems) = refs[:count], refs[count:]
    load(weights, held, held_sems)
    rot = rot_ref[...]
    sums = [near_ref[unit] for unit in range(near)]
    for unit in range(held.shape[0] // rows):
        block = pl.ds((near + unit) * rows, rows)
        feats = jnp.concatenate([mine_ref[:, block], other_ref[:, block]], axis=0)
        sums.append(group_sums(feats, held[pl.ds(unit * rows, rows), :], rot))
    all_ref[...] = jnp.zeros_like(all_ref)
    for unit, of_unit in enumerate(sums):
        all_ref[table[unit]] = of_unit.astype(all_ref.dtype)


def far_grad_kernel(rows, count, near, table, rot_ref, *refs):
    weights, refs = refs[:count], refs[count:]
    _, grad_ref, sent_ref, held, own, held_sems, own_sems = refs
    load(weights, held, held_sems)
    copies = put_grads(table, near, rows, held, rot_ref[...], own, sent_ref, grad_ref, own_sems)
    for copy in copies:
        copy.wait()


SMEM_SPEC = pl.BlockSpec(memory_space=pltpu.SMEM)
VMEM_SPEC = pl.BlockSpec(memory_space=pltpu.VMEM)
ANY_SPEC = pl.BlockSpec(memory_space=pl.ANY)


def cost(units, rows, cols, tokens, dots):
    return pl.CostEstimate(
        flops=4 * dots * units * rows * cols * tokens,
        bytes_accessed=units * rows * (cols * 2 + tokens * 4),
        transcendentals=0,
    )


def scratch(units, rows, cols, tokens, own):
    buffers = [pltpu.VMEM((units * rows, cols), jnp.bfloat16)]
    buffers += [pltpu.VMEM((tokens, units * rows), jnp.bfloat16)] * own
    return buffers + [pltpu.SemaphoreType.DMA((units,))] * (1 + own)


def pack(table, theirs, turn, cotangent, feats, rows):
    tokens, cols = cotangent.shape
    width = table.shape[0] * rows
    return pl.pallas_call(
        functools.partial(pack_kernel, rows),
        out_shape=tuple(
            jax.ShapeDtypeStruct((tokens, size), feats.dtype)
            for size in (cols, width, width + cols)
        ),
        in_specs=[SMEM_SPEC, SMEM_SPEC] + [VMEM_SPEC] * 4,
        out_specs=(VMEM_SPEC,) * 3,
        cost_estimate=pl.CostEstimate(
            flops=0, bytes_accessed=3 * feats.size * 2, transcendentals=0
        ),
        compiler_params=pltpu.CompilerParams(vmem_limit_bytes=VMEM),
        name="pack",
    )(table, theirs, *turn, cotangent, feats)


def halves_kernel(core, *refs):
    count = len(refs) // 2
    sems = refs[-1]
    copies = []
    for at, (whole, half) in enumerate(zip(refs[:count], refs[count:-1])):
        rows = half.shape[0]
        mine = pl.ds(pl.multiple_of(core[0] * rows, rows), rows)
        copies.append(pltpu.make_async_copy(whole.at[mine], half, sems.at[at]))
    for copy in copies:
        copy.start()
    for copy in copies:
        copy.wait()


def halves(core, arrays, rows):
    half = jax.ShapeDtypeStruct((rows, arrays[0].shape[1]), arrays[0].dtype)
    return pl.pallas_call(
        halves_kernel,
        out_shape=(half,) * len(arrays),
        in_specs=[SMEM_SPEC] + [ANY_SPEC] * len(arrays),
        out_specs=(VMEM_SPEC,) * len(arrays),
        scratch_shapes=[pltpu.SemaphoreType.DMA((len(arrays),))],
        cost_estimate=pl.CostEstimate(
            flops=0, bytes_accessed=4 * len(arrays) * half.size, transcendentals=0
        ),
        compiler_params=pltpu.CompilerParams(vmem_limit_bytes=VMEM),
        name="halves",
    )(core, *arrays)


def near_shards(table, mine, other, rot, weights, rows, width):
    tokens = mine.shape[0]
    cols = rot.shape[1]
    total = sum(weight.shape[0] for weight in weights) // rows
    return pl.pallas_call(
        functools.partial(near_kernel, rows, len(weights)),
        out_shape=(
            jax.ShapeDtypeStruct((tokens, width), jnp.bfloat16),
            jax.ShapeDtypeStruct((tokens, total * rows), jnp.bfloat16),
            jax.ShapeDtypeStruct((total, rows // GROUP, cols), jnp.float32),
        )
        + (jax.ShapeDtypeStruct((2 * tokens, cols), jnp.bfloat16),) * 2,
        in_specs=[SMEM_SPEC] + [VMEM_SPEC] * 3 + [ANY_SPEC] * len(weights),
        out_specs=(ANY_SPEC,) + (VMEM_SPEC,) * 4,
        scratch_shapes=scratch(total, rows, cols, tokens, 1),
        cost_estimate=cost(total, rows, cols, tokens, 2),
        compiler_params=pltpu.CompilerParams(vmem_limit_bytes=VMEM),
        name="near_shards",
    )(table, rot, mine, other, *weights)


def far_sums(table, mine, other, rot, weights, near_sums, rows, devices):
    tokens = mine.shape[0]
    near, groups, cols = near_sums.shape
    total = sum(weight.shape[0] for weight in weights) // rows
    return pl.pallas_call(
        functools.partial(far_sums_kernel, rows, len(weights), near),
        out_shape=jax.ShapeDtypeStruct((devices, groups, cols), jnp.bfloat16),
        in_specs=[SMEM_SPEC] + [VMEM_SPEC] * 4 + [ANY_SPEC] * len(weights),
        out_specs=VMEM_SPEC,
        scratch_shapes=scratch(total, rows, cols, tokens, 0),
        cost_estimate=cost(total, rows, cols, tokens, 1),
        compiler_params=pltpu.CompilerParams(vmem_limit_bytes=VMEM),
        name="far_sums",
    )(table, rot, near_sums, mine, other, *weights)


def far_grad(table, rot, weights, grad, rows, near):
    tokens = grad.shape[0]
    cols = rot.shape[1]
    total = sum(weight.shape[0] for weight in weights) // rows
    return pl.pallas_call(
        functools.partial(far_grad_kernel, rows, len(weights), near),
        out_shape=(
            jax.ShapeDtypeStruct(grad.shape, grad.dtype),
            jax.ShapeDtypeStruct((tokens, total * rows), jnp.bfloat16),
        ),
        in_specs=[SMEM_SPEC, VMEM_SPEC] + [ANY_SPEC] * (len(weights) + 1),
        out_specs=(ANY_SPEC, VMEM_SPEC),
        scratch_shapes=scratch(total, rows, cols, tokens, 1),
        input_output_aliases={2 + len(weights): 0},
        cost_estimate=cost(total, rows, cols, tokens, 1),
        compiler_params=pltpu.CompilerParams(vmem_limit_bytes=VMEM),
        name="far_grad",
    )(table, rot, *weights, grad)


def place_kernel(count, first, table, blocks_ref, grad_in, grad_ref, sems):
    rows = blocks_ref.shape[1] // count
    copies = [
        pltpu.make_async_copy(
            blocks_ref.at[:, pl.ds(unit * rows, rows)],
            grad_ref.at[:, columns_of(table, first + unit, rows)],
            sems.at[unit],
        )
        for unit in range(count)
    ]
    for copy in copies:
        copy.start()
    for copy in copies:
        copy.wait()


def place(table, blocks, grad, rows, first):
    count = blocks.shape[1] // rows
    return pl.pallas_call(
        functools.partial(place_kernel, count, first),
        out_shape=jax.ShapeDtypeStruct(grad.shape, grad.dtype),
        in_specs=[SMEM_SPEC, VMEM_SPEC, ANY_SPEC],
        out_specs=ANY_SPEC,
        scratch_shapes=[pltpu.SemaphoreType.DMA((count,))],
        input_output_aliases={2: 0},
        cost_estimate=pl.CostEstimate(
            flops=0, bytes_accessed=2 * blocks.size * 2, transcendentals=0
        ),
        compiler_params=pltpu.CompilerParams(vmem_limit_bytes=VMEM),
        name="place",
    )(table, blocks, grad)


def unit_table(x, y, core):
    sign = 2 * core - 1

    def owner(dx, dy, half):
        return (((y + sign * dy) % NYL) * NX + (x + sign * dx) % NX) * 2 + half

    return (
        [owner(0, 0, core)]
        + [owner(1, 0, 0), owner(1, 0, 1)]
        + [owner(0, 1, 0), owner(0, 1, 1)]
        + [owner(1, 1, 0), owner(1, 1, 1)]
        + [owner(1, -1, 0), owner(1, -1, 1)]
        + [owner(2, 0, core), owner(0, 2, core)]
        + [owner(1, 2, 0), owner(1, 2, 1)]
        + [owner(2, -1, 0), owner(2, -1, 1)]
        + [owner(2, 2, core)]
    )


def per_device(activations, key_cotangent, doc_lengths, weight_codes, zero_points, step_sizes):
    tokens = activations.shape[0]
    rows = weight_codes.shape[0]
    place_in = lax.axis_index("tensor")
    devices = NX * NYL * 2
    core = place_in % 2
    x = (place_in // 2) % NX
    y = place_in // (2 * NX)
    table = jnp.stack(unit_table(x, y, core)).astype(jnp.int32)
    theirs = jnp.stack(unit_table(x, y, 1 - core)).astype(jnp.int32)

    weight = dequant(weight_codes, zero_points, step_sizes)
    pairs = [[2 * chip, 2 * chip + 1] for chip in range(NX * NYL)]
    chip_weight = lax.all_gather(weight, "tensor", axis=0, tiled=True, axis_index_groups=pairs)

    from_y = send(chip_weight, 0, 1)
    from_x = send(chip_weight, 1, 0)

    indices = place_in * tokens + jnp.arange(tokens, dtype=jnp.int32)
    turn = rotation(token_positions(doc_lengths[0], indices))
    mine, mine_feats, to_other = pack(table, theirs, turn, key_cotangent, activations, rows)
    feats = (mine_feats, swap(to_other))
    from_x, _ = lax.optimization_barrier((from_x, to_other))

    from_xy = send(from_x, 0, 1)
    from_yx = send(from_y, 1, 0, cross=True)
    half_x, half_y = halves(core.reshape(1), [from_x, from_y], rows)
    half_x, half_y, _ = lax.optimization_barrier((half_x, half_y, feats[1]))
    from_xy, _, _ = lax.optimization_barrier((from_xy, half_x, half_y))

    far_y = send(from_xy, 0, 1)
    far_x = send(from_yx, 1, 0)
    far_xx = send(half_x, 1, 0)
    far_yy = send(half_y, 0, 1)
    half_xy = lax.dynamic_slice_in_dim(from_xy, core * rows, rows, axis=0)
    half_xy, _, _ = lax.optimization_barrier((half_xy, far_xx, far_yy))
    far = send(half_xy, 1, 1)

    near = [weight, from_x, from_y, from_xy, from_yx]
    grad, sent_near, sums_near, rot, rot_again = near_shards(
        table, *feats, mine, near, rows, activations.shape[1]
    )
    fars = [far_xx, far_yy, far_y, far_x, far]
    at_hand = sums_near.shape[0]
    sums = far_sums(table, *feats, rot, fars, sums_near, rows, devices)
    shares = lax.all_to_all(sums, "tensor", split_axis=0, concat_axis=0, tiled=True)

    grad, sent_far = far_grad(table, rot_again, fars, grad, rows, at_hand)
    got_near = swap(sent_near)
    share = jnp.sum(shares.astype(jnp.float32), axis=0).astype(jnp.bfloat16)
    share = jnp.broadcast_to(share[None], (lax.axis_size("dp"), *share.shape))
    share, sent_far = lax.optimization_barrier((share, sent_far))
    totals = lax.all_to_all(share, "dp", split_axis=0, concat_axis=0, tiled=True)
    grad = place(theirs, got_near, grad, rows, 0)
    grad = place(theirs, swap(sent_far), grad, rows, at_hand)
    seq_tokens = tokens * devices
    total = jnp.sum(totals.astype(jnp.float32), axis=0)
    step_grad = total / (seq_tokens * step_sizes)
    return (grad, step_grad)


def solution(mesh):
    in_specs = (
        P(("dp", "tensor"), None),
        P(("dp", "tensor"), None),
        P("dp", None),
        P("tensor", None),
        P("tensor", None),
        P("tensor", None),
    )
    out_specs = (P(("dp", "tensor"), None), P("tensor", None))
    return jax.shard_map(
        per_device, mesh=mesh, in_specs=in_specs, out_specs=out_specs, check_vma=False
    )
```
